32 devices in a mesh: dp: 4 (over y, x), strip: 2 (over core), tensor: 4 (over z).
Axes of the slice: x: 2, y: 2, z: 4, core: 2. Of those that a mesh axis runs over, the one named last changes fastest.
Arguments:
- res_code: int32 [12], P('dp'), may hold values from 768 to 1536, as said below
- vit_in: float32 [12, 24, 24, 1024], P('dp', 'strip'), may hold values from -6 to 6
- map_in: bfloat16 [12, 48, 48, 1536], P('dp', 'strip', 'tensor'), may hold values from -6 to 6
- dw_kernel: float32 [1536, 49], replicated, may hold values from -0.875 to 0.875
- conv_gain: float32 [1536], replicated, may hold values from 0.5 to 1.5
- conv_bias: float32 [1536], replicated, may hold values from -3 to 3
- w_expand: bfloat16 [1536, 6144], P(('strip', 'tensor')), may hold values from -0.15625 to 0.15625
- w_reduce: bfloat16 [1536, 6144], P(('strip', 'tensor')), may hold values from -0.078125 to 0.078125
- layer_scale: float32 [1536], replicated, may hold values from 0.5 to 1.5
- adapt_w: bfloat16 [1536, 1024], replicated, may hold values from -0.15625 to 0.15625
- mix_kernel: float32 [1024, 9], replicated, may hold values from -2 to 2
- gate_logit: float32 [1024], replicated, may hold values from -1.5 to 1.5
- gain_one: float32 [1024], replicated, may hold values from 0.5 to 1.5
- bias_one: float32 [1024], replicated, may hold values from -3 to 3
- w_qkv: bfloat16 [1024, 3, 1024], P(None, None, 'tensor'), may hold values from -0.1875 to 0.1875
- w_proj: bfloat16 [1024, 1024], P(None, 'tensor'), may hold values from -1.5 to 1.5
- gain_two: float32 [1024], replicated, may hold values from 0.5 to 1.5
- bias_two: float32 [1024], replicated, may hold values from -3 to 3
- w_up: bfloat16 [1024, 4096], P(None, 'tensor'), may hold values from -0.1875 to 0.1875
- w_down: bfloat16 [1024, 4096], P(None, 'tensor'), may hold values from -0.375 to 0.375
- d_vit: float32 [12, 24, 24, 1024], P('dp', 'strip'), may hold values from -6 to 6
- d_map: bfloat16 [12, 48, 48, 1536], P('dp', 'strip', 'tensor'), may hold values from -6 to 6
Outputs:
- vit_out: float32 [12, 24, 24, 1024], P('dp', 'strip')
- map_out: bfloat16 [12, 48, 48, 1536], P('dp', 'strip', 'tensor')
- grad_vit_in: float32 [12, 24, 24, 1024], P('dp', 'strip')
- grad_map_in: float32 [12, 48, 48, 1536], P('dp', 'strip', 'tensor')
- grad_dw_kernel: float32 [1536, 49], P(('strip', 'tensor'))
- grad_conv_gain: float32 [1536], P(('strip', 'tensor'))
- grad_conv_bias: float32 [1536], P(('strip', 'tensor'))
- grad_w_expand: float32 [1536, 6144], P(('strip', 'tensor'))
- grad_w_reduce: float32 [1536, 6144], P(('strip', 'tensor'))
- grad_layer_scale: float32 [1536], P(('strip', 'tensor'))
- grad_adapt_w: float32 [1536, 1024], P(('dp', 'strip'))
- grad_mix_kernel: float32 [1024, 9], P(('dp', 'strip'))
- grad_gate_logit: float32 [1024], P(('dp', 'strip'))
- grad_gain_one: float32 [1024], P(('dp', 'strip'))
- grad_bias_one: float32 [1024], P(('dp', 'strip'))
- grad_w_qkv: float32 [1024, 3, 1024], P(('dp', 'strip'), None, 'tensor')
- grad_w_proj: float32 [1024, 1024], P(('dp', 'strip'), 'tensor')
- grad_gain_two: float32 [1024], P(('dp', 'strip'))
- grad_bias_two: float32 [1024], P(('dp', 'strip'))
- grad_w_up: float32 [1024, 4096], P(('dp', 'strip'), 'tensor')
- grad_w_down: float32 [1024, 4096], P(('dp', 'strip'), 'tensor')
The draws below stay inside these ranges and needn't reach their ends.
Inputs may be any that keep to these rules, and one draw needn't show every extreme that they name: `res_code`: each entry is 768, 1024 or 1536 (maps of 24, 32 or 48 cells a side); 1536 occurs in every draw.
All inputs are finite; a program needn't handle non-finite values.
Results may differ from the reference program's by a relative error of at most 0.024.
Values may be sent and summed in bfloat16 or wider, within the bound.
No kernel may reach another device: no remote copies, remote signals or barrier semaphores. Data moves between devices by JAX's collectives and lax.ppermute only.
A program may use at most 384 MiB of HBM per device.

```python
import jax
import jax.numpy as jnp
from jax import lax

D = 1024
HD = 64
FFV = 4096
C = 1536
FFC = 6144
G = 24
MAXS = 48
ITEMS = 12


def draw_res_code(key, part):
    key = jax.random.fold_in(key, 7)
    pick_key, slot_key = jax.random.split(key)
    size_pick = jax.random.randint(pick_key, (ITEMS,), 0, 3)
    large_slot = jax.random.randint(slot_key, (), 0, ITEMS)
    size_pick = jnp.where(jnp.arange(ITEMS) == large_slot, 2, size_pick)
    return jnp.where(size_pick == 0, 768, jnp.where(size_pick == 1, 1024, 1536)).astype(jnp.int32)


def block_levels(own_key, extent, cuts, least, high):
    def one(dim, shards_of):
        heights = jax.random.uniform(jax.random.fold_in(jax.random.fold_in(own_key, 6), dim), (shards_of,), jnp.float32, least / len(cuts), high / len(cuts))
        return jnp.repeat(jnp.exp(heights), extent[dim] // shards_of).reshape((-1,) + (1,) * (len(extent) - dim - 1))

    level = one(*cuts[0])
    for cut in cuts[1:]:
        level = level * one(*cut)
    return level


def centred(own_key, extent, scale, limit, shards=(), held_as=jnp.bfloat16):
    values = jax.random.normal(own_key, extent, jnp.float32) * scale
    if len(shards) > 0:
        values = block_levels(own_key, extent, shards, -0.22, 0.18) * values
    return jnp.clip(values, min=-limit, max=limit).astype(held_as)


def setup_inputs(seed: int = 0) -> dict:
    arg_keys = jax.random.split(jax.random.key(seed), 23)
    return {
        "res_code": draw_res_code(jax.random.fold_in(arg_keys[22], 71), 0),
        "vit_in": centred(arg_keys[1], (ITEMS, G, G, D), 1.0, 6.0, ((0, 4), (1, 2)), jnp.float32),
        "map_in": centred(arg_keys[2], (ITEMS, MAXS, MAXS, C), 1.0, 6.0, ((0, 4), (1, 2), (2, 4))),
        "dw_kernel": centred(arg_keys[3], (C, 49), 49 ** -0.5, 0.875, (), jnp.float32),
        "conv_gain": jnp.clip(1.0 + 0.1 * jax.random.normal(arg_keys[4], (C,), jnp.float32), 0.5, 1.5),
        "conv_bias": centred(arg_keys[5], (C,), 0.5, 3.0, (), jnp.float32),
        "w_expand": centred(arg_keys[6], (C, FFC), C ** -0.5, 0.15625, ((0, 8),)),
        "w_reduce": centred(arg_keys[7], (C, FFC), FFC ** -0.5, 0.078125, ((0, 8),)),
        "layer_scale": jnp.clip(1.0 + 0.1 * jax.random.normal(arg_keys[8], (C,), jnp.float32), 0.5, 1.5),
        "adapt_w": centred(arg_keys[9], (C, D), C ** -0.5, 0.15625),
        "mix_kernel": centred(arg_keys[10], (D, 9), 9 ** -0.5, 2.0, (), jnp.float32),
        "gate_logit": jnp.clip(jax.random.uniform(arg_keys[11], (D,), jnp.float32, -1.5, 1.5), -1.5, 1.5),
        "gain_one": jnp.clip(1.0 + 0.1 * jax.random.normal(arg_keys[12], (D,), jnp.float32), 0.5, 1.5),
        "bias_one": centred(arg_keys[13], (D,), 0.5, 3.0, (), jnp.float32),
        "w_qkv": centred(arg_keys[14], (D, 3, D), D ** -0.5, 0.1875, ((2, 4),)),
        "w_proj": centred(arg_keys[15], (D, D), (max(D // 64, 1)) ** -0.5, 1.5, ((1, 4),)),
        "gain_two": jnp.clip(1.0 + 0.1 * jax.random.normal(arg_keys[16], (D,), jnp.float32), 0.5, 1.5),
        "bias_two": centred(arg_keys[17], (D,), 0.5, 3.0, (), jnp.float32),
        "w_up": centred(arg_keys[18], (D, FFV), D ** -0.5, 0.1875, ((1, 4),)),
        "w_down": centred(arg_keys[19], (D, FFV), (max(FFV // 16, 1)) ** -0.5, 0.375, ((1, 4),)),
        "d_vit": centred(arg_keys[20], (ITEMS, G, G, D), 1.0, 6.0, ((0, 4), (1, 2)), jnp.float32),
        "d_map": centred(arg_keys[21], (ITEMS, MAXS, MAXS, C), 1.0, 6.0, ((0, 4), (1, 2), (2, 4))),
    }


@jax.custom_vjp
def low(v):
    return lax.optimization_barrier(v.astype(jnp.bfloat16)).astype(jnp.float32)

@jax.custom_vjp
def low_back(v):
    return v

def low_keep(v):
    return (low(v), None)

def low_pass(kept, grad):
    return (grad,)

def back_keep(v):
    return (v, None)

def back_low(kept, grad):
    return (low(grad),)
low.defvjp(low_keep, low_pass)
low_back.defvjp(back_keep, back_low)
EPS = 1e-06
HIGH = lax.Precision.HIGHEST

def layer_norm(values, gain, bias):
    center = lax.optimization_barrier(jnp.mean(values, axis=-1, keepdims=True))
    shifted = values - center
    spread_sq = lax.optimization_barrier(jnp.mean(shifted * shifted, axis=-1, keepdims=True))
    return shifted * lax.rsqrt(spread_sq + EPS) * gain + bias

def depthwise(padded, kernel, reach, rows, cols):
    summed = jnp.zeros(padded.shape[:-3] + (rows, cols, padded.shape[-1]), jnp.float32)
    for row_off in range(reach):
        for col_off in range(reach):
            summed = summed + padded[..., row_off:row_off + rows, col_off:col_off + cols, :] * kernel[:, row_off * reach + col_off]
    return summed

def pool_matrix(pooled_index, buffer_index, map_side, offset):
    map_place = buffer_index[None, :] - offset
    bin_start = pooled_index[:, None] * map_side // G
    bin_stop = ((pooled_index[:, None] + 1) * map_side + G - 1) // G
    inside = jnp.logical_and(map_place >= bin_start, map_place < bin_stop)
    return jnp.where(inside, 1.0, 0.0).astype(jnp.float32) / (bin_stop - bin_start).astype(jnp.float32)

def item_forward(map_side, vit_item, map_item, params):
    dw_kernel, conv_gain, conv_bias, w_expand, w_reduce, layer_scale, adapt_w, mix_kernel, gate_logit, gain_one, bias_one, w_qkv, w_proj, gain_two, bias_two, w_up, w_down = params
    channels = map_item.shape[-1]
    width = vit_item.shape[-1]
    offset = (MAXS - map_side) // 2
    cell_index = jnp.arange(MAXS, dtype=jnp.int32)
    inside = jnp.logical_and(cell_index >= offset, cell_index < offset + map_side).astype(jnp.float32)
    cell_mask = inside[:, None, None] * inside[None, :, None]
    masked = map_item * cell_mask
    padded = jnp.pad(masked, ((3, 3), (3, 3), (0, 0)))
    spread = depthwise(padded, dw_kernel, 7, MAXS, MAXS)
    normed = low(layer_norm(spread, conv_gain, conv_bias)).reshape(MAXS * MAXS, channels)
    hidden = low_back(jnp.dot(normed, w_expand, precision=HIGH))
    active = low(jax.nn.gelu(hidden, approximate=False))
    branch = low_back(jnp.dot(active, w_reduce.T, precision=HIGH)).reshape(MAXS, MAXS, channels)
    map_value = cell_mask * (masked + layer_scale * branch)
    grid_index = jnp.arange(G, dtype=jnp.int32)
    pooling = pool_matrix(grid_index, cell_index, map_side, offset)
    row_pooled = jnp.einsum('ir,rcd->icd', pooling, map_value, precision=HIGH)
    pooled = jnp.einsum('jc,icd->ijd', pooling, row_pooled, precision=HIGH)
    adapted = low_back(jnp.dot(low(pooled).reshape(G * G, channels), adapt_w, precision=HIGH)).reshape(G, G, width)
    adapted_pad = jnp.pad(adapted, ((1, 1), (1, 1), (0, 0)))
    local_mix = depthwise(adapted_pad, mix_kernel, 3, G, G)
    joined_rows = (vit_item + jnp.tanh(gate_logit) * local_mix).reshape(G * G, width)
    normed_one = low(layer_norm(joined_rows, gain_one, bias_one))
    qkv_rows = low(low_back(jnp.einsum('td,dkh->tkh', normed_one, w_qkv, precision=HIGH)))
    head_view = qkv_rows.reshape(G * G, 3, width // HD, HD)
    scores = low_back(jnp.einsum('qhe,khe->hqk', head_view[:, 0], head_view[:, 1], precision=HIGH) * HD ** (-0.5))
    attn_probs = jax.nn.softmax(scores, axis=-1)
    mixed_heads = low(low_back(jnp.einsum('hqk,khe->qhe', low(attn_probs), head_view[:, 2], precision=HIGH)))
    attn_out = low_back(jnp.dot(mixed_heads.reshape(G * G, width), w_proj.T, precision=HIGH))
    after_attn = joined_rows + attn_out
    normed_two = low(layer_norm(after_attn, gain_two, bias_two))
    hidden_two = low_back(jnp.dot(normed_two, w_up, precision=HIGH))
    active_two = low(jax.nn.gelu(hidden_two, approximate=False))
    mlp_out = low_back(jnp.dot(active_two, w_down.T, precision=HIGH))
    vit_result = (after_attn + mlp_out).reshape(G, G, width)
    return (vit_result, map_value)

def reference(res_code, vit_in, map_in, dw_kernel, conv_gain, conv_bias, w_expand, w_reduce, layer_scale, adapt_w, mix_kernel, gate_logit, gain_one, bias_one, w_qkv, w_proj, gain_two, bias_two, w_up, w_down, d_vit, d_map):
    params = tuple((weight.astype(jnp.float32) for weight in (dw_kernel, conv_gain, conv_bias, w_expand, w_reduce, layer_scale, adapt_w, mix_kernel, gate_logit, gain_one, bias_one, w_qkv, w_proj, gain_two, bias_two, w_up, w_down)))

    def item_step(totals, item_data):
        item_code, vit_item, map_item, dvit_item, dmap_item = item_data
        map_side = item_code // 32

        def forward(vit_arg, map_arg, param_arg):
            return item_forward(map_side, vit_arg, map_arg, param_arg)
        (vit_result, map_value), pullback = jax.vjp(forward, vit_item, map_item.astype(jnp.float32), params)
        grad_vit, grad_map, grad_params = pullback((dvit_item, dmap_item.astype(jnp.float32)))
        totals = jax.tree.map(lambda first_term, second_term: first_term + second_term, totals, grad_params)
        return (totals, (vit_result, map_value.astype(jnp.bfloat16), grad_vit, grad_map))
    zero_grads = jax.tree.map(jnp.zeros_like, params)
    grads_all, (vit_out, map_out, grad_vit_in, grad_map_in) = lax.scan(item_step, zero_grads, (res_code, vit_in, map_in, d_vit, d_map))
    return (vit_out, map_out, grad_vit_in, grad_map_in, grads_all[0], grads_all[1], grads_all[2], grads_all[3], grads_all[4], grads_all[5], grads_all[6], grads_all[7], grads_all[8], grads_all[9], grads_all[10], grads_all[11], grads_all[12], grads_all[13], grads_all[14], grads_all[15], grads_all[16])
```

```python
import functools

import jax
import jax.numpy as jnp
from jax import lax
from jax.experimental import pallas as pl
from jax.experimental.pallas import tpu as pltpu
from jax.sharding import PartitionSpec as P

HD = 64
G = 24
MAXS = 48
EPS = 1e-06
BF = jnp.bfloat16
F32 = jnp.float32
DOWN_ROWS = (((0,), (0,)), ((), ()))
ACROSS = (((1,), (1,)), ((), ()))
VMEM = 48 * 2**20
EDGE = 8


def core_swap(v):
    return lax.ppermute(v, "strip", [(0, 1), (1, 0)])


def dp_swap(v, bit):
    return lax.ppermute(v, "dp", [(i, i ^ bit) for i in range(lax.axis_size("dp"))])


def shift(v, axis, step):
    count = lax.axis_size(axis)
    pairs = [(i, i + step) for i in range(count) if 0 <= i + step < count]
    return lax.ppermute(v, axis, pairs)


def all_sum(v, axes):
    for axis in axes:
        count, bit = lax.axis_size(axis), 1
        while bit < count:
            v = v + lax.ppermute(v, axis, [(i, i ^ bit) for i in range(count)])
            bit *= 2
    return v


def quarters():
    return 4 if lax.axis_size("dp") == 4 else 1


def gather_dp(own):
    if quarters() == 1:
        return [own]
    half = own.shape[0] // 2
    beside_x, beside_y = dp_swap(own, 1), dp_swap(own, 2)
    far = jnp.concatenate([dp_swap(beside_x[:half], 2), dp_swap(beside_y[half:], 1)], axis=0)
    return [own, beside_x, beside_y, far]


def reduce_dp(pieces):
    if len(pieces) == 1:
        return pieces[0]
    own, beside_x, beside_y, far = pieces
    half = own.shape[0] // 2
    near_a = dp_swap(jnp.concatenate([beside_x[:half], far[:half]], axis=0), 1)
    near_b = dp_swap(jnp.concatenate([beside_y[half:], far[half:]], axis=0), 2)
    add = lambda *terms: functools.reduce(lambda a, b: a + b, [t.astype(F32) for t in terms])
    last_a = dp_swap(add(beside_y[:half], near_a[half:]).astype(BF), 2)
    last_b = dp_swap(add(beside_x[half:], near_b[half:]).astype(BF), 1)
    top = add(own[:half], near_a[:half], last_a)
    low = add(own[half:], near_b[:half], last_b)
    return jnp.concatenate([top, low], axis=0).astype(BF)


def in_order(mine, other, at):
    first = at == 0
    return jnp.stack([jnp.where(first, mine, other), jnp.where(first, other, mine)], axis=0)


def dp_order(pieces):
    at = lax.axis_index("dp")
    bit_x, bit_y = at % 2 == 1, at // 2 == 1
    row_own = [jnp.where(bit_x, pieces[1], pieces[0]), jnp.where(bit_x, pieces[0], pieces[1])]
    row_far = [jnp.where(bit_x, pieces[3], pieces[2]), jnp.where(bit_x, pieces[2], pieces[3])]
    return jnp.stack(
        [jnp.where(bit_y, f, o) for o, f in zip(row_own, row_far)]
        + [jnp.where(bit_y, o, f) for o, f in zip(row_own, row_far)],
        axis=0,
    )


def pick(view, first, second):
    rows, _, _, width = view.shape
    return lax.dynamic_slice(view, (0, first, second, 0), (rows, 1, 1, width)).reshape(rows, width)


def gather_conv_weight(block):
    rows, hidden = block.shape
    q = quarters()
    strip_at = lax.axis_index("strip")
    dp_at = lax.axis_index("dp") if q > 1 else 0
    view = block.reshape(rows, 2, q, hidden // (2 * q))
    mine = pick(view, strip_at, dp_at)
    other = core_swap(pick(view, 1 - strip_at, dp_at))
    both = in_order(mine, other, strip_at)
    whole = lax.all_gather(both, "tensor", axis=0)
    whole = jnp.swapaxes(whole, 0, 1).reshape(-1, mine.shape[1])
    return gather_dp(whole)


def return_conv_grad(pieces):
    strip_at = lax.axis_index("strip")
    zs = lax.axis_size("tensor")
    own = reduce_dp(pieces)
    channels, width = own.shape
    rows = channels // (2 * zs)
    view = jnp.swapaxes(own.reshape(2, zs, rows, width), 0, 1)
    part = lax.psum_scatter(view, "tensor", scatter_dimension=0)
    mine = lax.dynamic_index_in_dim(part, strip_at, 0, keepdims=False)
    other = core_swap(lax.dynamic_index_in_dim(part, 1 - strip_at, 0, keepdims=False))
    both = in_order(mine, other, strip_at)
    if len(pieces) == 1:
        total = lax.psum(both, "dp")
        return jnp.swapaxes(total, 0, 1).reshape(rows, -1).astype(F32)
    every = dp_order(gather_dp(jnp.swapaxes(both, 0, 1)))
    return jnp.transpose(every, (1, 2, 0, 3)).reshape(rows, -1).astype(F32)


def gather_mlp_weight(block):
    width, hidden = block.shape
    q = quarters()
    dp_at = lax.axis_index("dp") if q > 1 else 0
    mine = pick(block.reshape(width, 2, q, hidden // (2 * q)), lax.axis_index("strip"), dp_at)
    whole = lax.all_gather(mine, "tensor", axis=0)
    return gather_dp(jnp.swapaxes(whole, 0, 1).reshape(width, -1))


def return_mlp_grad(pieces):
    own = reduce_dp(pieces)
    width, all_cols = own.shape
    zs = lax.axis_size("tensor")
    cols = all_cols // zs
    dps = lax.axis_size("dp")
    rows = width // (2 * dps)
    view = jnp.swapaxes(own.reshape(width, zs, cols), 0, 1)
    part = lax.psum_scatter(view, "tensor", scatter_dimension=0)
    if len(pieces) > 1:
        parts = lax.all_to_all(part, ("dp", "strip"), 0, 0, tiled=True)
        parts = parts.reshape(dps, 2, rows, cols)
        return jnp.transpose(parts, (2, 1, 0, 3)).reshape(rows, -1).astype(F32)
    strip_at = lax.axis_index("strip")
    part = lax.psum_scatter(part.reshape(dps, 2, rows, cols), "dp", scatter_dimension=0)
    mine = lax.dynamic_index_in_dim(part, strip_at, 0, keepdims=False)
    other = core_swap(lax.dynamic_index_in_dim(part, 1 - strip_at, 0, keepdims=False))
    both = in_order(mine, other, strip_at)
    return jnp.swapaxes(both, 0, 1).reshape(rows, -1).astype(F32)


def gather_rows(block):
    width, cols = block.shape
    dps = lax.axis_size("dp")
    rows = width // (2 * dps)
    at = lax.axis_index("dp") * 2 + lax.axis_index("strip")
    mine = lax.dynamic_slice_in_dim(block, at * rows, rows, 0)
    whole = lax.all_gather(mine, ("tensor", "dp", "strip"), axis=0, tiled=True)
    return whole.reshape(-1, width, cols)


def params(limit=VMEM):
    return pltpu.CompilerParams(vmem_limit_bytes=limit)


def conv7_kernel(rows, cols, x_ref, k_ref, out_ref, wide):
    wide[...] = x_ref[0].astype(F32)

    def tap_row(i, sums):
        sums = list(sums)
        taps = k_ref[i]
        for m in range(cols + 6):
            x = wide[m, pl.ds(i + EDGE - 3, rows), :]
            for j in range(7):
                c = m - j
                if 0 <= c < cols:
                    sums[c] = sums[c] + x * taps[j : j + 1]
        return tuple(sums)

    sums = lax.fori_loop(0, 7, tap_row, tuple(jnp.zeros((rows, 128), F32) for _ in range(cols)))
    for c in range(cols):
        out_ref[0, c] = sums[c]


def conv7(padded, taps, rows, cols):
    items, _, _, channels = padded.shape
    return pl.pallas_call(
        functools.partial(conv7_kernel, rows, cols),
        grid=(items, channels // 128),
        in_specs=[
            pl.BlockSpec((1, cols + 6, rows + 2 * EDGE, 128), lambda b, c: (b, 0, 0, c)),
            pl.BlockSpec((7, 8, 128), lambda b, c: (0, 0, c)),
        ],
        out_specs=pl.BlockSpec((1, cols, rows, 128), lambda b, c: (b, 0, 0, c)),
        out_shape=jax.ShapeDtypeStruct((items, cols, rows, channels), F32),
        scratch_shapes=[pltpu.VMEM((cols + 6, rows + 2 * EDGE, 128), F32)],
        compiler_params=params(),
        cost_estimate=pl.CostEstimate(
            flops=items * cols * rows * channels * 98, bytes_accessed=padded.size * 2 + items * cols * rows * channels * 4, transcendentals=0
        ),
        name="depthwise",
    )(padded, taps)


def tap_grad_kernel(rows, cols, x_ref, g_ref, out_ref, wide):
    wide[...] = x_ref[0].astype(F32)

    @pl.when(pl.program_id(1) == 0)
    def _():
        out_ref[...] = jnp.zeros_like(out_ref)

    def tap_row(i, _):
        sums = [jnp.zeros((8, 128), F32) for _ in range(7)]
        grads = [g_ref[0, c] for c in range(cols)]
        for m in range(cols + 6):
            x = wide[m, pl.ds(i + EDGE - 3, rows), :]
            for j in range(7):
                c = m - j
                if 0 <= c < cols:
                    sums[j] = sums[j] + (x * grads[c]).reshape(rows // 8, 8, 128).sum(axis=0)
        lines = [jnp.sum(s, axis=0, keepdims=True) for s in sums]
        out_ref[i] += jnp.concatenate(lines + [jnp.zeros((1, 128), F32)], axis=0)
        return 0

    lax.fori_loop(0, 7, tap_row, 0)


def tap_grad(padded, grad, rows, cols):
    items, _, _, channels = padded.shape
    return pl.pallas_call(
        functools.partial(tap_grad_kernel, rows, cols),
        grid=(channels // 128, items),
        in_specs=[
            pl.BlockSpec((1, cols + 6, rows + 2 * EDGE, 128), lambda c, b: (b, 0, 0, c)),
            pl.BlockSpec((1, cols, rows, 128), lambda c, b: (b, 0, 0, c)),
        ],
        out_specs=pl.BlockSpec((7, 8, 128), lambda c, b: (0, 0, c)),
        out_shape=jax.ShapeDtypeStruct((7, 8, channels), F32),
        scratch_shapes=[pltpu.VMEM((cols + 6, rows + 2 * EDGE, 128), F32)],
        compiler_params=params(),
        cost_estimate=pl.CostEstimate(
            flops=items * cols * rows * channels * 98, bytes_accessed=padded.size * 2 + items * cols * rows * channels * 4, transcendentals=0
        ),
        name="tap_grad",
    )(padded, grad)


def gelu_pair(h):
    cdf = 0.5 * (1.0 + lax.erf(h * (0.5**0.5)))
    pdf = jnp.exp(h * h * -0.5) * 0.3989422804014327
    return h * cdf, cdf + h * pdf


def expand_kernel(step, x_ref, w_ref, act_ref, slope_ref):
    x = x_ref[...]
    for at in range(0, w_ref.shape[1], step):
        h = jnp.dot(x, w_ref[:, at : at + step], preferred_element_type=F32)
        act, slope = gelu_pair(h)
        act_ref[:, at : at + step] = act.astype(BF)
        slope_ref[:, at : at + step] = slope.astype(BF)


def row_block(rows, most):
    best = 16
    for block in range(16, most + 1, 16):
        if rows % block == 0:
            best = block
    return best


def expand(x, w):
    m, k = x.shape
    n = w.shape[1]
    bm = row_block(m, 432)
    bn = min(n, 768)
    spec = pl.BlockSpec((bm, bn), lambda j, i: (i, j))
    return pl.pallas_call(
        functools.partial(expand_kernel, 256),
        grid=(n // bn, m // bm),
        in_specs=[pl.BlockSpec((bm, k), lambda j, i: (i, 0)), pl.BlockSpec((k, bn), lambda j, i: (0, j))],
        out_specs=[spec, spec],
        out_shape=[jax.ShapeDtypeStruct((m, n), BF)] * 2,
        compiler_params=params(),
        cost_estimate=pl.CostEstimate(flops=2 * m * n * k + 40 * m * n, bytes_accessed=2 * (m * k + n * k + 2 * m * n), transcendentals=2 * m * n),
        name="expand_gelu",
    )(x, w)


def back_sum_kernel(count, *refs):
    out_ref = refs[-1]
    total = None
    for a_ref, w_ref in zip(refs[:count], refs[count : 2 * count]):
        term = lax.dot_general(a_ref[...], w_ref[...], ACROSS, preferred_element_type=F32)
        total = term if total is None else total + term
    out_ref[...] = total.astype(out_ref.dtype)


def back_sum(parts, weights, first, rows, dtype):
    n = weights[0].shape[0]
    ks = [w.shape[1] for w in weights]
    bm = row_block(rows, 432)
    bn = 512
    skip = first // bm
    return pl.pallas_call(
        functools.partial(back_sum_kernel, len(parts)),
        grid=(n // bn, rows // bm),
        in_specs=[pl.BlockSpec((bm, k), lambda j, i: (i + skip, 0)) for k in ks]
        + [pl.BlockSpec((bn, k), lambda j, i: (j, 0)) for k in ks],
        out_specs=pl.BlockSpec((bm, bn), lambda j, i: (i, j)),
        out_shape=jax.ShapeDtypeStruct((rows, n), dtype),
        compiler_params=params(),
        cost_estimate=pl.CostEstimate(flops=2 * rows * n * sum(ks), bytes_accessed=2 * sum(ks) * (rows + n) + 4 * rows * n, transcendentals=0),
        name="reduce_sum",
    )(*parts, *weights)


def normalise(v):
    center = jnp.mean(v, axis=-1, keepdims=True)
    shifted = v - center
    scale = lax.rsqrt(jnp.mean(shifted * shifted, axis=-1, keepdims=True) + EPS)
    return shifted * scale, scale


def normalise_back(g, unit, scale, gain):
    gg = g * gain
    along = jnp.mean(gg * unit, axis=-1, keepdims=True)
    return scale * (gg - jnp.mean(gg, axis=-1, keepdims=True) - unit * along)


def pool_matrix(pooled_index, buffer_index, map_side, offset):
    map_place = buffer_index[None, :] - offset
    bin_start = pooled_index[:, None] * map_side // G
    bin_stop = ((pooled_index[:, None] + 1) * map_side + G - 1) // G
    inside = jnp.logical_and(map_place >= bin_start, map_place < bin_stop)
    real = jnp.logical_and(pooled_index >= 0, pooled_index < G)[:, None]
    return jnp.where(jnp.logical_and(inside, real), 1.0, 0.0).astype(F32) / (bin_stop - bin_start).astype(F32)


def depthwise3(padded, kernel, rows, cols):
    total = None
    for i in range(3):
        for j in range(3):
            term = padded[:, i : i + rows, j : j + cols, :] * kernel[:, 3 * i + j]
            total = term if total is None else total + term
    return total


def rim(v):
    v = jnp.concatenate([shift(v[:, -1:], "strip", 1), v, shift(v[:, :1], "strip", -1)], axis=1)
    return jnp.concatenate([shift(v[:, :, -1:], "tensor", 1), v, shift(v[:, :, :1], "tensor", -1)], axis=2)


def wide_rim(v):
    v = jnp.concatenate([shift(v[:, -3:], "tensor", 1), v, shift(v[:, :3], "tensor", -1)], axis=1)
    return jnp.concatenate([shift(v[:, :, -EDGE:], "strip", 1), v, shift(v[:, :, :EDGE], "strip", -1)], axis=2)


def shards(
    res_code, vit_in, map_in, dw_kernel, conv_gain, conv_bias, w_expand, w_reduce, layer_scale, adapt_w, mix_kernel,
    gate_logit, gain_one, bias_one, w_qkv, w_proj, gain_two, bias_two, w_up, w_down, d_vit, d_map,
):
    strip_at, tensor_at, dp_at = (lax.axis_index(a) for a in ("strip", "tensor", "dp"))
    dps, zs = lax.axis_size("dp"), lax.axis_size("tensor")
    items, grid_rows, _, width = vit_in.shape
    _, map_rows, map_cols, channels = map_in.shape
    grid_cols = G // zs
    cells = items * map_rows * map_cols
    tokens = items * grid_rows * grid_cols
    head_cols = w_qkv.shape[2]
    score_scale = HD**-0.5

    expand_pieces = gather_conv_weight(w_expand)
    reduce_pieces = gather_conv_weight(w_reduce)
    qkv_whole = gather_rows(w_qkv.reshape(width, -1))
    proj_whole = gather_rows(w_proj)
    up_pieces = gather_mlp_weight(w_up)
    down_pieces = gather_mlp_weight(w_down)
    count = len(expand_pieces)

    side = res_code // 32
    offset = (MAXS - side) // 2
    row_cells = strip_at * map_rows + jnp.arange(map_rows, dtype=jnp.int32)
    col_cells = tensor_at * map_cols + jnp.arange(map_cols, dtype=jnp.int32)

    def inside(at):
        low, high = offset[:, None], (offset + side)[:, None]
        return jnp.logical_and(at[None] >= low, at[None] < high).astype(F32)

    row_ok, col_ok = inside(row_cells), inside(col_cells)
    cell_mask = col_ok[:, :, None, None] * row_ok[:, None, :, None]
    many_pools = jax.vmap(pool_matrix, in_axes=(None, None, 0, 0))
    pooled_rows = strip_at * grid_rows + jnp.arange(grid_rows, dtype=jnp.int32)
    pooled_cols = (tensor_at - 1) * grid_cols + jnp.arange(3 * grid_cols, dtype=jnp.int32)
    row_pool = many_pools(pooled_rows, row_cells, side, offset)
    col_pool = many_pools(pooled_cols, col_cells, side, offset).reshape(items, 3, grid_cols, map_cols)
    pool = jnp.einsum("bir,bgjc->bgijcr", row_pool, col_pool)
    pool = pool.reshape(items, 3 * grid_rows * grid_cols, map_cols * map_rows).astype(BF)

    masked = jnp.swapaxes(map_in, 1, 2) * cell_mask.astype(BF)
    padded = wide_rim(masked)
    taps = jnp.pad(dw_kernel.T.reshape(7, 7, channels), ((0, 0), (0, 1), (0, 0)))
    spread = conv7(padded, taps, map_rows, map_cols).reshape(cells, channels)
    conv_unit, conv_std = normalise(spread)
    conv_unit = conv_unit.astype(BF)
    normed = (conv_unit.astype(F32) * conv_gain + conv_bias).astype(BF)
    normed_both = jnp.concatenate([normed, core_swap(normed)], axis=0)
    acts, slopes = zip(*[expand(normed_both, w) for w in expand_pieces])
    branch_there = core_swap(back_sum(acts, reduce_pieces, cells, cells, BF))
    branch_here = back_sum(acts, reduce_pieces, 0, cells, F32)
    branch = (branch_here + branch_there.astype(F32)).reshape(masked.shape)
    map_value = cell_mask * (masked.astype(F32) + layer_scale * branch)
    map_low = map_value.astype(BF)
    map_out = jnp.swapaxes(map_low, 1, 2)

    pooled3 = lax.dot_general(
        pool, map_low.reshape(items, -1, channels), (((2,), (1,)), ((0,), (0,))), preferred_element_type=F32
    ).reshape(items, 3, -1, channels)
    pooled = (
        pooled3[:, 1]
        + shift(pooled3[:, 0].astype(BF), "tensor", -1).astype(F32)
        + shift(pooled3[:, 2].astype(BF), "tensor", 1).astype(F32)
    )
    pooled_low = pooled.astype(BF).reshape(tokens, channels)
    grid_shape = (items, grid_rows, grid_cols, width)
    adapted = jnp.dot(pooled_low, adapt_w, preferred_element_type=F32).reshape(grid_shape)
    adapted_pad = rim(adapted)
    local_mix = depthwise3(adapted_pad, mix_kernel, grid_rows, grid_cols)
    gate = jnp.tanh(gate_logit)
    mine = lambda v: lax.dynamic_slice_in_dim(v, tensor_at * grid_cols, grid_cols, 2)
    joined = (mine(vit_in) + gate * local_mix).reshape(tokens, width)

    unit_one, std_one = normalise(joined)
    normed_one = (unit_one * gain_one + bias_one).astype(BF)
    group = head_cols // 2
    heads = group // HD

    def to_heads(parts):
        a = parts[0].shape[1]
        out = jnp.stack(parts, axis=0).reshape(zs, items, -1, a, 2, group)
        out = jnp.transpose(out, (4, 0, 1, 2, 3, 5)).reshape(2 * zs, items, -1, a * group)
        out = lax.all_to_all(out, ("strip", "tensor"), 0, 0, tiled=True)
        return jnp.swapaxes(out, 0, 1).reshape(items, -1, a, heads, HD)

    def to_tokens(v):
        a = v.shape[2]
        out = jnp.swapaxes(v.reshape(items, 2 * zs, -1, a * group), 0, 1)
        out = lax.all_to_all(out, ("strip", "tensor"), 0, 0, tiled=True)
        out = jnp.transpose(out.reshape(2, zs, tokens, a, group), (1, 2, 3, 0, 4))
        return out.reshape(zs, tokens, a * 2 * group)

    qkv = [jnp.dot(normed_one, w, preferred_element_type=F32).astype(BF).reshape(tokens, 3, 2, group) for w in qkv_whole]
    qkv = to_heads(qkv)
    q, k, v = qkv[:, :, 0], qkv[:, :, 1], qkv[:, :, 2]
    scores = jnp.einsum("bqhe,bkhe->bhqk", q, k, preferred_element_type=F32) * score_scale
    top = jnp.max(scores, axis=-1, keepdims=True)
    powers = jnp.exp(scores - top)
    probs = powers / jnp.sum(powers, axis=-1, keepdims=True)
    probs_low = probs.astype(BF)
    mixed = jnp.einsum("bhqk,bkhe->bqhe", probs_low, v, preferred_element_type=F32).astype(BF)
    attention = to_tokens(mixed[:, :, None])
    attn_out = sum(
        lax.dot_general(attention[z], proj_whole[z], ACROSS, preferred_element_type=F32) for z in range(zs)
    )
    after_attn = joined + attn_out

    unit_two, std_two = normalise(after_attn)
    normed_two = (unit_two * gain_two + bias_two).astype(BF)
    two_both = jnp.concatenate([normed_two, core_swap(normed_two)], axis=0)
    ups = [gelu_pair(jnp.dot(two_both, w, preferred_element_type=F32)) for w in up_pieces]
    actives = [u[0].astype(BF) for u in ups]
    up_slopes = [u[1] for u in ups]
    mlp = sum(lax.dot_general(a, w, ACROSS, preferred_element_type=F32) for a, w in zip(actives, down_pieces))
    mlp_out = mlp[:tokens] + core_swap(mlp[tokens:].astype(BF)).astype(F32)

    def to_grid(v):
        every = lax.all_gather(v.astype(BF).reshape(grid_shape), "tensor", axis=0)
        return jnp.transpose(every, (1, 2, 0, 3, 4)).reshape(items, grid_rows, G, width).astype(F32)

    vit_out = to_grid(after_attn + mlp_out)

    grad_out = mine(d_vit).reshape(tokens, width)
    grad_mlp = grad_out.astype(BF)
    grad_mlp_both = jnp.concatenate([grad_mlp, core_swap(grad_mlp)], axis=0)
    grad_down = [
        lax.dot_general(grad_mlp_both, a, DOWN_ROWS, preferred_element_type=F32).astype(BF) for a in actives
    ]
    grad_ups = [
        (jnp.dot(grad_mlp_both, w, preferred_element_type=F32) * s).astype(BF) for w, s in zip(down_pieces, up_slopes)
    ]
    grad_up = [lax.dot_general(two_both, g, DOWN_ROWS, preferred_element_type=F32).astype(BF) for g in grad_ups]
    grad_two = sum(lax.dot_general(g, w, ACROSS, preferred_element_type=F32) for g, w in zip(grad_ups, up_pieces))
    grad_two = grad_two[:tokens] + core_swap(grad_two[tokens:].astype(BF)).astype(F32)
    grad_after = grad_out + normalise_back(grad_two, unit_two, std_two, gain_two)
    out_down = return_mlp_grad(grad_down)
    out_up = return_mlp_grad(grad_up)

    grad_att = grad_after.astype(BF)

    def return_rows(parts):
        whole = jnp.concatenate(parts, axis=0)
        return lax.psum_scatter(whole, ("tensor", "dp", "strip"), scatter_dimension=0, tiled=True).astype(F32)

    out_proj = return_rows(
        [lax.dot_general(grad_att, attention[z], DOWN_ROWS, preferred_element_type=F32).astype(BF) for z in range(zs)]
    )
    grad_mixed = [
        jnp.dot(grad_att, proj_whole[z], preferred_element_type=F32).astype(BF).reshape(tokens, 1, 2, group)
        for z in range(zs)
    ]
    grad_mixed = to_heads(grad_mixed)[:, :, 0]
    grad_probs = jnp.einsum("bqhe,bkhe->bhqk", grad_mixed, v, preferred_element_type=F32)
    row_dot = jnp.sum(probs * grad_probs, axis=-1, keepdims=True)
    grad_scores = (probs * (grad_probs - row_dot)).astype(BF)
    grad_q = jnp.einsum("bhqk,bkhe->bqhe", grad_scores, k, preferred_element_type=F32) * score_scale
    grad_k = jnp.einsum("bhqk,bqhe->bkhe", grad_scores, q, preferred_element_type=F32) * score_scale
    grad_v = jnp.einsum("bhqk,bqhe->bkhe", probs_low, grad_mixed, preferred_element_type=F32)
    grad_qkv = to_tokens(jnp.stack([grad_q, grad_k, grad_v], axis=2).astype(BF))
    out_qkv = return_rows(
        [lax.dot_general(normed_one, grad_qkv[z], DOWN_ROWS, preferred_element_type=F32).astype(BF) for z in range(zs)]
    )
    grad_one = sum(
        lax.dot_general(grad_qkv[z], qkv_whole[z], ACROSS, preferred_element_type=F32) for z in range(zs)
    )
    grad_joined = grad_after + normalise_back(grad_one, unit_one, std_one, gain_one)
    grad_vit = to_grid(grad_joined)

    grad_grid = grad_joined.reshape(grid_shape)
    over = (0, 1, 2)
    grad_gate = jnp.sum(grad_grid * local_mix, axis=over) * (1.0 - gate * gate)
    grad_mix = grad_grid * gate
    grad_adapted = depthwise3(rim(grad_mix), mix_kernel[:, ::-1], grid_rows, grid_cols)
    grad_adapted = grad_adapted.astype(BF).reshape(tokens, width)
    grad_taps = [
        jnp.sum(adapted_pad[:, i : i + grid_rows, j : j + grid_cols] * grad_mix, axis=over)
        for i in range(3)
        for j in range(3)
    ]
    small_vit = jnp.stack(
        grad_taps
        + [
            grad_gate,
            jnp.sum(grad_one * unit_one, axis=0),
            jnp.sum(grad_one, axis=0),
            jnp.sum(grad_two * unit_two, axis=0),
            jnp.sum(grad_two, axis=0),
        ],
        axis=0,
    )
    grad_adapt = lax.dot_general(pooled_low, grad_adapted, DOWN_ROWS, preferred_element_type=F32).astype(BF)
    grad_adapt = lax.psum_scatter(grad_adapt, ("dp", "strip"), scatter_dimension=0, tiled=True)
    out_adapt = all_sum(grad_adapt.astype(F32), ("tensor",))
    grad_pooled = lax.dot_general(grad_adapted, adapt_w, ACROSS, preferred_element_type=F32).astype(BF)
    grad_pooled = grad_pooled.reshape(items, -1, channels)
    grad_pooled = jnp.concatenate(
        [shift(grad_pooled, "tensor", 1), grad_pooled, shift(grad_pooled, "tensor", -1)], axis=1
    )
    grad_map = lax.dot_general(pool, grad_pooled, (((1,), (1,)), ((0,), (0,))), preferred_element_type=F32)
    grad_map = jnp.swapaxes(d_map, 1, 2).astype(F32) + grad_map.reshape(masked.shape)

    kept = cell_mask * grad_map
    grad_scale = jnp.sum(kept * branch, axis=over)
    grad_branch = (kept * layer_scale).astype(BF).reshape(cells, channels)
    grad_branch_both = jnp.concatenate([grad_branch, core_swap(grad_branch)], axis=0)
    grad_reduce = [
        lax.dot_general(grad_branch_both, a, DOWN_ROWS, preferred_element_type=F32).astype(BF) for a in acts
    ]
    out_reduce = return_conv_grad(grad_reduce)
    grad_hidden = [
        (jnp.dot(grad_branch_both, w, preferred_element_type=F32) * s.astype(F32)).astype(BF)
        for w, s in zip(reduce_pieces, slopes)
    ]
    grad_expand = [
        lax.dot_general(normed_both, g, DOWN_ROWS, preferred_element_type=F32).astype(BF) for g in grad_hidden
    ]
    out_expand = return_conv_grad(grad_expand)
    normed_there = core_swap(back_sum(grad_hidden, expand_pieces, cells, cells, BF))
    grad_normed = back_sum(grad_hidden, expand_pieces, 0, cells, F32) + normed_there.astype(F32)
    unit_full = conv_unit.astype(F32)
    grad_spread = normalise_back(grad_normed, unit_full, conv_std, conv_gain)
    grad_spread = grad_spread.astype(BF).reshape(masked.shape)
    grad_taps = tap_grad(padded, grad_spread.astype(F32), map_rows, map_cols)
    small_conv = jnp.concatenate(
        [
            grad_taps.reshape(56, channels),
            jnp.sum(grad_normed * unit_full, axis=0)[None],
            jnp.sum(grad_normed, axis=0)[None],
            grad_scale[None],
        ],
        axis=0,
    )
    grad_map_in = conv7(wide_rim(grad_spread), taps[::-1, [6, 5, 4, 3, 2, 1, 0, 7]], map_rows, map_cols)
    grad_map_in = jnp.swapaxes(cell_mask * (kept + grad_map_in), 1, 2)

    everywhere = ("strip", "tensor", "dp")
    small_vit = all_sum(small_vit, everywhere)
    small_conv = all_sum(small_conv, everywhere)
    vit_share = width // (2 * dps)
    small_vit = lax.dynamic_slice_in_dim(small_vit, (dp_at * 2 + strip_at) * vit_share, vit_share, 1)
    conv_share = channels // (2 * zs)
    small_conv = lax.dynamic_slice_in_dim(small_conv, (strip_at * zs + tensor_at) * conv_share, conv_share, 1)
    out_taps = small_conv[:56].reshape(7, 8, conv_share)[:, :7].reshape(49, conv_share).T
    return (
        vit_out,
        map_out,
        grad_vit,
        grad_map_in,
        out_taps,
        small_conv[56],
        small_conv[57],
        out_expand,
        out_reduce,
        small_conv[58],
        out_adapt,
        small_vit[:9].T,
        small_vit[9],
        small_vit[10],
        small_vit[11],
        out_qkv.reshape(-1, 3, head_cols),
        out_proj,
        small_vit[12],
        small_vit[13],
        out_up,
        out_down,
    )


def solution(mesh):
    rows = P("dp", "strip", None, None)
    maps = P("dp", "strip", "tensor", None)
    conv = ("strip", "tensor")
    vit = ("dp", "strip")
    in_specs = (
        P("dp"), rows, maps, P(), P(), P(), P(conv, None), P(conv, None), P(), P(), P(), P(), P(), P(),
        P(None, None, "tensor"), P(None, "tensor"), P(), P(), P(None, "tensor"), P(None, "tensor"), rows, maps,
    )
    out_specs = (
        rows, maps, rows, maps, P(conv, None), P(conv), P(conv), P(conv, None), P(conv, None), P(conv),
        P(vit, None), P(vit, None), P(vit), P(vit), P(vit), P(vit, None, "tensor"), P(vit, "tensor"), P(vit), P(vit),
        P(vit, "tensor"), P(vit, "tensor"),
    )
    return jax.shard_map(shards, mesh=mesh, in_specs=in_specs, out_specs=out_specs, check_vma=False)
```

```python
import functools

import jax
import jax.numpy as jnp
from jax import lax
from jax.experimental import pallas as pl
from jax.experimental.pallas import tpu as pltpu
from jax.sharding import PartitionSpec as P

HD = 64
G = 24
MAXS = 48
EPS = 1e-06
BF = jnp.bfloat16
F32 = jnp.float32
DOWN_ROWS = (((0,), (0,)), ((), ()))
ACROSS = (((1,), (1,)), ((), ()))
VMEM = 48 * 2**20
EDGE = 8
LIGHT = pl.CostEstimate(flops=1, bytes_accessed=1, transcendentals=0)


def core_swap(v):
    return lax.ppermute(v, "strip", [(0, 1), (1, 0)])


def dp_swap(v, bit):
    return lax.ppermute(v, "dp", [(i, i ^ bit) for i in range(lax.axis_size("dp"))])


def shift(v, axis, step):
    count = lax.axis_size(axis)
    pairs = [(i, i + step) for i in range(count) if 0 <= i + step < count]
    return lax.ppermute(v, axis, pairs)


def all_sum(v, axes):
    for axis in axes:
        count, bit = lax.axis_size(axis), 1
        while bit < count:
            v = v + lax.ppermute(v, axis, [(i, i ^ bit) for i in range(count)])
            bit *= 2
    return v


def gather_bits(v, axis="tensor"):
    count, at, bit = lax.axis_size(axis), lax.axis_index(axis), 1
    while bit < count:
        other = lax.ppermute(v, axis, [(i, i ^ bit) for i in range(count)])
        upper = (at // bit) % 2 == 1
        v = jnp.concatenate([jnp.where(upper, other, v), jnp.where(upper, v, other)], axis=1)
        bit *= 2
    return v


def quarters():
    return 4 if lax.axis_size("dp") == 4 else 1


def reduce_dp(near_a, near_b, keep_a, keep_b):
    near_a, near_b = dp_swap(near_a, 1), dp_swap(near_b, 2)

    def first(*waits):
        a, b = later(near_a, *waits), later(near_b, *waits)
        sent = add(keep_a[1], a[1]).astype(BF), add(keep_b[1], b[1]).astype(BF)
        last_a, last_b = dp_swap(sent[0], 2), dp_swap(sent[1], 1)

        def second(*waits):
            got_a, got_b = later(last_a, *waits), later(last_b, *waits)
            return add(keep_a[0], a[0], got_a).astype(BF), add(keep_b[0], b[0], got_b).astype(BF)

        return sent, second

    return first


def in_order(mine, other, at):
    first = at == 0
    return jnp.stack([jnp.where(first, mine, other), jnp.where(first, other, mine)], axis=0)


def dp_order(pieces):
    at = lax.axis_index("dp")
    bit_x, bit_y = at % 2 == 1, at // 2 == 1
    row_own = [jnp.where(bit_x, pieces[1], pieces[0]), jnp.where(bit_x, pieces[0], pieces[1])]
    row_far = [jnp.where(bit_x, pieces[3], pieces[2]), jnp.where(bit_x, pieces[2], pieces[3])]
    return jnp.stack(
        [jnp.where(bit_y, f, o) for o, f in zip(row_own, row_far)]
        + [jnp.where(bit_y, o, f) for o, f in zip(row_own, row_far)],
        axis=0,
    )


def later(v, *others):
    return lax.optimization_barrier((v, *others))[0]


def add(*terms):
    return functools.reduce(lambda a, b: a + b, [t.astype(F32) for t in terms])


def at_index(v, i, axis=0):
    return lax.dynamic_index_in_dim(v, i, axis, keepdims=False)


def hidden_share(block, strip_at, part, q):
    width = block.shape[1] // (2 * q)
    return lax.dynamic_slice_in_dim(block, (strip_at * q + part) * width, width, 1)


def gather_conv_weight(block):
    q = quarters()
    strip_at = lax.axis_index("strip")
    parts = [0] if q == 1 else [lax.axis_index("dp"), lax.axis_index("dp") ^ 3]
    mine = [hidden_share(block, strip_at, part, q) for part in parts]
    width = mine[0].shape[1]
    others = core_swap(jnp.concatenate([hidden_share(block, 1 - strip_at, part, q) for part in parts], axis=1))
    both = [in_order(own, others[:, i * width : (i + 1) * width], strip_at) for i, own in enumerate(mine)]

    def along_z(i, *waits):
        whole = lax.all_gather(both[i], "tensor", axis=0)
        whole = later(whole, *waits) if waits else whole
        return jnp.swapaxes(whole, 0, 1).reshape(-1, width)

    return along_z


def dp_neighbours(own):
    return [] if quarters() == 1 else [dp_swap(own, 1), dp_swap(own, 2)]


def conv_terms(left, rights, in_turn):
    if len(rights) == 1:
        return [lax.dot_general(left, rights[0], DOWN_ROWS, preferred_element_type=F32).astype(BF)]
    own, beside_x, beside_y, far = rights
    near = tall(in_turn(left), [beside_x, beside_y, far], [(0, 2), (1, 2)], "tall_near")
    keep = tall(later(left, near[0]), [own, beside_x, beside_y], [(0, 2), (0, 1)], "tall_keep")
    return [*near, *keep]


def conv_halves(halves):
    zs = lax.axis_size("tensor")
    rows = halves[0].shape[0] // zs
    view = jnp.concatenate([h[z * rows : (z + 1) * rows] for z in range(zs) for h in halves], axis=0)
    return lax.psum_scatter(view, "tensor", scatter_dimension=0, tiled=True).reshape(2, rows, -1)


def conv_rows(part, waits=()):
    strip_at = lax.axis_index("strip")
    mine = at_index(part, strip_at)
    other = core_swap(at_index(part, 1 - strip_at))
    both = in_order(mine, other, strip_at)
    if quarters() == 1:
        return jnp.concatenate(list(lax.psum(both, "dp")), axis=1).astype(F32)
    near = [dp_swap(both, k) for k in (1, 2, 3)]
    every = dp_order([both] + [later(n, *waits) if waits else n for n in near])
    return jnp.concatenate([every[d, c] for c in range(2) for d in range(4)], axis=1).astype(F32)


def gather_mlp_weights(up, down):
    q = quarters()
    strip_at, dp_at = lax.axis_index("strip"), lax.axis_index("dp") if q > 1 else 0
    mine = jnp.concatenate([hidden_share(w, strip_at, dp_at, q) for w in (up, down)], axis=0)
    whole = lax.all_gather(mine, "tensor", axis=0)
    return jnp.concatenate(list(whole), axis=1).reshape(2, up.shape[0], -1)


def mlp_far(near):
    return [dp_swap(near[0][0], 2), dp_swap(near[1][1], 1)] if near else []


def mlp_scatter(own, dps):
    width, all_cols = own[0].shape
    zs = lax.axis_size("tensor")
    cols = all_cols // zs
    view = jnp.concatenate([v[:, z * cols : (z + 1) * cols] for z in range(zs) for v in own], axis=0)
    part = lax.psum_scatter(view, "tensor", scatter_dimension=0, tiled=True)
    return part.reshape(2, dps * 2, -1, cols)


def mlp_rows(part, dps):
    rows, cols = part.shape[2:]
    if quarters() > 1:
        parts = lax.all_to_all(part, ("dp", "strip"), 0, 0).reshape(dps, 2, 2, rows, cols)
        return [
            jnp.concatenate([parts[d, c, i] for c in range(2) for d in range(dps)], axis=1).astype(F32) for i in range(2)
        ]
    strip_at = lax.axis_index("strip")
    part = lax.psum_scatter(part.reshape(dps, 2, 2, rows, cols), "dp", scatter_dimension=0)
    mine = at_index(part, strip_at)
    other = core_swap(at_index(part, 1 - strip_at))
    both = in_order(mine, other, strip_at)
    return [jnp.concatenate([both[0, i], both[1, i]], axis=1).astype(F32) for i in range(2)]


def rows_layout(whole):
    zs, dps = lax.axis_size("tensor"), lax.axis_size("dp")
    cut = min(w.shape[1] for w in whole) // zs
    return [w.reshape(dps, 2, -1, w.shape[1]) for w in whole], cut


def rows_scatter(whole):
    zs, dps, strip_at = lax.axis_size("tensor"), lax.axis_size("dp"), lax.axis_index("strip")
    view, cut = rows_layout(whole)

    def of_core(core):
        parts = [at_index(v, core, 1) for v in view]
        groups = []
        for z in range(zs):
            group = []
            for v in parts:
                share = v.shape[2] // zs
                group += [v[:, :, z * share + c : z * share + c + cut] for c in range(0, share, cut)]
            groups.append(jnp.concatenate(group, axis=1))
        return jnp.concatenate(groups, axis=0)

    sums = add(of_core(strip_at), core_swap(of_core(1 - strip_at))).astype(BF)
    part = lax.psum_scatter(sums.reshape(-1, cut), "tensor", scatter_dimension=0, tiled=True)
    return sums, part.reshape(dps, -1, cut)


def rows_sum(whole, part):
    zs, dp_at = lax.axis_size("tensor"), lax.axis_index("dp")
    view, cut = rows_layout(whole)
    if quarters() == 1:
        total = lax.psum_scatter(part, "dp", scatter_dimension=0).astype(F32)
    else:
        total = add(at_index(part, dp_at), *[dp_swap(at_index(part, dp_at ^ k), k) for k in (1, 2, 3)])
    outs, at = [], 0
    for v in view:
        rows = v.shape[2]
        count = v.shape[3] // zs // cut
        outs.append(jnp.concatenate([total[at + i * rows : at + (i + 1) * rows] for i in range(count)], axis=1))
        at += count * rows
    return outs


def scatter_small(v, order):
    for axis in order:
        count, bit, at = lax.axis_size(axis), lax.axis_size(axis) // 2, lax.axis_index(axis)
        while bit >= 1:
            half = v.shape[1] // 2
            upper = (at // bit) % 2
            mine = lax.dynamic_slice_in_dim(v, upper * half, half, 1)
            other = lax.dynamic_slice_in_dim(v, (1 - upper) * half, half, 1)
            v = mine + lax.ppermute(other, axis, [(i, i ^ bit) for i in range(count)])
            bit //= 2
    return all_sum(v, [a for a in ("strip", "tensor", "dp") if a not in order])


def gather_rows(block):
    width, cols = block.shape[-2:]
    dps, zs = lax.axis_size("dp"), lax.axis_size("tensor")
    rows = width // (2 * dps)
    at = lax.axis_index("dp") * 2 + lax.axis_index("strip")
    mine = lax.dynamic_slice_in_dim(block.reshape(-1, width, cols), at * rows, rows, 1)
    whole = lax.all_gather(mine, ("tensor", "dp", "strip"), axis=0).reshape(zs, 2 * dps, -1, rows, cols)
    return jnp.concatenate([whole[:, :, a].reshape(zs, width, cols) for a in range(whole.shape[2])], axis=2)


def params(limit=VMEM):
    return pltpu.CompilerParams(vmem_limit_bytes=limit)


def conv7_kernel(rows, cols, x_ref, k_ref, out_ref, wide):
    wide[...] = x_ref[0].astype(F32)

    def tap_row(i, sums):
        sums = list(sums)
        taps = k_ref[i]
        for m in range(cols + 6):
            x = wide[m, pl.ds(i + EDGE - 3, rows), :]
            for j in range(7):
                c = m - j
                if 0 <= c < cols:
                    sums[c] = sums[c] + x * taps[j : j + 1]
        return tuple(sums)

    sums = lax.fori_loop(0, 7, tap_row, tuple(jnp.zeros((rows, 128), F32) for _ in range(cols)))
    for c in range(cols):
        out_ref[0, c] = sums[c]


def conv7(padded, taps, rows, cols):
    items, _, _, channels = padded.shape
    return pl.pallas_call(
        functools.partial(conv7_kernel, rows, cols),
        grid=(items, channels // 128),
        in_specs=[
            pl.BlockSpec((1, cols + 6, rows + 2 * EDGE, 128), lambda b, c: (b, 0, 0, c)),
            pl.BlockSpec((7, 8, 128), lambda b, c: (0, 0, c)),
        ],
        out_specs=pl.BlockSpec((1, cols, rows, 128), lambda b, c: (b, 0, 0, c)),
        out_shape=jax.ShapeDtypeStruct((items, cols, rows, channels), F32),
        scratch_shapes=[pltpu.VMEM((cols + 6, rows + 2 * EDGE, 128), F32)],
        compiler_params=params(8 * 2**20),
        cost_estimate=LIGHT,
        name="depthwise",
    )(padded, taps)


def tap_grad_kernel(rows, cols, x_ref, g_ref, out_ref, wide, full):
    wide[...] = x_ref[0].astype(F32)
    full[...] = g_ref[0].astype(F32)

    @pl.when(pl.program_id(1) == 0)
    def _():
        out_ref[...] = jnp.zeros_like(out_ref)

    def tap_row(i, _):
        sums = [jnp.zeros((8, 128), F32) for _ in range(7)]
        grads = [full[c] for c in range(cols)]
        for m in range(cols + 6):
            x = wide[m, pl.ds(i + EDGE - 3, rows), :]
            for j in range(7):
                c = m - j
                if 0 <= c < cols:
                    sums[j] = sums[j] + (x * grads[c]).reshape(rows // 8, 8, 128).sum(axis=0)
        lines = [jnp.sum(s, axis=0, keepdims=True) for s in sums]
        out_ref[i] += jnp.concatenate(lines + [jnp.zeros((1, 128), F32)], axis=0)
        return 0

    lax.fori_loop(0, 7, tap_row, 0)


def tap_grad(padded, grad, rows, cols):
    items, _, _, channels = padded.shape
    return pl.pallas_call(
        functools.partial(tap_grad_kernel, rows, cols),
        grid=(channels // 128, items),
        in_specs=[
            pl.BlockSpec((1, cols + 6, rows + 2 * EDGE, 128), lambda c, b: (b, 0, 0, c)),
            pl.BlockSpec((1, cols, rows, 128), lambda c, b: (b, 0, 0, c)),
        ],
        out_specs=pl.BlockSpec((7, 8, 128), lambda c, b: (0, 0, c)),
        out_shape=jax.ShapeDtypeStruct((7, 8, channels), F32),
        scratch_shapes=[pltpu.VMEM((cols + 6, rows + 2 * EDGE, 128), F32), pltpu.VMEM((cols, rows, 128), F32)],
        compiler_params=params(8 * 2**20),
        cost_estimate=LIGHT,
        name="tap_grad",
    )(padded, grad)


def norm_kernel(v_ref, gain_ref, bias_ref, out_ref):
    unit, _ = normalise(v_ref[...])
    out_ref[...] = (unit * gain_ref[...] + bias_ref[...]).astype(BF)


def norm_rows(v, gain, bias):
    rows, width = v.shape
    block = row_block(rows, 144)
    tile, line = pl.BlockSpec((block, width), lambda i: (i, 0)), pl.BlockSpec((1, width), lambda i: (0, 0))
    return pl.pallas_call(
        norm_kernel,
        grid=(rows // block,),
        in_specs=[tile, line, line],
        out_specs=tile,
        out_shape=jax.ShapeDtypeStruct((rows, width), BF),
        compiler_params=params(16 * 2**20),
        cost_estimate=LIGHT,
        name="norm",
    )(v, gain.reshape(1, width), bias.reshape(1, width))


def norm_back_kernel(here_ref, there_ref, v_ref, gain_ref, out_ref, sums_ref):
    @pl.when(pl.program_id(0) == 0)
    def _():
        sums_ref[...] = jnp.zeros_like(sums_ref)

    grad = here_ref[...] + there_ref[...].astype(F32)
    unit, scale = normalise(v_ref[...])
    sums_ref[...] += lines(jnp.sum(grad * unit, axis=0, keepdims=True), jnp.sum(grad, axis=0, keepdims=True))
    out_ref[...] = normalise_back(grad, unit, scale, gain_ref[...]).astype(BF)


def norm_rows_back(here, there, v, gain):
    rows, width = v.shape
    block = row_block(rows, 144)
    tile, line = pl.BlockSpec((block, width), lambda i: (i, 0)), pl.BlockSpec((1, width), lambda i: (0, 0))
    return pl.pallas_call(
        norm_back_kernel,
        grid=(rows // block,),
        in_specs=[tile, tile, tile, line],
        out_specs=[tile, pl.BlockSpec((8, width), lambda i: (0, 0))],
        out_shape=[jax.ShapeDtypeStruct((rows, width), BF), jax.ShapeDtypeStruct((8, width), F32)],
        compiler_params=params(20 * 2**20),
        cost_estimate=LIGHT,
        name="norm_back",
    )(here, there, v, gain.reshape(1, width))


def gelu_pair(h):
    cdf = 0.5 * (1.0 + lax.erf(h * (0.5**0.5)))
    pdf = jnp.exp(h * h * -0.5) * 0.3989422804014327
    return h * cdf, cdf + h * pdf


def expand_kernel(step, x_ref, w_ref, act_ref, slope_ref):
    x = x_ref[...]
    for at in range(0, w_ref.shape[1], step):
        h = jnp.dot(x, w_ref[:, at : at + step], preferred_element_type=F32)
        act, slope = gelu_pair(h)
        act_ref[:, at : at + step] = act.astype(BF)
        slope_ref[:, at : at + step] = slope.astype(BF)


def row_block(rows, most):
    best = 16
    for block in range(16, most + 1, 16):
        if rows % block == 0:
            best = block
    return best


def expand(x, w):
    m, k = x.shape
    n = w.shape[1]
    bm = row_block(m, 432)
    bn = min(n, 768)
    spec = pl.BlockSpec((bm, bn), lambda j, i: (i, j))
    return pl.pallas_call(
        functools.partial(expand_kernel, 256),
        grid=(n // bn, m // bm),
        in_specs=[pl.BlockSpec((bm, k), lambda j, i: (i, 0)), pl.BlockSpec((k, bn), lambda j, i: (0, j))],
        out_specs=[spec, spec],
        out_shape=[jax.ShapeDtypeStruct((m, n), BF)] * 2,
        compiler_params=params(20 * 2**20),
        cost_estimate=LIGHT,
        name="expand_gelu",
    )(x, w)


def back_sum_kernel(count, *refs):
    out_ref = refs[-1]
    total = None
    for a_ref, w_ref in zip(refs[:count], refs[count : 2 * count]):
        term = lax.dot_general(a_ref[...], w_ref[...], ACROSS, preferred_element_type=F32)
        total = term if total is None else total + term
    out_ref[...] = total.astype(out_ref.dtype)


def back_sum(parts, weights, first, rows, dtype):
    n = weights[0].shape[0]
    ks = [w.shape[1] for w in weights]
    bm = row_block(rows, 432)
    bn = 512
    skip = first // bm
    return pl.pallas_call(
        functools.partial(back_sum_kernel, len(parts)),
        grid=(n // bn, rows // bm),
        in_specs=[pl.BlockSpec((bm, k), lambda j, i: (i + skip, 0)) for k in ks]
        + [pl.BlockSpec((bn, k), lambda j, i: (j, 0)) for k in ks],
        out_specs=pl.BlockSpec((bm, bn), lambda j, i: (i, j)),
        out_shape=jax.ShapeDtypeStruct((rows, n), dtype),
        compiler_params=params(24 * 2**20),
        cost_estimate=LIGHT,
        name="reduce_sum",
    )(*parts, *weights)


def tall(a, rights, uses, name):
    m, n = a.shape
    cols = rights[0].shape[1]
    bm = 256
    steps = n // 2 // bm

    def kernel(a_ref, *refs):
        outs = refs[-2:]
        for half in range(2):

            @pl.when(pl.program_id(0) // steps == half)
            def _():
                left = a_ref[...]
                for i, use in enumerate(uses[half]):
                    outs[half][i] = lax.dot_general(left, refs[use][...], DOWN_ROWS, preferred_element_type=F32).astype(BF)

    def out_spec(half):
        place = lambda i: (0, jnp.clip(i - half * steps, 0, steps - 1), 0)
        return pl.BlockSpec((len(uses[half]), bm, cols), place)

    return pl.pallas_call(
        kernel,
        grid=(2 * steps,),
        in_specs=[pl.BlockSpec((m, bm), lambda i: (0, i))] + [pl.BlockSpec((m, cols), lambda i: (0, 0)) for _ in rights],
        out_specs=[out_spec(0), out_spec(1)],
        out_shape=[jax.ShapeDtypeStruct((len(u), n // 2, cols), BF) for u in uses],
        compiler_params=params(28 * 2**20),
        cost_estimate=LIGHT,
        name=name,
    )(a, *rights)


def back_slope(a, w, slope):
    m, k = a.shape
    n = w.shape[1]
    bm, bn = row_block(m, 432), min(n, 768)

    def kernel(a_ref, w_ref, s_ref, out_ref):
        left = a_ref[...]
        for at in range(0, bn, 256):
            cut = slice(at, at + 256)
            grad = jnp.dot(left, w_ref[:, cut], preferred_element_type=F32)
            out_ref[:, cut] = (grad * s_ref[:, cut].astype(F32)).astype(BF)

    spec = pl.BlockSpec((bm, bn), lambda j, i: (i, j))
    return pl.pallas_call(
        kernel,
        grid=(n // bn, m // bm),
        in_specs=[pl.BlockSpec((bm, k), lambda j, i: (i, 0)), pl.BlockSpec((k, bn), lambda j, i: (0, j)), spec],
        out_specs=spec,
        out_shape=jax.ShapeDtypeStruct((m, n), BF),
        compiler_params=params(20 * 2**20),
        cost_estimate=LIGHT,
        name="back_slope",
    )(a, w, slope)


def whole_call(kernel, outs, args, flops, name):
    vmem = pl.BlockSpec(memory_space=pltpu.VMEM)
    bytes_accessed = sum(a.size * a.dtype.itemsize for a in args) + sum(o.size * o.dtype.itemsize for o in outs)
    return pl.pallas_call(
        kernel,
        in_specs=[vmem] * len(args),
        out_specs=[vmem] * len(outs),
        out_shape=outs,
        compiler_params=params(36 * 2**20),
        cost_estimate=LIGHT,
        name=name,
    )(*args)


def shape(dtype, *dims):
    return jax.ShapeDtypeStruct(dims, dtype)


def qkv_kernel(zs, group, joined_ref, gain_ref, bias_ref, w_ref, normed_ref, out_ref):
    unit, _ = normalise(joined_ref[...])
    normed = (unit * gain_ref[...] + bias_ref[...]).astype(BF)
    normed_ref[...] = normed
    for z in range(zs):
        part = jnp.dot(normed, w_ref[z], preferred_element_type=F32).astype(BF)
        for a in range(3):
            for core in range(2):
                at = (2 * a + core) * group
                out_ref[core * zs + z, :, a * group : (a + 1) * group] = part[:, at : at + group]


def tokens_of(ref):
    v = ref[:, 0].astype(F32)
    return v.reshape(v.shape[0] * v.shape[1], v.shape[2]).astype(BF)


def head_lanes(heads, lanes):
    lane = lax.broadcasted_iota(jnp.int32, (1, lanes), 1)
    return [jnp.logical_and(lane >= h * HD, lane < (h + 1) * HD) for h in range(heads)]


def only(lanes, v):
    return jnp.where(lanes, v, jnp.zeros((), v.dtype))


def head_probs(q, k):
    scores = lax.dot_general(q, k, ACROSS, preferred_element_type=F32) * HD**-0.5
    powers = jnp.exp(scores - jnp.max(scores, axis=-1, keepdims=True))
    return powers * (1.0 / jnp.sum(powers, axis=-1, keepdims=True))


def attention_kernel(group, qkv_ref, out_ref):
    qkv = tokens_of(qkv_ref)
    q, k, v = (qkv[:, a * group : (a + 1) * group] for a in range(3))
    mixed = jnp.zeros(v.shape, F32)
    for lanes in head_lanes(group // HD, group):
        probs = head_probs(only(lanes, q), k).astype(BF)
        mixed = jnp.where(lanes, jnp.dot(probs, v, preferred_element_type=F32), mixed)
    out_ref[:, 0] = mixed.reshape(out_ref.shape[0], out_ref.shape[2], group).astype(BF)


def attention_back_kernel(group, qkv_ref, grad_ref, out_ref):
    qkv = tokens_of(qkv_ref)
    grad = tokens_of(grad_ref)
    q, k, v = (qkv[:, a * group : (a + 1) * group] for a in range(3))
    sums = [jnp.zeros(v.shape, F32) for _ in range(3)]
    for lanes in head_lanes(group // HD, group):
        probs = head_probs(only(lanes, q), k)
        grad_h = only(lanes, grad)
        grad_probs = lax.dot_general(grad_h, v, ACROSS, preferred_element_type=F32)
        along = jnp.sum(probs * grad_probs, axis=-1, keepdims=True)
        grad_scores = (probs * (grad_probs - along)).astype(BF)
        terms = (
            jnp.dot(grad_scores, k, preferred_element_type=F32) * HD**-0.5,
            lax.dot_general(grad_scores, q, DOWN_ROWS, preferred_element_type=F32) * HD**-0.5,
            lax.dot_general(probs.astype(BF), grad, DOWN_ROWS, preferred_element_type=F32),
        )
        sums = [jnp.where(lanes, term, total) for term, total in zip(terms, sums)]
    for a, total in enumerate(sums):
        part = total.reshape(out_ref.shape[0], out_ref.shape[2], group).astype(BF)
        out_ref[:, 0, :, a * group : (a + 1) * group] = part


def by_item(kernel, arrays, lanes, flops, name):
    sources, items, tokens, _ = arrays[0].shape
    block = lambda n: pl.BlockSpec((sources, 1, tokens, n), lambda b: (0, b, 0, 0))
    return pl.pallas_call(
        kernel,
        grid=(items,),
        in_specs=[block(v.shape[3]) for v in arrays],
        out_specs=block(lanes),
        out_shape=shape(BF, sources, items, tokens, lanes),
        compiler_params=params(28 * 2**20),
        cost_estimate=LIGHT,
        name=name,
    )(*arrays)


def project_kernel(zs, group, heads_ref, w_ref, joined_ref, gain_ref, bias_ref, mixed_ref, after_ref, normed_ref):
    total = joined_ref[...]
    for z in range(zs):
        mixed = jnp.concatenate([heads_ref[z], heads_ref[zs + z]], axis=1)
        mixed_ref[:, z * 2 * group : (z + 1) * 2 * group] = mixed
        total = total + lax.dot_general(mixed, w_ref[z], ACROSS, preferred_element_type=F32)
    after_ref[...] = total
    unit, _ = normalise(total)
    normed_ref[...] = (unit * gain_ref[...] + bias_ref[...]).astype(BF)


def mlp_kernel(count, x_ref, g_ref, *refs):
    given = 1 if count == 1 else count + 1
    weights = [(r.at[0], r.at[1]) for r in refs[: count - 1 or 1]]
    if count > 1:
        weights.append((refs[count - 1], refs[count]))
    out_ref, back_ref = refs[given : given + 2]
    acts, grads = refs[given + 2 : given + 2 + count], refs[given + 2 + count :]
    x, g = x_ref[...], g_ref[...]
    for p, (up, down) in enumerate(weights):
        act, slope = gelu_pair(jnp.dot(x, up[...], preferred_element_type=F32))
        act = act.astype(BF)
        acts[p][...] = act
        grad = (jnp.dot(g, down[...], preferred_element_type=F32) * slope).astype(BF)
        grads[p][...] = grad
        out = lax.dot_general(act, down[...], ACROSS, preferred_element_type=F32)
        back = lax.dot_general(grad, up[...], ACROSS, preferred_element_type=F32)
        if p == 0:
            out_ref[...] = out
            back_ref[...] = back
        else:
            out_ref[...] += out
            back_ref[...] += back


def lines(*rows):
    width = rows[0].shape[1]
    return jnp.concatenate(list(rows) + [jnp.zeros((8 - len(rows), width), F32)], axis=0)


def norm_back_two_kernel(zs, group, here_ref, there_ref, after_ref, d_ref, gain_ref, w_ref, grad_ref, low_ref, sums_ref, out_ref):
    grad_two = here_ref[...] + there_ref[...].astype(F32)
    unit, scale = normalise(after_ref[...])
    sums_ref[...] = lines(jnp.sum(grad_two * unit, axis=0, keepdims=True), jnp.sum(grad_two, axis=0, keepdims=True))
    grad = d_ref[...] + normalise_back(grad_two, unit, scale, gain_ref[...])
    grad_ref[...] = grad
    low = grad.astype(BF)
    low_ref[...] = low
    for z in range(zs):
        part = jnp.dot(low, w_ref[z], preferred_element_type=F32).astype(BF)
        for core in range(2):
            out_ref[core * zs + z] = part[:, core * group : (core + 1) * group]


def norm_back_one_kernel(zs, group, g_ref, w_ref, joined_ref, after_ref, gain_ref, all_ref, grad_ref, sums_ref):
    grad_one = jnp.zeros(joined_ref.shape, F32)
    for z in range(zs):
        part = jnp.concatenate(
            [g_ref[core * zs + z, :, a * group : (a + 1) * group] for a in range(3) for core in range(2)], axis=1
        )
        all_ref[:, z * 6 * group : (z + 1) * 6 * group] = part
        grad_one = grad_one + lax.dot_general(part, w_ref[z], ACROSS, preferred_element_type=F32)
    unit, scale = normalise(joined_ref[...])
    sums_ref[...] = lines(jnp.sum(grad_one * unit, axis=0, keepdims=True), jnp.sum(grad_one, axis=0, keepdims=True))
    grad_ref[...] = after_ref[...] + normalise_back(grad_one, unit, scale, gain_ref[...])


def normalise(v):
    center = jnp.mean(v, axis=-1, keepdims=True)
    shifted = v - center
    scale = lax.rsqrt(jnp.mean(shifted * shifted, axis=-1, keepdims=True) + EPS)
    return shifted * scale, scale


def normalise_back(g, unit, scale, gain):
    gg = g * gain
    along = jnp.mean(gg * unit, axis=-1, keepdims=True)
    return scale * (gg - jnp.mean(gg, axis=-1, keepdims=True) - unit * along)


def pool_matrix(pooled_index, buffer_index, map_side, offset):
    map_place = buffer_index[None, :] - offset
    bin_start = pooled_index[:, None] * map_side // G
    bin_stop = ((pooled_index[:, None] + 1) * map_side + G - 1) // G
    inside = jnp.logical_and(map_place >= bin_start, map_place < bin_stop)
    real = jnp.logical_and(pooled_index >= 0, pooled_index < G)[:, None]
    return jnp.where(jnp.logical_and(inside, real), 1.0, 0.0).astype(F32) / (bin_stop - bin_start).astype(F32)


def depthwise3(padded, kernel, rows, cols):
    total = None
    for i in range(3):
        for j in range(3):
            term = padded[:, i : i + rows, j : j + cols, :] * kernel[:, 3 * i + j]
            total = term if total is None else total + term
    return total


def rim(v):
    v = jnp.concatenate([shift(v[:, -1:], "strip", 1), v, shift(v[:, :1], "strip", -1)], axis=1)
    return jnp.concatenate([shift(v[:, :, -1:], "tensor", 1), v, shift(v[:, :, :1], "tensor", -1)], axis=2)


def wide_rim(v):
    v = jnp.concatenate([shift(v[:, -3:], "tensor", 1), v, shift(v[:, :3], "tensor", -1)], axis=1)
    return jnp.concatenate([shift(v[:, :, -EDGE:], "strip", 1), v, shift(v[:, :, :EDGE], "strip", -1)], axis=2)


def shards(
    res_code, vit_in, map_in, dw_kernel, conv_gain, conv_bias, w_expand, w_reduce, layer_scale, adapt_w, mix_kernel,
    gate_logit, gain_one, bias_one, w_qkv, w_proj, gain_two, bias_two, w_up, w_down, d_vit, d_map,
):
    strip_at, tensor_at, dp_at = (lax.axis_index(a) for a in ("strip", "tensor", "dp"))
    dps, zs = lax.axis_size("dp"), lax.axis_size("tensor")
    items, grid_rows, _, width = vit_in.shape
    _, map_rows, map_cols, channels = map_in.shape
    grid_cols = G // zs
    cells = items * map_rows * map_cols
    tokens = items * grid_rows * grid_cols
    head_cols = w_qkv.shape[2]
    score_scale = HD**-0.5

    expand_z, reduce_z = gather_conv_weight(w_expand), gather_conv_weight(w_reduce)
    expand_own, reduce_own = expand_z(0), reduce_z(0)
    expand_near = dp_neighbours(expand_own)
    qkv_whole = gather_rows(jnp.swapaxes(w_qkv, 0, 1))
    mlp_own = gather_mlp_weights(w_up, w_down)
    proj_whole = gather_rows(w_proj)
    count = quarters()

    side = res_code // 32
    offset = (MAXS - side) // 2
    row_cells = strip_at * map_rows + jnp.arange(map_rows, dtype=jnp.int32)
    col_cells = tensor_at * map_cols + jnp.arange(map_cols, dtype=jnp.int32)

    def inside(at):
        low, high = offset[:, None], (offset + side)[:, None]
        return jnp.logical_and(at[None] >= low, at[None] < high).astype(F32)

    row_ok, col_ok = inside(row_cells), inside(col_cells)
    cell_mask = col_ok[:, :, None, None] * row_ok[:, None, :, None]
    many_pools = jax.vmap(pool_matrix, in_axes=(None, None, 0, 0))
    pooled_rows = strip_at * grid_rows + jnp.arange(grid_rows, dtype=jnp.int32)
    pooled_cols = (tensor_at - 1) * grid_cols + jnp.arange(3 * grid_cols, dtype=jnp.int32)
    row_pool = many_pools(pooled_rows, row_cells, side, offset)
    col_pool = many_pools(pooled_cols, col_cells, side, offset).reshape(items, 3, grid_cols, map_cols)
    pool = jnp.einsum("bir,bgjc->bgijcr", row_pool, col_pool)
    pool = pool.reshape(items, 3 * grid_rows * grid_cols, map_cols * map_rows).astype(BF)

    masked = jnp.swapaxes(map_in, 1, 2) * cell_mask.astype(BF)
    padded = later(wide_rim(masked), expand_own)
    taps = jnp.pad(dw_kernel.T.reshape(7, 7, channels), ((0, 0), (0, 1), (0, 0)))
    spread = conv7(padded, taps, map_rows, map_cols).reshape(cells, channels)
    reduce_near = dp_neighbours(later(reduce_own, spread))
    normed = norm_rows(spread, conv_gain, conv_bias)
    normed_both = jnp.concatenate([normed, core_swap(normed)], axis=0)
    expand_pieces, reduce_pieces, pairs = [expand_own, *expand_near], [reduce_own, *reduce_near], []
    x = later(normed_both, *expand_near)
    for k in range(count):
        if k == 3:
            expand_pieces.append(expand_z(1, pairs[2][0]))
        pairs.append(expand(x, expand_pieces[k]))
        x = later(normed_both, pairs[k][0])
    acts, slopes = zip(*pairs)
    if count > 1:
        reduce_pieces.append(reduce_z(1, acts[3]))
    branch_there = core_swap(back_sum(acts, reduce_pieces, cells, cells, BF))
    branch_here = back_sum(acts, reduce_pieces, 0, cells, F32)
    branch = (branch_here + branch_there.astype(F32)).reshape(masked.shape)
    map_value = cell_mask * (masked.astype(F32) + layer_scale * branch)
    map_low = map_value.astype(BF)
    map_out = jnp.swapaxes(map_low, 1, 2)

    pooled3 = lax.dot_general(
        pool, map_low.reshape(items, -1, channels), (((2,), (1,)), ((0,), (0,))), preferred_element_type=F32
    ).reshape(items, 3, -1, channels)
    pooled = (
        pooled3[:, 1]
        + shift(pooled3[:, 0].astype(BF), "tensor", -1).astype(F32)
        + shift(pooled3[:, 2].astype(BF), "tensor", 1).astype(F32)
    )
    pooled_low = pooled.astype(BF).reshape(tokens, channels)
    grid_shape = (items, grid_rows, grid_cols, width)
    adapted = jnp.dot(pooled_low, adapt_w, preferred_element_type=F32).reshape(grid_shape)
    adapted_pad = rim(adapted)
    local_mix = depthwise3(adapted_pad, mix_kernel, grid_rows, grid_cols)
    gate = jnp.tanh(gate_logit)
    mine = lambda v: lax.dynamic_slice_in_dim(v, tensor_at * grid_cols, grid_cols, 2)
    grad_out = mine(d_vit).reshape(tokens, width)
    grad_mlp = grad_out.astype(BF)
    grad_mlp_both = jnp.concatenate([grad_mlp, core_swap(grad_mlp)], axis=0)
    joined = (mine(vit_in) + gate * local_mix).reshape(tokens, width)

    group = head_cols // 2
    line = lambda v: v.reshape(1, width)
    dots = lambda m, n, k: 2 * m * n * k
    spread_heads = lambda v: lax.all_to_all(v, ("strip", "tensor"), 0, 0, tiled=True)
    by_source = lambda v: v.reshape(2 * zs, items, -1, v.shape[-1])
    normed_one, qkv = whole_call(
        functools.partial(qkv_kernel, zs, group),
        [shape(BF, tokens, width), shape(BF, 2 * zs, tokens, 3 * group)],
        [joined, line(gain_one), line(bias_one), qkv_whole],
        dots(tokens, width, 3 * zs * head_cols),
        "qkv",
    )
    mlp_near = dp_neighbours(mlp_own)
    if mlp_near:
        qkv = later(qkv, *mlp_near)
    qkv = by_source(spread_heads(qkv))
    mlp_weights = [mlp_own, *mlp_near, *mlp_far(mlp_near)]
    attention_flops = items * 2 * dots(24 * 24, 24 * 24, group)
    heads = by_item(functools.partial(attention_kernel, group), [qkv], group, 2 * attention_flops, "attention")
    heads = later(heads, *mlp_weights)
    heads = spread_heads(heads).reshape(2 * zs, tokens, group)
    mixed, after_attn, normed_two = whole_call(
        functools.partial(project_kernel, zs, group),
        [shape(BF, tokens, width), shape(F32, tokens, width), shape(BF, tokens, width)],
        [heads, proj_whole, joined, line(gain_two), line(bias_two)],
        dots(tokens, width, width),
        "project",
    )

    two_both = jnp.concatenate([normed_two, core_swap(normed_two)], axis=0)
    some = mlp_own.shape[2]
    mlp, back, *halves = whole_call(
        functools.partial(mlp_kernel, count),
        [shape(F32, 2 * tokens, width)] * 2 + [shape(BF, 2 * tokens, some)] * (2 * count),
        [two_both, grad_mlp_both, *mlp_weights],
        4 * count * dots(2 * tokens, width, some),
        "mlp",
    )
    actives, grad_ups = halves[:count], halves[count:]
    back_there = core_swap(back[tokens:].astype(BF))
    grad_after, grad_att, sums_two, grad_heads = whole_call(
        functools.partial(norm_back_two_kernel, zs, group),
        [shape(F32, tokens, width), shape(BF, tokens, width), shape(F32, 8, width), shape(BF, 2 * zs, tokens, group)],
        [back[:tokens], back_there, after_attn, grad_out, line(gain_two), proj_whole],
        dots(tokens, width, width),
        "norm_back_two",
    )
    grad_heads = by_source(spread_heads(grad_heads))
    mlp_there = core_swap(mlp[tokens:].astype(BF))
    every = lambda v: lax.all_gather(v.astype(BF).reshape(grid_shape), "tensor", axis=0)
    to_grid = lambda v: jnp.concatenate(list(v), axis=2).astype(F32)
    down_terms = lambda left, rights: [
        lax.dot_general(left, r, DOWN_ROWS, preferred_element_type=F32).astype(BF) for r in rights
    ]
    grad_down = down_terms(grad_mlp_both, actives)
    grad_up = down_terms(two_both, grad_ups)

    grad_qkv = by_item(
        functools.partial(attention_back_kernel, group), [qkv, grad_heads], 3 * group, 5 * attention_flops, "attention_back"
    )
    vit_every = every(after_attn + mlp[:tokens] + later(mlp_there, grad_qkv).astype(F32))
    grad_qkv = later(spread_heads(grad_qkv).reshape(2 * zs, tokens, 3 * group), *grad_down, *grad_up)
    grad_qkv, grad_joined, sums_one = whole_call(
        functools.partial(norm_back_one_kernel, zs, group),
        [shape(BF, tokens, 3 * width), shape(F32, tokens, width), shape(F32, 8, width)],
        [grad_qkv, qkv_whole, joined, grad_after, line(gain_one)],
        dots(tokens, width, 3 * width),
        "norm_back_one",
    )
    grad_vit_every = every(grad_joined)

    grad_grid = grad_joined.reshape(grid_shape)
    over = (0, 1, 2)
    grad_gate = jnp.sum(grad_grid * local_mix, axis=over) * (1.0 - gate * gate)
    grad_mix = grad_grid * gate
    grad_adapted = depthwise3(rim(grad_mix), mix_kernel[:, ::-1], grid_rows, grid_cols)
    grad_adapted = grad_adapted.astype(BF).reshape(tokens, width)
    grad_taps = [
        jnp.sum(adapted_pad[:, i : i + grid_rows, j : j + grid_cols] * grad_mix, axis=over)
        for i in range(3)
        for j in range(3)
    ]
    small_vit = jnp.stack(
        grad_taps
        + [
            grad_gate,
            sums_one[0],
            sums_one[1],
            sums_two[0],
            sums_two[1],
        ],
        axis=0,
    )
    row_terms = down_terms(normed_one, [grad_qkv]) + down_terms(grad_att, [mixed]) + down_terms(pooled_low, [grad_adapted])
    grad_pooled = lax.dot_general(grad_adapted, adapt_w, ACROSS, preferred_element_type=F32).astype(BF)
    grad_pooled = grad_pooled.reshape(items, -1, channels)
    grad_pooled = jnp.concatenate(
        [later(shift(grad_pooled, "tensor", 1), *row_terms), grad_pooled, shift(grad_pooled, "tensor", -1)], axis=1
    )
    grad_map = lax.dot_general(pool, grad_pooled, (((1,), (1,)), ((0,), (0,))), preferred_element_type=F32)
    grad_map = jnp.swapaxes(d_map, 1, 2).astype(F32) + grad_map.reshape(masked.shape)

    kept = cell_mask * grad_map
    grad_scale = jnp.sum(kept * branch, axis=over)
    grad_branch = (kept * layer_scale).astype(BF).reshape(cells, channels)
    grad_branch_both = jnp.concatenate([grad_branch, core_swap(grad_branch)], axis=0)
    pair = lambda a, b: jnp.stack([a, b], axis=0)
    own_up, own_down = grad_up[0], grad_down[0]
    four = count > 1
    if four:
        mlp_first = reduce_dp(
            pair(grad_up[1], grad_up[3]), pair(grad_down[2], grad_down[3]), [own_up, grad_up[2]], [own_down, grad_down[1]]
        )
    rows_sums, rows_part = rows_scatter(row_terms)
    reduce_terms = conv_terms(grad_branch_both, acts, lambda v: later(v, rows_sums))
    grad_hidden, last = [], [reduce_terms[-1]]
    if four:
        reduce_first = reduce_dp(*reduce_terms)
    for k in range(count):
        if four and k == 2:
            mlp_sent, mlp_second = mlp_first(last[0])
            last += [*mlp_sent]
        last = [back_slope(later(grad_branch_both, *last), reduce_pieces[k], slopes[k])]
        grad_hidden += last
    reduce_halves = jnp.split(reduce_terms[0], 2, axis=0)
    if four:
        reduce_sent, reduce_second = reduce_first(last[0])
        last += [*reduce_sent]
    expand_terms = conv_terms(normed_both, grad_hidden, lambda v: later(v, *last))
    expand_halves = jnp.split(expand_terms[0], 2, axis=0)
    last = [expand_terms[-1], rows_part]
    if four:
        expand_first = reduce_dp(*expand_terms)
        own_up, own_down = mlp_second(expand_terms[-1])
        last += [own_up, own_down]
    mlp_part = mlp_scatter([own_up, own_down], dps)
    sent = later(grad_hidden[0], *last)
    normed_sent = back_sum([sent] + grad_hidden[1:], expand_pieces, cells, cells, BF)
    last = [normed_sent]
    if four:
        reduce_halves = reduce_second(normed_sent)
        last += [*reduce_halves]
    reduce_part = conv_halves(reduce_halves)
    normed_there = core_swap(normed_sent)
    kept_here = later(grad_hidden[0], *last)
    normed_here = back_sum([kept_here] + grad_hidden[1:], expand_pieces, 0, cells, F32)
    last = [normed_here]
    if four:
        expand_sent, expand_second = expand_first(normed_here)
        last += [*expand_sent]
    grad_spread, sums_conv = norm_rows_back(later(normed_here, *last), normed_there, spread, conv_gain)
    grad_spread = grad_spread.reshape(masked.shape)
    mlp_part = later(mlp_part, grad_spread)
    mlp_turned = jnp.swapaxes(mlp_part, 0, 1)
    grad_taps = tap_grad(padded, later(grad_spread, mlp_turned), map_rows, map_cols)
    if four:
        expand_halves = expand_second(grad_taps)
    expand_part = conv_halves(expand_halves)
    out_qkv, out_proj, out_adapt = rows_sum(row_terms, later(rows_part, grad_taps))
    out_reduce = conv_rows(later(reduce_part, grad_taps))
    grad_map_in = conv7(
        later(wide_rim(grad_spread), *expand_halves, out_reduce, out_qkv), taps[::-1, [6, 5, 4, 3, 2, 1, 0, 7]], map_rows, map_cols
    )
    grad_map_in = jnp.swapaxes(cell_mask * (kept + grad_map_in), 1, 2)
    small_conv = jnp.concatenate(
        [
            grad_taps.reshape(56, channels),
            sums_conv[:2],
            grad_scale[None],
        ],
        axis=0,
    )
    out_up, out_down = mlp_rows(later(mlp_turned, grad_map_in), dps)
    out_adapt = gather_bits(later(out_adapt.astype(BF), grad_map_in)).astype(F32)
    vit_out = to_grid(later(vit_every, normed_here))
    grad_vit = to_grid(later(grad_vit_every, grad_taps))
    out_expand = conv_rows(expand_part)
    small_vit, small_conv = later(small_vit, grad_map_in), later(small_conv, grad_map_in)
    small_vit = scatter_small(small_vit, ("dp", "strip"))
    small_conv = scatter_small(small_conv, ("strip", "tensor"))
    conv_share = channels // (2 * zs)
    out_taps = small_conv[:56].reshape(7, 8, conv_share)[:, :7].reshape(49, conv_share).T
    return (
        vit_out,
        map_out,
        grad_vit,
        grad_map_in,
        out_taps,
        small_conv[56],
        small_conv[57],
        out_expand,
        out_reduce,
        small_conv[58],
        out_adapt,
        small_vit[:9].T,
        small_vit[9],
        small_vit[10],
        small_vit[11],
        out_qkv.reshape(-1, 3, head_cols),
        out_proj,
        small_vit[12],
        small_vit[13],
        out_up,
        out_down,
    )


def solution(mesh):
    rows = P("dp", "strip", None, None)
    maps = P("dp", "strip", "tensor", None)
    conv = ("strip", "tensor")
    vit = ("dp", "strip")
    in_specs = (
        P("dp"), rows, maps, P(), P(), P(), P(conv, None), P(conv, None), P(), P(), P(), P(), P(), P(),
        P(None, None, "tensor"), P(None, "tensor"), P(), P(), P(None, "tensor"), P(None, "tensor"), rows, maps,
    )
    out_specs = (
        rows, maps, rows, maps, P(conv, None), P(conv), P(conv), P(conv, None), P(conv, None), P(conv),
        P(vit, None), P(vit, None), P(vit), P(vit), P(vit), P(vit, None, "tensor"), P(vit, "tensor"), P(vit), P(vit),
        P(vit, "tensor"), P(vit, "tensor"),
    )
    return jax.shard_map(shards, mesh=mesh, in_specs=in_specs, out_specs=out_specs, check_vma=False)
```

```python
import functools

import jax
import jax.numpy as jnp
from jax import lax
from jax.experimental import pallas as pl
from jax.experimental.pallas import tpu as pltpu
from jax.sharding import PartitionSpec as P

HD = 64
G = 24
MAXS = 48
EPS = 1e-06
BF = jnp.bfloat16
F32 = jnp.float32
DOWN_ROWS = (((0,), (0,)), ((), ()))
ACROSS = (((1,), (1,)), ((), ()))
VMEM = 48 * 2**20
EDGE = 8
LIGHT = pl.CostEstimate(flops=1, bytes_accessed=1, transcendentals=0)


def core_swap(v):
    return lax.ppermute(v, "strip", [(0, 1), (1, 0)])


def dp_swap(v, bit):
    return lax.ppermute(v, "dp", [(i, i ^ bit) for i in range(lax.axis_size("dp"))])


def shift(v, axis, step):
    count = lax.axis_size(axis)
    pairs = [(i, i + step) for i in range(count) if 0 <= i + step < count]
    return lax.ppermute(v, axis, pairs)


def all_sum(v, axes):
    for axis in axes:
        count, bit = lax.axis_size(axis), 1
        while bit < count:
            v = v + lax.ppermute(v, axis, [(i, i ^ bit) for i in range(count)])
            bit *= 2
    return v


def gather_bits(v, axis="tensor"):
    count, at, bit = lax.axis_size(axis), lax.axis_index(axis), 1
    while bit < count:
        other = lax.ppermute(v, axis, [(i, i ^ bit) for i in range(count)])
        upper = (at // bit) % 2 == 1
        v = jnp.concatenate([jnp.where(upper, other, v), jnp.where(upper, v, other)], axis=1)
        bit *= 2
    return v


def quarters():
    return 4 if lax.axis_size("dp") == 4 else 1


def reduce_dp(near_a, near_b, keep_a, keep_b, arrange):
    near_a, near_b = dp_swap(near_a, 1), dp_swap(near_b, 2)

    def first(*waits):
        a, b = later(near_a, *waits), later(near_b, *waits)
        sent = sum_pairs([keep_a[1], (a, 1)], [keep_b[1], (b, 1)])
        last_a, last_b = dp_swap(sent[0], 2), dp_swap(sent[1], 1)

        def second(*waits):
            got_a, got_b = later(last_a, *waits), later(last_b, *waits)
            return arrange([keep_a[0], (a, 0), (got_a, None)], [keep_b[0], (b, 0), (got_b, None)])

        return sent, second

    return first


def in_order(mine, other, at):
    first = at == 0
    return jnp.stack([jnp.where(first, mine, other), jnp.where(first, other, mine)], axis=0)


def dp_order(pieces):
    at = lax.axis_index("dp")
    bit_x, bit_y = at % 2 == 1, at // 2 == 1
    row_own = [jnp.where(bit_x, pieces[1], pieces[0]), jnp.where(bit_x, pieces[0], pieces[1])]
    row_far = [jnp.where(bit_x, pieces[3], pieces[2]), jnp.where(bit_x, pieces[2], pieces[3])]
    return jnp.stack(
        [jnp.where(bit_y, f, o) for o, f in zip(row_own, row_far)]
        + [jnp.where(bit_y, o, f) for o, f in zip(row_own, row_far)],
        axis=0,
    )


def later(v, *others):
    return lax.optimization_barrier((v, *others))[0]


def add(*terms):
    return functools.reduce(lambda a, b: a + b, [t.astype(F32) for t in terms])


def sum_dp(v, before, after):
    count = lax.axis_size("dp")
    v = later(v, before)
    return functools.reduce(lambda a, b: a + b, [v] + [later(dp_swap(v, k), after) for k in range(1, count)])


def at_index(v, i, axis=0):
    return lax.dynamic_index_in_dim(v, i, axis, keepdims=False)


def hidden_share(block, strip_at, part, q):
    width = block.shape[1] // (2 * q)
    return lax.dynamic_slice_in_dim(block, (strip_at * q + part) * width, width, 1)


def gather_conv_weight(block, across):
    q = quarters()
    strip_at = lax.axis_index("strip")
    width = block.shape[1] // (2 * q)
    parts = [(0, width)] if q == 1 else [(lax.axis_index("dp"), width), (lax.axis_index("dp") ^ 3, int(width * across))]
    cut = lambda core: [hidden_share(block, core, part, q)[:, :cols] for part, cols in parts]
    mine = cut(strip_at)
    others = core_swap(jnp.concatenate(cut(1 - strip_at), axis=1))
    ends = [0, width, others.shape[1]]
    both = [in_order(own, others[:, ends[i] : ends[i + 1]], strip_at) for i, own in enumerate(mine)]

    def along_z(i, *waits):
        whole = lax.all_gather(both[i], "tensor", axis=0)
        whole = later(whole, *waits) if waits else whole
        return jnp.swapaxes(whole, 0, 1).reshape(-1, both[i].shape[2])

    return along_z


def dp_across(near, first, *waits):
    half, skip = near[0].shape[0] // 2, first.shape[1]
    near = [later(n, *waits)[:, skip:] for n in near]
    rest = jnp.concatenate([dp_swap(near[0][:half], 2), dp_swap(near[1][half:], 1)], axis=0)
    return jnp.concatenate([first, rest], axis=1)


def dp_neighbours(own):
    return [] if quarters() == 1 else [dp_swap(own, 1), dp_swap(own, 2)]


def conv_terms(left, rights, in_turn):
    if len(rights) == 1:
        return [lax.dot_general(left, rights[0], DOWN_ROWS, preferred_element_type=F32).astype(BF)]
    own, beside_x, beside_y, far = rights
    near = tall(in_turn(left), [beside_x, beside_y, far], [(0, 2), (1, 2)], "tall_near")
    keep = tall(later(left, near[0]), [own, beside_x, beside_y], [(0, 2), (0, 1)], "tall_keep")
    return [*near, *keep]


def conv_dp(terms):
    near_a, near_b, keep_a, keep_b = terms
    return reduce_dp(near_a, near_b, [(keep_a, 0), (keep_a, 1)], [(keep_b, 0), (keep_b, 1)], sum_rows)


def conv_scatter(view):
    _, _, rows, width = view.shape
    return lax.psum_scatter(view.reshape(-1, width), "tensor", scatter_dimension=0, tiled=True).reshape(2, rows, width)


def conv_cores(part):
    strip_at = lax.axis_index("strip")
    mine = at_index(part, strip_at)
    other = core_swap(at_index(part, 1 - strip_at))
    return in_order(mine, other, strip_at)


def conv_rows(both, *waits):
    if quarters() == 1:
        return jnp.concatenate(list(lax.psum(both, "dp")), axis=1).astype(F32)
    near = [dp_swap(both, k) for k in (1, 2, 3)]
    every = dp_order([both] + [later(n, *waits) for n in near])
    return jnp.concatenate([every[d, c] for c in range(2) for d in range(4)], axis=1).astype(F32)


def gather_mlp_weights(up, down, *waits):
    q = quarters()
    strip_at, dp_at = lax.axis_index("strip"), lax.axis_index("dp") if q > 1 else 0
    mine = later(jnp.concatenate([hidden_share(w, strip_at, dp_at, q) for w in (up, down)], axis=0), *waits)
    whole = lax.all_gather(mine, "tensor", axis=0)
    return jnp.concatenate(list(whole), axis=1).reshape(2, up.shape[0], -1)


def mlp_far(near):
    return [dp_swap(near[0][0], 2), dp_swap(near[1][1], 1)] if near else []


def mlp_scatter(terms, dps):
    _, _, width, cols = terms.shape
    if quarters() > 1:
        terms = lax.psum_scatter(terms.reshape(-1, cols), "dp", scatter_dimension=0, tiled=True)
    terms = terms.reshape(2, width, cols)
    view = sum_cols([(terms, 0)], [(terms, 1)])
    cols = view.shape[3]
    part = lax.psum_scatter(view.reshape(-1, cols), "tensor", scatter_dimension=0, tiled=True)
    return view, part.reshape(2, dps * 2, -1, cols)


def mlp_rows(part, dps):
    rows, cols = part.shape[2:]
    if quarters() > 1:
        parts = lax.all_to_all(part, ("dp", "strip"), 0, 0).reshape(dps, 2, 2, rows, cols)
        return [
            jnp.concatenate([parts[d, c, i] for c in range(2) for d in range(dps)], axis=1).astype(F32) for i in range(2)
        ]
    strip_at = lax.axis_index("strip")
    part = lax.psum_scatter(part.reshape(dps, 2, 2, rows, cols), "dp", scatter_dimension=0)
    mine = at_index(part, strip_at)
    other = core_swap(at_index(part, 1 - strip_at))
    both = in_order(mine, other, strip_at)
    return [jnp.concatenate([both[0, i], both[1, i]], axis=1).astype(F32) for i in range(2)]


def rows_layout(whole):
    zs, dps = lax.axis_size("tensor"), lax.axis_size("dp")
    cut = min(w.shape[1] for w in whole) // zs
    return [w.reshape(dps, 2, -1, w.shape[1]) for w in whole], cut


def rows_scatter(whole):
    zs, dps, strip_at = lax.axis_size("tensor"), lax.axis_size("dp"), lax.axis_index("strip")
    view, cut = rows_layout(whole)

    def of_core(core):
        parts = [at_index(v, core, 1) for v in view]
        groups = []
        for z in range(zs):
            group = []
            for v in parts:
                share = v.shape[2] // zs
                group += [v[:, :, z * share + c : z * share + c + cut] for c in range(0, share, cut)]
            groups.append(jnp.concatenate(group, axis=1))
        return jnp.concatenate(groups, axis=0)

    sums = add(of_core(strip_at), core_swap(of_core(1 - strip_at))).astype(BF)

    def over_z(*waits):
        part = lax.psum_scatter(later(sums, *waits).reshape(-1, cut), "tensor", scatter_dimension=0, tiled=True)
        return part.reshape(dps, -1, cut)

    return sums, over_z


def rows_sum(whole, part, *waits):
    zs, dp_at = lax.axis_size("tensor"), lax.axis_index("dp")
    view, cut = rows_layout(whole)
    if quarters() == 1:
        total = lax.psum_scatter(part, "dp", scatter_dimension=0).astype(F32)
    else:
        near = [dp_swap(at_index(part, dp_at ^ k), k) for k in (1, 2, 3)]
        total = add(at_index(part, dp_at), *[later(n, *waits) for n in near])
    outs, at = [], 0
    for v in view:
        rows = v.shape[2]
        count = v.shape[3] // zs // cut
        outs.append(jnp.concatenate([total[at + i * rows : at + (i + 1) * rows] for i in range(count)], axis=1))
        at += count * rows
    return outs


def scatter_steps(v, axis):
    count, bit, at = lax.axis_size(axis), lax.axis_size(axis) // 2, lax.axis_index(axis)
    while bit >= 1:
        half = v.shape[1] // 2
        upper = (at // bit) % 2
        mine = lax.dynamic_slice_in_dim(v, upper * half, half, 1)
        other = lax.dynamic_slice_in_dim(v, (1 - upper) * half, half, 1)
        v = mine + lax.ppermute(other, axis, [(i, i ^ bit) for i in range(count)])
        bit //= 2
    return v


def gather_rows(block):
    width, cols = block.shape[-2:]
    dps, zs = lax.axis_size("dp"), lax.axis_size("tensor")
    rows = width // (2 * dps)
    at = lax.axis_index("dp") * 2 + lax.axis_index("strip")
    mine = lax.dynamic_slice_in_dim(block.reshape(-1, width, cols), at * rows, rows, 1)
    whole = lax.all_gather(mine, ("tensor", "dp", "strip"), axis=0).reshape(zs, 2 * dps, -1, rows, cols)
    return jnp.concatenate([whole[:, :, a].reshape(zs, width, cols) for a in range(whole.shape[2])], axis=2)


def params(limit=VMEM):
    return pltpu.CompilerParams(vmem_limit_bytes=limit)


def add_kernel(counts, *refs):
    outs = refs[sum(counts) :]
    at = 0
    for i, count in enumerate(counts):
        total = add(*[r[0] if len(r.shape) == 3 else r[...] for r in refs[at : at + count]]).astype(BF)
        if len(outs) == 1:
            outs[0][0, i] = total
        else:
            outs[i][...] = total
        at += count


def sum_call(groups, grid, block, place, out_specs, out_shape, name):
    specs = []
    for array, lead in [term for group in groups for term in group]:
        if lead is None:
            specs.append(pl.BlockSpec(block, place))
        else:
            specs.append(pl.BlockSpec((1, *block), lambda i, lead=lead: (lead, *place(i))))
    return pl.pallas_call(
        functools.partial(add_kernel, [len(g) for g in groups]),
        grid=(grid,),
        in_specs=specs,
        out_specs=out_specs,
        out_shape=out_shape,
        compiler_params=params(20 * 2**20),
        cost_estimate=LIGHT,
        name=name,
    )(*[array for group in groups for array, _ in group])


def sum_pairs(*groups):
    rows, cols = groups[0][0][0].shape[-2:]
    block, place = (256, cols), lambda i: (i, 0)
    return sum_call(
        groups,
        rows // 256,
        block,
        place,
        [pl.BlockSpec(block, place)] * len(groups),
        [jax.ShapeDtypeStruct((rows, cols), BF)] * len(groups),
        "sum_pairs",
    )


def sum_rows(*groups):
    zs = lax.axis_size("tensor")
    rows, cols = groups[0][0][0].shape[-2:]
    rows = rows // zs
    return sum_call(
        groups,
        zs,
        (rows, cols),
        lambda i: (i, 0),
        pl.BlockSpec((1, 2, rows, cols), lambda i: (i, 0, 0, 0)),
        jax.ShapeDtypeStruct((zs, 2, rows, cols), BF),
        "sum_rows",
    )


def sum_cols(*groups):
    zs = lax.axis_size("tensor")
    rows, cols = groups[0][0][0].shape[-2:]
    cols = cols // zs
    return sum_call(
        groups,
        zs,
        (rows, cols),
        lambda i: (0, i),
        pl.BlockSpec((1, 2, rows, cols), lambda i: (i, 0, 0, 0)),
        jax.ShapeDtypeStruct((zs, 2, rows, cols), BF),
        "sum_cols",
    )


def conv7_kernel(rows, cols, back, x_ref, k_ref, out_ref, wide):
    wide[...] = x_ref[0].astype(F32)

    def tap_row(i, sums):
        sums = list(sums)
        taps = k_ref[6 - i if back else i]
        for m in range(cols + 6):
            x = wide[m, pl.ds(i + EDGE - 3, rows), :]
            for j in range(7):
                c = m - j
                if 0 <= c < cols:
                    tap = 6 - j if back else j
                    sums[c] = sums[c] + x * taps[tap : tap + 1]
        return tuple(sums)

    sums = lax.fori_loop(0, 7, tap_row, tuple(jnp.zeros((rows, 128), F32) for _ in range(cols)))
    for c in range(cols):
        out_ref[0, c] = sums[c]


def conv7(padded, taps, rows, cols, back=False):
    items, _, _, channels = padded.shape
    return pl.pallas_call(
        functools.partial(conv7_kernel, rows, cols, back),
        grid=(items, channels // 128),
        in_specs=[
            pl.BlockSpec((1, cols + 6, rows + 2 * EDGE, 128), lambda b, c: (b, 0, 0, c)),
            pl.BlockSpec((7, 8, 128), lambda b, c: (0, 0, c)),
        ],
        out_specs=pl.BlockSpec((1, cols, rows, 128), lambda b, c: (b, 0, 0, c)),
        out_shape=jax.ShapeDtypeStruct((items, cols, rows, channels), F32),
        scratch_shapes=[pltpu.VMEM((cols + 6, rows + 2 * EDGE, 128), F32)],
        compiler_params=params(8 * 2**20),
        cost_estimate=LIGHT,
        name="depthwise",
    )(padded, taps)


def tap_grad_kernel(rows, cols, x_ref, g_ref, out_ref, wide, full):
    wide[...] = x_ref[0].astype(F32)
    full[...] = g_ref[0].astype(F32)

    @pl.when(pl.program_id(1) == 0)
    def _():
        out_ref[...] = jnp.zeros_like(out_ref)

    def tap_row(i, _):
        sums = [jnp.zeros((8, 128), F32) for _ in range(7)]
        grads = [full[c] for c in range(cols)]
        for m in range(cols + 6):
            x = wide[m, pl.ds(i + EDGE - 3, rows), :]
            for j in range(7):
                c = m - j
                if 0 <= c < cols:
                    sums[j] = sums[j] + (x * grads[c]).reshape(rows // 8, 8, 128).sum(axis=0)
        lines = [jnp.sum(s, axis=0, keepdims=True) for s in sums]
        out_ref[i] += jnp.concatenate(lines + [jnp.zeros((1, 128), F32)], axis=0)
        return 0

    lax.fori_loop(0, 7, tap_row, 0)


def tap_grad(padded, grad, rows, cols):
    items, _, _, channels = padded.shape
    return pl.pallas_call(
        functools.partial(tap_grad_kernel, rows, cols),
        grid=(channels // 128, items),
        in_specs=[
            pl.BlockSpec((1, cols + 6, rows + 2 * EDGE, 128), lambda c, b: (b, 0, 0, c)),
            pl.BlockSpec((1, cols, rows, 128), lambda c, b: (b, 0, 0, c)),
        ],
        out_specs=pl.BlockSpec((7, 8, 128), lambda c, b: (0, 0, c)),
        out_shape=jax.ShapeDtypeStruct((7, 8, channels), F32),
        scratch_shapes=[pltpu.VMEM((cols + 6, rows + 2 * EDGE, 128), F32), pltpu.VMEM((cols, rows, 128), F32)],
        compiler_params=params(8 * 2**20),
        cost_estimate=LIGHT,
        name="tap_grad",
    )(padded, grad)


def norm_kernel(v_ref, gain_ref, bias_ref, out_ref):
    unit, _ = normalise(v_ref[...])
    out_ref[...] = (unit * gain_ref[...] + bias_ref[...]).astype(BF)


def norm_rows(v, gain, bias):
    rows, width = v.shape
    block = row_block(rows, 144)
    tile, line = pl.BlockSpec((block, width), lambda i: (i, 0)), pl.BlockSpec((1, width), lambda i: (0, 0))
    return pl.pallas_call(
        norm_kernel,
        grid=(rows // block,),
        in_specs=[tile, line, line],
        out_specs=tile,
        out_shape=jax.ShapeDtypeStruct((rows, width), BF),
        compiler_params=params(16 * 2**20),
        cost_estimate=LIGHT,
        name="norm",
    )(v, gain.reshape(1, width), bias.reshape(1, width))


def norm_back_kernel(here_ref, there_ref, v_ref, gain_ref, out_ref, sums_ref):
    @pl.when(pl.program_id(0) == 0)
    def _():
        sums_ref[...] = jnp.zeros_like(sums_ref)

    grad = here_ref[...] + there_ref[...].astype(F32)
    unit, scale = normalise(v_ref[...])
    sums_ref[...] += lines(jnp.sum(grad * unit, axis=0, keepdims=True), jnp.sum(grad, axis=0, keepdims=True))
    out_ref[...] = normalise_back(grad, unit, scale, gain_ref[...]).astype(BF)


def norm_rows_back(here, there, v, gain):
    rows, width = v.shape
    block = row_block(rows, 144)
    tile, line = pl.BlockSpec((block, width), lambda i: (i, 0)), pl.BlockSpec((1, width), lambda i: (0, 0))
    return pl.pallas_call(
        norm_back_kernel,
        grid=(rows // block,),
        in_specs=[tile, tile, tile, line],
        out_specs=[tile, pl.BlockSpec((8, width), lambda i: (0, 0))],
        out_shape=[jax.ShapeDtypeStruct((rows, width), BF), jax.ShapeDtypeStruct((8, width), F32)],
        compiler_params=params(20 * 2**20),
        cost_estimate=LIGHT,
        name="norm_back",
    )(here, there, v, gain.reshape(1, width))


def gelu_pair(h):
    cdf = 0.5 * (1.0 + lax.erf(h * (0.5**0.5)))
    pdf = jnp.exp(h * h * -0.5) * 0.3989422804014327
    return h * cdf, cdf + h * pdf


def expand_kernel(step, x_ref, w_ref, act_ref, slope_ref):
    x = x_ref[...]
    for at in range(0, w_ref.shape[1], step):
        h = jnp.dot(x, w_ref[:, at : at + step], preferred_element_type=F32)
        act, slope = gelu_pair(h)
        act_ref[:, at : at + step] = act.astype(BF)
        slope_ref[:, at : at + step] = slope.astype(BF)


def row_block(rows, most):
    best = 16
    for block in range(16, most + 1, 16):
        if rows % block == 0:
            best = block
    return best


def expand(x, w):
    m, k = x.shape
    n = w.shape[1]
    bm = row_block(m, 432)
    bn = min(n, 768)
    spec = pl.BlockSpec((bm, bn), lambda j, i: (i, j))
    return pl.pallas_call(
        functools.partial(expand_kernel, 256),
        grid=(n // bn, m // bm),
        in_specs=[pl.BlockSpec((bm, k), lambda j, i: (i, 0)), pl.BlockSpec((k, bn), lambda j, i: (0, j))],
        out_specs=[spec, spec],
        out_shape=[jax.ShapeDtypeStruct((m, n), BF)] * 2,
        compiler_params=params(20 * 2**20),
        cost_estimate=LIGHT,
        name="expand_gelu",
    )(x, w)


def back_sum_kernel(count, *refs):
    out_ref = refs[-1]
    total = None
    for a_ref, w_ref in zip(refs[:count], refs[count : 2 * count]):
        term = lax.dot_general(a_ref[...], w_ref[...], ACROSS, preferred_element_type=F32)
        total = term if total is None else total + term
    out_ref[...] = total.astype(out_ref.dtype)


def back_sum(parts, weights, first, rows, dtype):
    n = weights[0].shape[0]
    ks = [w.shape[1] for w in weights]
    bm = row_block(rows, 432)
    bn = 512
    skip = first // bm
    return pl.pallas_call(
        functools.partial(back_sum_kernel, len(parts)),
        grid=(n // bn, rows // bm),
        in_specs=[pl.BlockSpec((bm, k), lambda j, i: (i + skip, 0)) for k in ks]
        + [pl.BlockSpec((bn, k), lambda j, i: (j, 0)) for k in ks],
        out_specs=pl.BlockSpec((bm, bn), lambda j, i: (i, j)),
        out_shape=jax.ShapeDtypeStruct((rows, n), dtype),
        compiler_params=params(52 * 2**20),
        cost_estimate=LIGHT,
        name="reduce_sum",
    )(*parts, *weights)


def tall(a, rights, uses, name):
    m, n = a.shape
    cols = rights[0].shape[1]
    bm = 256
    steps = n // 2 // bm

    def kernel(a_ref, *refs):
        outs = refs[-2:]
        for half in range(2):

            @pl.when(pl.program_id(0) // steps == half)
            def _():
                left = a_ref[...]
                for i, use in enumerate(uses[half]):
                    outs[half][i] = lax.dot_general(left, refs[use][...], DOWN_ROWS, preferred_element_type=F32).astype(BF)

    def out_spec(half):
        place = lambda i: (0, jnp.clip(i - half * steps, 0, steps - 1), 0)
        return pl.BlockSpec((len(uses[half]), bm, cols), place)

    return pl.pallas_call(
        kernel,
        grid=(2 * steps,),
        in_specs=[pl.BlockSpec((m, bm), lambda i: (0, i))] + [pl.BlockSpec((m, cols), lambda i: (0, 0)) for _ in rights],
        out_specs=[out_spec(0), out_spec(1)],
        out_shape=[jax.ShapeDtypeStruct((len(u), n // 2, cols), BF) for u in uses],
        compiler_params=params(28 * 2**20),
        cost_estimate=LIGHT,
        name=name,
    )(a, *rights)


def back_slope(a, w, slope):
    m, k = a.shape
    n = w.shape[1]
    bm, bn = row_block(m, 432), min(n, 768)

    def kernel(a_ref, w_ref, s_ref, out_ref):
        left = a_ref[...]
        for at in range(0, bn, 256):
            cut = slice(at, at + 256)
            grad = jnp.dot(left, w_ref[:, cut], preferred_element_type=F32)
            out_ref[:, cut] = (grad * s_ref[:, cut].astype(F32)).astype(BF)

    spec = pl.BlockSpec((bm, bn), lambda j, i: (i, j))
    return pl.pallas_call(
        kernel,
        grid=(n // bn, m // bm),
        in_specs=[pl.BlockSpec((bm, k), lambda j, i: (i, 0)), pl.BlockSpec((k, bn), lambda j, i: (0, j)), spec],
        out_specs=spec,
        out_shape=jax.ShapeDtypeStruct((m, n), BF),
        compiler_params=params(20 * 2**20),
        cost_estimate=LIGHT,
        name="back_slope",
    )(a, w, slope)


def whole_call(kernel, outs, args, flops, name):
    vmem = pl.BlockSpec(memory_space=pltpu.VMEM)
    bytes_accessed = sum(a.size * a.dtype.itemsize for a in args) + sum(o.size * o.dtype.itemsize for o in outs)
    return pl.pallas_call(
        kernel,
        in_specs=[vmem] * len(args),
        out_specs=[vmem] * len(outs),
        out_shape=outs,
        compiler_params=params(36 * 2**20),
        cost_estimate=LIGHT,
        name=name,
    )(*args)


def shape(dtype, *dims):
    return jax.ShapeDtypeStruct(dims, dtype)


def qkv_kernel(zs, group, joined_ref, gain_ref, bias_ref, w_ref, normed_ref, out_ref):
    unit, _ = normalise(joined_ref[...])
    normed = (unit * gain_ref[...] + bias_ref[...]).astype(BF)
    normed_ref[...] = normed
    for z in range(zs):
        part = jnp.dot(normed, w_ref[z], preferred_element_type=F32).astype(BF)
        for a in range(3):
            for core in range(2):
                at = (2 * a + core) * group
                out_ref[core * zs + z, :, a * group : (a + 1) * group] = part[:, at : at + group]


def tokens_of(ref):
    v = ref[:, 0].astype(F32)
    return v.reshape(v.shape[0] * v.shape[1], v.shape[2]).astype(BF)


def head_lanes(heads, lanes):
    lane = lax.broadcasted_iota(jnp.int32, (1, lanes), 1)
    return [jnp.logical_and(lane >= h * HD, lane < (h + 1) * HD) for h in range(heads)]


def only(lanes, v):
    return jnp.where(lanes, v, jnp.zeros((), v.dtype))


def head_probs(q, k):
    scores = lax.dot_general(q, k, ACROSS, preferred_element_type=F32) * HD**-0.5
    powers = jnp.exp(scores - jnp.max(scores, axis=-1, keepdims=True))
    return powers * (1.0 / jnp.sum(powers, axis=-1, keepdims=True))


def attention_kernel(group, qkv_ref, out_ref):
    qkv = tokens_of(qkv_ref)
    q, k, v = (qkv[:, a * group : (a + 1) * group] for a in range(3))
    mixed = jnp.zeros(v.shape, F32)
    for lanes in head_lanes(group // HD, group):
        probs = head_probs(only(lanes, q), k).astype(BF)
        mixed = jnp.where(lanes, jnp.dot(probs, v, preferred_element_type=F32), mixed)
    out_ref[:, 0] = mixed.reshape(out_ref.shape[0], out_ref.shape[2], group).astype(BF)


def attention_back_kernel(group, qkv_ref, grad_ref, out_ref):
    qkv = tokens_of(qkv_ref)
    grad = tokens_of(grad_ref)
    q, k, v = (qkv[:, a * group : (a + 1) * group] for a in range(3))
    sums = [jnp.zeros(v.shape, F32) for _ in range(3)]
    for lanes in head_lanes(group // HD, group):
        probs = head_probs(only(lanes, q), k)
        grad_h = only(lanes, grad)
        grad_probs = lax.dot_general(grad_h, v, ACROSS, preferred_element_type=F32)
        along = jnp.sum(probs * grad_probs, axis=-1, keepdims=True)
        grad_scores = (probs * (grad_probs - along)).astype(BF)
        terms = (
            jnp.dot(grad_scores, k, preferred_element_type=F32) * HD**-0.5,
            lax.dot_general(grad_scores, q, DOWN_ROWS, preferred_element_type=F32) * HD**-0.5,
            lax.dot_general(probs.astype(BF), grad, DOWN_ROWS, preferred_element_type=F32),
        )
        sums = [jnp.where(lanes, term, total) for term, total in zip(terms, sums)]
    for a, total in enumerate(sums):
        part = total.reshape(out_ref.shape[0], out_ref.shape[2], group).astype(BF)
        out_ref[:, 0, :, a * group : (a + 1) * group] = part


def by_item(kernel, arrays, lanes, flops, name):
    sources, items, tokens, _ = arrays[0].shape
    block = lambda n: pl.BlockSpec((sources, 1, tokens, n), lambda b: (0, b, 0, 0))
    return pl.pallas_call(
        kernel,
        grid=(items,),
        in_specs=[block(v.shape[3]) for v in arrays],
        out_specs=block(lanes),
        out_shape=shape(BF, sources, items, tokens, lanes),
        compiler_params=params(28 * 2**20),
        cost_estimate=LIGHT,
        name=name,
    )(*arrays)


def project_kernel(zs, group, heads_ref, w_ref, joined_ref, gain_ref, bias_ref, mixed_ref, after_ref, normed_ref):
    total = joined_ref[...]
    for z in range(zs):
        mixed = jnp.concatenate([heads_ref[z], heads_ref[zs + z]], axis=1)
        mixed_ref[:, z * 2 * group : (z + 1) * 2 * group] = mixed
        total = total + lax.dot_general(mixed, w_ref[z], ACROSS, preferred_element_type=F32)
    after_ref[...] = total
    unit, _ = normalise(total)
    normed_ref[...] = (unit * gain_ref[...] + bias_ref[...]).astype(BF)


def pair_kernel(after_ref, here_ref, there_ref, grad_ref, out_ref):
    out_ref[0] = (after_ref[...] + here_ref[...] + there_ref[...].astype(F32)).astype(BF)
    out_ref[1] = grad_ref[...].astype(BF)


def mlp_kernel(count, x_ref, g_ref, *refs):
    given = 1 if count == 1 else count + 1
    weights = [(r.at[0], r.at[1]) for r in refs[: count - 1 or 1]]
    if count > 1:
        weights.append((refs[count - 1], refs[count]))
    out_ref, back_ref = refs[given : given + 2]
    acts, grads = refs[given + 2 : given + 2 + count], refs[given + 2 + count :]
    x, g = x_ref[...], g_ref[...]
    for p, (up, down) in enumerate(weights):
        act, slope = gelu_pair(jnp.dot(x, up[...], preferred_element_type=F32))
        act = act.astype(BF)
        acts[p][...] = act
        grad = (jnp.dot(g, down[...], preferred_element_type=F32) * slope).astype(BF)
        grads[p][...] = grad
        out = lax.dot_general(act, down[...], ACROSS, preferred_element_type=F32)
        back = lax.dot_general(grad, up[...], ACROSS, preferred_element_type=F32)
        if p == 0:
            out_ref[...] = out
            back_ref[...] = back
        else:
            out_ref[...] += out
            back_ref[...] += back


def mlp_terms(two, grad_out, actives, grads, dp_at):
    count = len(actives)
    cells, width = two.shape
    cols = actives[0].shape[1]

    def kernel(at_ref, two_ref, out_ref, *refs):
        acts, ups, terms = refs[:count], refs[count : 2 * count], refs[-1]
        for k in range(count):

            @pl.when(pl.program_id(0) == k)
            def _():
                terms[0, 0] = lax.dot_general(two_ref[...], ups[k][...], DOWN_ROWS, preferred_element_type=F32).astype(BF)
                terms[0, 1] = lax.dot_general(out_ref[...], acts[k][...], DOWN_ROWS, preferred_element_type=F32).astype(BF)

    whole = lambda v: pl.BlockSpec(v.shape, lambda k, at: (0, 0))
    arrays = [two, grad_out, *actives, *grads]
    return pl.pallas_call(
        kernel,
        grid_spec=pltpu.PrefetchScalarGridSpec(
            num_scalar_prefetch=1,
            grid=(count,),
            in_specs=[whole(v) for v in arrays],
            out_specs=pl.BlockSpec((1, 2, width, cols), lambda k, at: (k ^ at[0], 0, 0, 0)),
        ),
        out_shape=jax.ShapeDtypeStruct((count, 2, width, cols), BF),
        compiler_params=params(32 * 2**20),
        cost_estimate=LIGHT,
        name="mlp_terms",
    )(dp_at.astype(jnp.int32).reshape(1) if count > 1 else jnp.zeros((1,), jnp.int32), *arrays)


def lines(*rows):
    width = rows[0].shape[1]
    return jnp.concatenate(list(rows) + [jnp.zeros((8 - len(rows), width), F32)], axis=0)


def norm_back_two_kernel(zs, group, here_ref, there_ref, after_ref, d_ref, gain_ref, w_ref, grad_ref, low_ref, sums_ref, out_ref):
    grad_two = here_ref[...] + there_ref[...].astype(F32)
    unit, scale = normalise(after_ref[...])
    sums_ref[...] = lines(jnp.sum(grad_two * unit, axis=0, keepdims=True), jnp.sum(grad_two, axis=0, keepdims=True))
    grad = d_ref[...] + normalise_back(grad_two, unit, scale, gain_ref[...])
    grad_ref[...] = grad
    low = grad.astype(BF)
    low_ref[...] = low
    for z in range(zs):
        part = jnp.dot(low, w_ref[z], preferred_element_type=F32).astype(BF)
        for core in range(2):
            out_ref[core * zs + z] = part[:, core * group : (core + 1) * group]


def norm_back_one_kernel(zs, group, g_ref, w_ref, joined_ref, after_ref, gain_ref, all_ref, grad_ref, sums_ref):
    grad_one = jnp.zeros(joined_ref.shape, F32)
    for z in range(zs):
        part = jnp.concatenate(
            [g_ref[core * zs + z, :, a * group : (a + 1) * group] for a in range(3) for core in range(2)], axis=1
        )
        all_ref[:, z * 6 * group : (z + 1) * 6 * group] = part
        grad_one = grad_one + lax.dot_general(part, w_ref[z], ACROSS, preferred_element_type=F32)
    unit, scale = normalise(joined_ref[...])
    sums_ref[...] = lines(jnp.sum(grad_one * unit, axis=0, keepdims=True), jnp.sum(grad_one, axis=0, keepdims=True))
    grad_ref[...] = after_ref[...] + normalise_back(grad_one, unit, scale, gain_ref[...])


def normalise(v):
    center = jnp.mean(v, axis=-1, keepdims=True)
    shifted = v - center
    scale = lax.rsqrt(jnp.mean(shifted * shifted, axis=-1, keepdims=True) + EPS)
    return shifted * scale, scale


def normalise_back(g, unit, scale, gain):
    gg = g * gain
    along = jnp.mean(gg * unit, axis=-1, keepdims=True)
    return scale * (gg - jnp.mean(gg, axis=-1, keepdims=True) - unit * along)


def pool_matrix(pooled_index, buffer_index, map_side, offset):
    map_place = buffer_index[None, :] - offset
    bin_start = pooled_index[:, None] * map_side // G
    bin_stop = ((pooled_index[:, None] + 1) * map_side + G - 1) // G
    inside = jnp.logical_and(map_place >= bin_start, map_place < bin_stop)
    real = jnp.logical_and(pooled_index >= 0, pooled_index < G)[:, None]
    return jnp.where(jnp.logical_and(inside, real), 1.0, 0.0).astype(F32) / (bin_stop - bin_start).astype(F32)


def depthwise3(padded, kernel, rows, cols):
    total = None
    for i in range(3):
        for j in range(3):
            term = padded[:, i : i + rows, j : j + cols, :] * kernel[:, 3 * i + j]
            total = term if total is None else total + term
    return total


def rim(v):
    v = jnp.concatenate([shift(v[:, -1:], "strip", 1), v, shift(v[:, :1], "strip", -1)], axis=1)
    return jnp.concatenate([shift(v[:, :, -1:], "tensor", 1), v, shift(v[:, :, :1], "tensor", -1)], axis=2)


def wide_rim(v):
    return rows_rim(jnp.concatenate([shift(v[:, -3:], "tensor", 1), v, shift(v[:, :3], "tensor", -1)], axis=1))


def rows_rim(v):
    return jnp.concatenate([shift(v[:, :, -EDGE:], "strip", 1), v, shift(v[:, :, :EDGE], "strip", -1)], axis=2)


def shards(
    res_code, vit_in, map_in, dw_kernel, conv_gain, conv_bias, w_expand, w_reduce, layer_scale, adapt_w, mix_kernel,
    gate_logit, gain_one, bias_one, w_qkv, w_proj, gain_two, bias_two, w_up, w_down, d_vit, d_map,
):
    strip_at, tensor_at, dp_at = (lax.axis_index(a) for a in ("strip", "tensor", "dp"))
    dps, zs = lax.axis_size("dp"), lax.axis_size("tensor")
    items, grid_rows, _, width = vit_in.shape
    _, map_rows, map_cols, channels = map_in.shape
    grid_cols = G // zs
    cells = items * map_rows * map_cols
    tokens = items * grid_rows * grid_cols
    head_cols = w_qkv.shape[2]
    score_scale = HD**-0.5

    expand_z, reduce_z = gather_conv_weight(w_expand, 1), gather_conv_weight(w_reduce, 0.5)
    expand_own, reduce_own = expand_z(0), reduce_z(0)
    expand_near = dp_neighbours(expand_own)
    qkv_whole = gather_rows(jnp.swapaxes(w_qkv, 0, 1))
    proj_whole = gather_rows(w_proj)
    count = quarters()

    side = res_code // 32
    offset = (MAXS - side) // 2
    row_cells = strip_at * map_rows + jnp.arange(map_rows, dtype=jnp.int32)
    col_cells = tensor_at * map_cols + jnp.arange(map_cols, dtype=jnp.int32)

    def inside(at):
        low, high = offset[:, None], (offset + side)[:, None]
        return jnp.logical_and(at[None] >= low, at[None] < high).astype(F32)

    row_ok, col_ok = inside(row_cells), inside(col_cells)
    cell_mask = col_ok[:, :, None, None] * row_ok[:, None, :, None]
    many_pools = jax.vmap(pool_matrix, in_axes=(None, None, 0, 0))
    pooled_rows = strip_at * grid_rows + jnp.arange(grid_rows, dtype=jnp.int32)
    pooled_cols = (tensor_at - 1) * grid_cols + jnp.arange(3 * grid_cols, dtype=jnp.int32)
    row_pool = many_pools(pooled_rows, row_cells, side, offset)
    col_pool = many_pools(pooled_cols, col_cells, side, offset).reshape(items, 3, grid_cols, map_cols)
    pool = jnp.einsum("bir,bgjc->bgijcr", row_pool, col_pool)
    pool = pool.reshape(items, 3 * grid_rows * grid_cols, map_cols * map_rows).astype(BF)

    masked = jnp.swapaxes(map_in, 1, 2) * cell_mask.astype(BF)
    taps = jnp.pad(dw_kernel.T.reshape(7, 7, channels), ((0, 0), (0, 1), (0, 0)))
    padded = later(wide_rim(masked), expand_own)
    spread = conv7(padded, taps, map_rows, map_cols).reshape(cells, channels)
    reduce_near = dp_neighbours(later(reduce_own, spread))
    normed = norm_rows(spread, conv_gain, conv_bias)
    if expand_near:
        normed = later(normed, *expand_near)
    normed_both = jnp.concatenate([normed, core_swap(normed)], axis=0)
    expand_pieces, reduce_pieces, pairs = [expand_own, *expand_near], [reduce_own, *reduce_near], []
    x = normed_both
    for k in range(count):
        if k == 3:
            expand_pieces.append(expand_z(1, pairs[2][0]))
        pairs.append(expand(x, expand_pieces[k]))
        x = later(normed_both, pairs[k][0])
    acts, slopes = zip(*pairs)
    if count > 1:
        reduce_pieces.append(dp_across(reduce_near, reduce_z(1, acts[2]), acts[2]))
    branch_sent = back_sum(acts, reduce_pieces, cells, cells, BF)
    branch_there = core_swap(branch_sent)
    branch_here = back_sum(acts, reduce_pieces, 0, cells, F32)
    branch = (branch_here + branch_there.astype(F32)).reshape(masked.shape)
    map_value = cell_mask * (masked.astype(F32) + layer_scale * branch)
    map_low = map_value.astype(BF)
    map_out = jnp.swapaxes(map_low, 1, 2)

    pooled3 = lax.dot_general(
        pool, map_low.reshape(items, -1, channels), (((2,), (1,)), ((0,), (0,))), preferred_element_type=F32
    ).reshape(items, 3, -1, channels)
    pooled = (
        pooled3[:, 1]
        + shift(pooled3[:, 0].astype(BF), "tensor", -1).astype(F32)
        + shift(pooled3[:, 2].astype(BF), "tensor", 1).astype(F32)
    )
    pooled_low = pooled.astype(BF).reshape(tokens, channels)
    grid_shape = (items, grid_rows, grid_cols, width)
    adapted = jnp.dot(pooled_low, adapt_w, preferred_element_type=F32).reshape(grid_shape)
    mlp_own = gather_mlp_weights(w_up, w_down, branch)
    adapted_pad = rim(adapted)
    local_mix = depthwise3(adapted_pad, mix_kernel, grid_rows, grid_cols)
    gate = jnp.tanh(gate_logit)
    mine = lambda v: lax.dynamic_slice_in_dim(v, tensor_at * grid_cols, grid_cols, 2)
    grad_out = mine(d_vit).reshape(tokens, width)
    grad_mlp = grad_out.astype(BF)
    grad_mlp_both = jnp.concatenate([grad_mlp, core_swap(grad_mlp)], axis=0)
    joined = (mine(vit_in) + gate * local_mix).reshape(tokens, width)

    group = head_cols // 2
    line = lambda v: v.reshape(1, width)
    dots = lambda m, n, k: 2 * m * n * k
    spread_heads = lambda v: lax.all_to_all(v, ("strip", "tensor"), 0, 0, tiled=True)
    by_source = lambda v: v.reshape(2 * zs, items, -1, v.shape[-1])
    normed_one, qkv = whole_call(
        functools.partial(qkv_kernel, zs, group),
        [shape(BF, tokens, width), shape(BF, 2 * zs, tokens, 3 * group)],
        [joined, line(gain_one), line(bias_one), qkv_whole],
        dots(tokens, width, 3 * zs * head_cols),
        "qkv",
    )
    mlp_near = dp_neighbours(mlp_own)
    qkv = later(by_source(spread_heads(qkv)), mlp_own, *mlp_near)
    mlp_weights = [mlp_own, *mlp_near, *mlp_far(mlp_near)]
    attention_flops = items * 2 * dots(24 * 24, 24 * 24, group)
    heads = by_item(functools.partial(attention_kernel, group), [qkv], group, 2 * attention_flops, "attention")
    heads = later(spread_heads(heads).reshape(2 * zs, tokens, group), *mlp_weights)
    mixed, after_attn, normed_two = whole_call(
        functools.partial(project_kernel, zs, group),
        [shape(BF, tokens, width), shape(F32, tokens, width), shape(BF, tokens, width)],
        [heads, proj_whole, joined, line(gain_two), line(bias_two)],
        dots(tokens, width, width),
        "project",
    )

    two_both = jnp.concatenate([normed_two, core_swap(normed_two)], axis=0)
    some = mlp_own.shape[2]
    mlp, back, *halves = whole_call(
        functools.partial(mlp_kernel, count),
        [shape(F32, 2 * tokens, width)] * 2 + [shape(BF, 2 * tokens, some)] * (2 * count),
        [two_both, grad_mlp_both, *mlp_weights],
        4 * count * dots(2 * tokens, width, some),
        "mlp",
    )
    actives, grad_ups = halves[:count], halves[count:]
    back_there = core_swap(back[tokens:].astype(BF))
    grad_after, grad_att, sums_two, grad_heads = whole_call(
        functools.partial(norm_back_two_kernel, zs, group),
        [shape(F32, tokens, width), shape(BF, tokens, width), shape(F32, 8, width), shape(BF, 2 * zs, tokens, group)],
        [back[:tokens], back_there, after_attn, grad_out, line(gain_two), proj_whole],
        dots(tokens, width, width),
        "norm_back_two",
    )
    down_terms = lambda left, rights: [
        lax.dot_general(left, r, DOWN_ROWS, preferred_element_type=F32).astype(BF) for r in rights
    ]
    four = count > 1
    mlp_grads = mlp_terms(two_both, grad_mlp_both, actives, grad_ups, dp_at)
    grad_heads = by_source(spread_heads(grad_heads))
    mlp_view, mlp_part = mlp_scatter(mlp_grads, dps)
    mlp_there = core_swap(mlp[tokens:].astype(BF))
    to_grid = lambda v: jnp.concatenate(list(v), axis=2).astype(F32)

    grad_qkv = by_item(
        functools.partial(attention_back_kernel, group), [qkv, grad_heads], 3 * group, 5 * attention_flops, "attention_back"
    )
    grad_qkv = later(spread_heads(grad_qkv).reshape(2 * zs, tokens, 3 * group), mlp_grads)
    grad_qkv, grad_joined, sums_one = whole_call(
        functools.partial(norm_back_one_kernel, zs, group),
        [shape(BF, tokens, 3 * width), shape(F32, tokens, width), shape(F32, 8, width)],
        [grad_qkv, qkv_whole, joined, grad_after, line(gain_one)],
        dots(tokens, width, 3 * width),
        "norm_back_one",
    )

    grad_grid = grad_joined.reshape(grid_shape)
    over = (0, 1, 2)
    grad_gate = jnp.sum(grad_grid * local_mix, axis=over) * (1.0 - gate * gate)
    grad_mix = grad_grid * gate
    grad_adapted = depthwise3(rim(grad_mix), mix_kernel[:, ::-1], grid_rows, grid_cols)
    grad_adapted = grad_adapted.astype(BF).reshape(tokens, width)
    grad_taps = [
        jnp.sum(adapted_pad[:, i : i + grid_rows, j : j + grid_cols] * grad_mix, axis=over)
        for i in range(3)
        for j in range(3)
    ]
    grad_adapted = later(grad_adapted, mlp_view)
    grad_pooled = lax.dot_general(grad_adapted, adapt_w, ACROSS, preferred_element_type=F32).astype(BF)
    small_vit = jnp.stack(
        grad_taps
        + [
            grad_gate,
            sums_one[0],
            sums_one[1],
            sums_two[0],
            sums_two[1],
        ],
        axis=0,
    )
    small_vit = scatter_steps(scatter_steps(later(small_vit, grad_pooled), "dp"), "strip")
    row_terms = (
        down_terms(later(normed_one, grad_pooled), [grad_qkv])
        + down_terms(later(grad_att, grad_pooled), [mixed])
        + down_terms(later(pooled_low, grad_pooled), [grad_adapted])
    )
    grad_pooled = grad_pooled.reshape(items, -1, channels)
    rows_sums, rows_over_z = rows_scatter(row_terms)
    grad_pooled = jnp.concatenate(
        [later(shift(grad_pooled, "tensor", 1), *row_terms, small_vit), grad_pooled, shift(grad_pooled, "tensor", -1)], axis=1
    )
    grad_map = lax.dot_general(pool, grad_pooled, (((1,), (1,)), ((0,), (0,))), preferred_element_type=F32)
    grad_map = jnp.swapaxes(d_map, 1, 2).astype(F32) + grad_map.reshape(masked.shape)

    kept = cell_mask * grad_map
    grad_scale = jnp.sum(kept * branch, axis=over)
    grad_branch = (kept * layer_scale).astype(BF).reshape(cells, channels)
    grad_branch_both = jnp.concatenate([grad_branch, core_swap(grad_branch)], axis=0)
    rows_part = rows_over_z(grad_map)
    reduce_terms = conv_terms(grad_branch_both, acts, lambda v: later(v, rows_sums))
    grad_hidden, last = [], [reduce_terms[-1]]
    if four:
        reduce_first = conv_dp(reduce_terms)
    for k in range(count):
        last = [back_slope(later(grad_branch_both, *last), reduce_pieces[k], slopes[k])]
        grad_hidden += last
    (both_low,) = whole_call(
        pair_kernel,
        [shape(BF, 2, tokens, width)],
        [after_attn, mlp[:tokens], later(mlp_there, rows_sums), grad_joined],
        tokens * width,
        "vit_pair",
    )
    both_every = lax.all_gather(both_low.reshape(2, *grid_shape), "tensor", axis=0)
    if four:
        near = tall(later(normed_both, last[0]), grad_hidden[1:], [(0, 2), (1, 2)], "tall_near")
        keep = tall(later(normed_both, near[0]), grad_hidden[:3], [(0, 2), (0, 1)], "tall_keep")
        expand_first = conv_dp([*near, *keep])
        done = keep[0]
    else:
        expand_terms = conv_terms(normed_both, grad_hidden, lambda v: later(v, *last))
        done = expand_terms[0]
    sent = later(grad_hidden[0], done)
    normed_sent = back_sum([sent] + grad_hidden[1:], expand_pieces, cells, cells, BF)
    last = [normed_sent, rows_part]
    if four:
        reduce_sent, reduce_second = reduce_first(normed_sent)
        last += [*reduce_sent]
    else:
        reduce_view, expand_view = (
            jnp.swapaxes(t[0].reshape(2, zs, -1, t[0].shape[1]), 0, 1) for t in (reduce_terms, expand_terms)
        )
    normed_there = core_swap(normed_sent)
    kept_here = later(grad_hidden[0], *last)
    normed_here = back_sum([kept_here] + grad_hidden[1:], expand_pieces, 0, cells, F32)
    last = [normed_here]
    if four:
        expand_sent, expand_second = expand_first(normed_here)
        last += [*expand_sent]
    grad_spread, sums_conv = norm_rows_back(later(normed_here, *last), normed_there, spread, conv_gain)
    grad_spread = grad_spread.reshape(masked.shape)
    beside = shift(grad_spread[:, -3:], "tensor", 1), shift(grad_spread[:, :3], "tensor", -1)
    last = [both_every]
    if four:
        reduce_view = reduce_second(grad_spread)
        last += [reduce_view]
    reduce_part = conv_scatter(reduce_view)
    grad_taps = tap_grad(padded, later(grad_spread, *last), map_rows, map_cols)
    small_conv = jnp.concatenate([grad_taps.reshape(56, channels), sums_conv[:2], grad_scale[None]], axis=0)
    rim_spread = jnp.concatenate([later(beside[0], grad_taps), grad_spread, later(beside[1], grad_taps)], axis=1)
    if four:
        expand_view = expand_second(rim_spread)
    expand_part = conv_scatter(expand_view)
    reduce_both = conv_cores(later(reduce_part, rim_spread))
    small_conv = scatter_steps(later(small_conv, rim_spread), "strip")
    grad_map_in = conv7(
        later(rows_rim(rim_spread), expand_view, reduce_both, small_conv),
        taps,
        map_rows,
        map_cols,
        True,
    )
    out_reduce = conv_rows(reduce_both, grad_map_in)
    small_conv = sum_dp(small_conv, reduce_both, grad_map_in)
    out_up, out_down = mlp_rows(jnp.swapaxes(later(mlp_part, grad_map_in), 0, 1), dps)
    out_qkv, out_proj, out_adapt = rows_sum(row_terms, rows_part, grad_map_in)
    grad_map_in = jnp.swapaxes(cell_mask * (kept + later(grad_map_in, out_up)), 1, 2)
    expand_both = conv_cores(later(expand_part, grad_map_in))
    out_expand = conv_rows(expand_both)
    both_every = later(both_every, expand_both)
    vit_out, grad_vit = to_grid(both_every[:, 0]), to_grid(both_every[:, 1])
    out_adapt = gather_bits(later(out_adapt.astype(BF), expand_both)).astype(F32)
    small_conv = scatter_steps(later(small_conv, expand_both), "tensor")
    small_vit = all_sum(later(small_vit, expand_both), ("tensor",))
    conv_share = channels // (2 * zs)
    out_taps = small_conv[:56].reshape(7, 8, conv_share)[:, :7].reshape(49, conv_share).T
    return (
        vit_out,
        map_out,
        grad_vit,
        grad_map_in,
        out_taps,
        small_conv[56],
        small_conv[57],
        out_expand,
        out_reduce,
        small_conv[58],
        out_adapt,
        small_vit[:9].T,
        small_vit[9],
        small_vit[10],
        small_vit[11],
        out_qkv.reshape(-1, 3, head_cols),
        out_proj,
        small_vit[12],
        small_vit[13],
        out_up,
        out_down,
    )


def solution(mesh):
    rows = P("dp", "strip", None, None)
    maps = P("dp", "strip", "tensor", None)
    conv = ("strip", "tensor")
    vit = ("dp", "strip")
    in_specs = (
        P("dp"), rows, maps, P(), P(), P(), P(conv, None), P(conv, None), P(), P(), P(), P(), P(), P(),
        P(None, None, "tensor"), P(None, "tensor"), P(), P(), P(None, "tensor"), P(None, "tensor"), rows, maps,
    )
    out_specs = (
        rows, maps, rows, maps, P(conv, None), P(conv), P(conv), P(conv, None), P(conv, None), P(conv),
        P(vit, None), P(vit, None), P(vit), P(vit), P(vit), P(vit, None, "tensor"), P(vit, "tensor"), P(vit), P(vit),
        P(vit, "tensor"), P(vit, "tensor"),
    )
    return jax.shard_map(shards, mesh=mesh, in_specs=in_specs, out_specs=out_specs, check_vma=False)
```

```python
import functools

import jax
import jax.numpy as jnp
from jax import lax
from jax.experimental import pallas as pl
from jax.experimental.pallas import tpu as pltpu
from jax.sharding import PartitionSpec as P

HD = 64
G = 24
MAXS = 48
EPS = 1e-06
BF = jnp.bfloat16
F32 = jnp.float32
DOWN_ROWS = (((0,), (0,)), ((), ()))
ACROSS = (((1,), (1,)), ((), ()))
VMEM = 48 * 2**20
EDGE = 8
LIGHT = pl.CostEstimate(flops=1, bytes_accessed=1, transcendentals=0)


def core_swap(v):
    return lax.ppermute(v, "strip", [(0, 1), (1, 0)])


def dp_swap(v, bit):
    return lax.ppermute(v, "dp", [(i, i ^ bit) for i in range(lax.axis_size("dp"))])


def shift(v, axis, step):
    count = lax.axis_size(axis)
    pairs = [(i, i + step) for i in range(count) if 0 <= i + step < count]
    return lax.ppermute(v, axis, pairs)


def all_sum(v, axes):
    for axis in axes:
        count, bit = lax.axis_size(axis), 1
        while bit < count:
            v = v + lax.ppermute(v, axis, [(i, i ^ bit) for i in range(count)])
            bit *= 2
    return v


def gather_bits(v, axis="tensor"):
    count, at, bit = lax.axis_size(axis), lax.axis_index(axis), 1
    while bit < count:
        other = lax.ppermute(v, axis, [(i, i ^ bit) for i in range(count)])
        upper = (at // bit) % 2 == 1
        v = jnp.concatenate([jnp.where(upper, other, v), jnp.where(upper, v, other)], axis=1)
        bit *= 2
    return v


def quarters():
    return 4 if lax.axis_size("dp") == 4 else 1


def reduce_dp(near_a, near_b, keep_a, keep_b, arrange):
    near_a, near_b = dp_swap(near_a, 1), dp_swap(near_b, 2)

    def first(*waits):
        a, b = later(near_a, *waits), later(near_b, *waits)
        sent = sum_pairs([keep_a[1], (a, 1)], [keep_b[1], (b, 1)])
        last_a, last_b = dp_swap(sent[0], 2), dp_swap(sent[1], 1)

        def second(*waits):
            got_a, got_b = later(last_a, *waits), later(last_b, *waits)
            return arrange([keep_a[0], (a, 0), (got_a, None)], [keep_b[0], (b, 0), (got_b, None)])

        return sent, second

    return first


def in_order(mine, other, at):
    first = at == 0
    return jnp.stack([jnp.where(first, mine, other), jnp.where(first, other, mine)], axis=0)


def dp_order(pieces):
    at = lax.axis_index("dp")
    bit_x, bit_y = at % 2 == 1, at // 2 == 1
    row_own = [jnp.where(bit_x, pieces[1], pieces[0]), jnp.where(bit_x, pieces[0], pieces[1])]
    row_far = [jnp.where(bit_x, pieces[3], pieces[2]), jnp.where(bit_x, pieces[2], pieces[3])]
    return jnp.stack(
        [jnp.where(bit_y, f, o) for o, f in zip(row_own, row_far)]
        + [jnp.where(bit_y, o, f) for o, f in zip(row_own, row_far)],
        axis=0,
    )


def later(v, *others):
    return lax.optimization_barrier((v, *others))[0]


def add(*terms):
    return functools.reduce(lambda a, b: a + b, [t.astype(F32) for t in terms])


def sum_dp(v, before, after):
    count = lax.axis_size("dp")
    v = later(v, before)
    return functools.reduce(lambda a, b: a + b, [v] + [later(dp_swap(v, k), after) for k in range(1, count)])


def at_index(v, i, axis=0):
    return lax.dynamic_index_in_dim(v, i, axis, keepdims=False)


def hidden_share(block, strip_at, part, q):
    width = block.shape[1] // (2 * q)
    return lax.dynamic_slice_in_dim(block, (strip_at * q + part) * width, width, 1)


def gather_conv_weight(block, across):
    q = quarters()
    strip_at = lax.axis_index("strip")
    width = block.shape[1] // (2 * q)
    parts = [(0, width)] if q == 1 else [(lax.axis_index("dp"), width), (lax.axis_index("dp") ^ 3, int(width * across))]
    cut = lambda core: [hidden_share(block, core, part, q)[:, :cols] for part, cols in parts]
    mine = cut(strip_at)
    others = core_swap(jnp.concatenate(cut(1 - strip_at), axis=1))
    ends = [0, width, others.shape[1]]
    both = [in_order(own, others[:, ends[i] : ends[i + 1]], strip_at) for i, own in enumerate(mine)]

    def along_z(i, *waits):
        whole = lax.all_gather(both[i], "tensor", axis=0)
        whole = later(whole, *waits) if waits else whole
        return jnp.swapaxes(whole, 0, 1).reshape(-1, both[i].shape[2])

    return along_z


def dp_across(near, first, *waits):
    half, skip = near[0].shape[0] // 2, first.shape[1]
    near = [later(n, *waits)[:, skip:] for n in near]
    rest = jnp.concatenate([dp_swap(near[0][:half], 2), dp_swap(near[1][half:], 1)], axis=0)
    return jnp.concatenate([first, rest], axis=1)


def dp_neighbours(own):
    return [] if quarters() == 1 else [dp_swap(own, 1), dp_swap(own, 2)]


def conv_terms(left, rights, in_turn):
    if len(rights) == 1:
        return [lax.dot_general(left, rights[0], DOWN_ROWS, preferred_element_type=F32).astype(BF)]
    own, beside_x, beside_y, far = rights
    near = tall(in_turn(left), [beside_x, beside_y, far], [(0, 2), (1, 2)], "tall_near")
    keep = tall(later(left, near[0]), [own, beside_x, beside_y], [(0, 2), (0, 1)], "tall_keep")
    return [*near, *keep]


def conv_dp(terms):
    near_a, near_b, keep_a, keep_b = terms
    return reduce_dp(near_a, near_b, [(keep_a, 0), (keep_a, 1)], [(keep_b, 0), (keep_b, 1)], sum_rows)


def conv_scatter(view):
    _, _, rows, width = view.shape
    return lax.psum_scatter(view.reshape(-1, width), "tensor", scatter_dimension=0, tiled=True).reshape(2, rows, width)


def conv_cores(part):
    strip_at = lax.axis_index("strip")
    mine = at_index(part, strip_at)
    other = core_swap(at_index(part, 1 - strip_at))
    return in_order(mine, other, strip_at)


def conv_rows(both, *waits):
    if quarters() == 1:
        return jnp.concatenate(list(lax.psum(both, "dp")), axis=1).astype(F32)
    near = [dp_swap(both, k) for k in (1, 2, 3)]
    every = dp_order([both] + [later(n, *waits) for n in near])
    return jnp.concatenate([every[d, c] for c in range(2) for d in range(4)], axis=1).astype(F32)


def gather_mlp_weights(up, down):
    q = quarters()
    strip_at, dp_at = lax.axis_index("strip"), lax.axis_index("dp") if q > 1 else 0
    mine = jnp.concatenate([hidden_share(w, strip_at, dp_at, q) for w in (up, down)], axis=0)
    whole = lax.all_gather(mine, "tensor", axis=0)
    return jnp.concatenate(list(whole), axis=1).reshape(2, up.shape[0], -1), whole


def mlp_far(near):
    return [dp_swap(near[0][0], 2), dp_swap(near[1][1], 1)] if near else []


def mlp_scatter(terms, dps):
    _, _, width, cols = terms.shape
    if quarters() > 1:
        terms = lax.psum_scatter(terms.reshape(-1, cols), "dp", scatter_dimension=0, tiled=True)
    terms = terms.reshape(2, width, cols)
    view = sum_cols([(terms, 0)], [(terms, 1)])
    cols = view.shape[3]

    def over_z(*waits):
        part = lax.psum_scatter(later(view, *waits).reshape(-1, cols), "tensor", scatter_dimension=0, tiled=True)
        return part.reshape(2, dps * 2, -1, cols)

    return view, over_z


def mlp_rows(part, dps):
    rows, cols = part.shape[2:]
    if quarters() > 1:
        parts = lax.all_to_all(part, ("dp", "strip"), 0, 0).reshape(dps, 2, 2, rows, cols)
        return [
            jnp.concatenate([parts[d, c, i] for c in range(2) for d in range(dps)], axis=1).astype(F32) for i in range(2)
        ]
    strip_at = lax.axis_index("strip")
    part = lax.psum_scatter(part.reshape(dps, 2, 2, rows, cols), "dp", scatter_dimension=0)
    mine = at_index(part, strip_at)
    other = core_swap(at_index(part, 1 - strip_at))
    both = in_order(mine, other, strip_at)
    return [jnp.concatenate([both[0, i], both[1, i]], axis=1).astype(F32) for i in range(2)]


def rows_layout(whole):
    zs, dps = lax.axis_size("tensor"), lax.axis_size("dp")
    cut = min(w.shape[1] for w in whole) // zs
    return [w.reshape(dps, 2, -1, w.shape[1]) for w in whole], cut


def rows_scatter(whole):
    zs, dps, strip_at = lax.axis_size("tensor"), lax.axis_size("dp"), lax.axis_index("strip")
    view, cut = rows_layout(whole)

    def of_core(core):
        parts = [at_index(v, core, 1) for v in view]
        groups = []
        for z in range(zs):
            group = []
            for v in parts:
                share = v.shape[2] // zs
                group += [v[:, :, z * share + c : z * share + c + cut] for c in range(0, share, cut)]
            groups.append(jnp.concatenate(group, axis=1))
        return jnp.concatenate(groups, axis=0)

    sums = add(of_core(strip_at), core_swap(of_core(1 - strip_at))).astype(BF)

    def over_z(*waits):
        part = lax.psum_scatter(later(sums, *waits).reshape(-1, cut), "tensor", scatter_dimension=0, tiled=True)
        return part.reshape(dps, -1, cut)

    return sums, over_z


def rows_sum(whole, part, *waits):
    zs, dp_at = lax.axis_size("tensor"), lax.axis_index("dp")
    view, cut = rows_layout(whole)
    if quarters() == 1:
        total = lax.psum_scatter(part, "dp", scatter_dimension=0).astype(F32)
    else:
        near = [dp_swap(at_index(part, dp_at ^ k), k) for k in (1, 2, 3)]
        total = add(at_index(part, dp_at), *[later(n, *waits) for n in near])
    outs, at = [], 0
    for v in view:
        rows = v.shape[2]
        count = v.shape[3] // zs // cut
        outs.append(jnp.concatenate([total[at + i * rows : at + (i + 1) * rows] for i in range(count)], axis=1))
        at += count * rows
    return outs


def scatter_steps(v, axis):
    count, bit, at = lax.axis_size(axis), lax.axis_size(axis) // 2, lax.axis_index(axis)
    while bit >= 1:
        half = v.shape[1] // 2
        upper = (at // bit) % 2
        mine = lax.dynamic_slice_in_dim(v, upper * half, half, 1)
        other = lax.dynamic_slice_in_dim(v, (1 - upper) * half, half, 1)
        v = mine + lax.ppermute(other, axis, [(i, i ^ bit) for i in range(count)])
        bit //= 2
    return v


def gather_rows(block, *waits):
    _, width, cols = block.shape
    dps, zs = lax.axis_size("dp"), lax.axis_size("tensor")
    rows = width // (2 * dps)
    at = lax.axis_index("dp") * 2 + lax.axis_index("strip")
    mine = lax.dynamic_slice_in_dim(block, at * rows, rows, 1)
    if waits:
        mine = later(mine, *waits)
    whole = lax.all_gather(mine, ("tensor", "dp", "strip"), axis=0)
    return whole.reshape(zs, 2 * dps, -1, rows, cols)


def params(limit=VMEM):
    return pltpu.CompilerParams(vmem_limit_bytes=limit)


def add_kernel(counts, *refs):
    outs = refs[sum(counts) :]
    at = 0
    for i, count in enumerate(counts):
        total = add(*[r[0] if len(r.shape) == 3 else r[...] for r in refs[at : at + count]]).astype(BF)
        if len(outs) == 1:
            outs[0][0, i] = total
        else:
            outs[i][...] = total
        at += count


def sum_call(groups, grid, block, place, out_specs, out_shape, name):
    specs = []
    for array, lead in [term for group in groups for term in group]:
        if lead is None:
            specs.append(pl.BlockSpec(block, place))
        else:
            specs.append(pl.BlockSpec((1, *block), lambda i, lead=lead: (lead, *place(i))))
    return pl.pallas_call(
        functools.partial(add_kernel, [len(g) for g in groups]),
        grid=(grid,),
        in_specs=specs,
        out_specs=out_specs,
        out_shape=out_shape,
        compiler_params=params(20 * 2**20),
        cost_estimate=LIGHT,
        name=name,
    )(*[array for group in groups for array, _ in group])


def sum_pairs(*groups):
    rows, cols = groups[0][0][0].shape[-2:]
    block, place = (256, cols), lambda i: (i, 0)
    return sum_call(
        groups,
        rows // 256,
        block,
        place,
        [pl.BlockSpec(block, place)] * len(groups),
        [jax.ShapeDtypeStruct((rows, cols), BF)] * len(groups),
        "sum_pairs",
    )


def sum_rows(*groups):
    zs = lax.axis_size("tensor")
    rows, cols = groups[0][0][0].shape[-2:]
    rows = rows // zs
    return sum_call(
        groups,
        zs,
        (rows, cols),
        lambda i: (i, 0),
        pl.BlockSpec((1, 2, rows, cols), lambda i: (i, 0, 0, 0)),
        jax.ShapeDtypeStruct((zs, 2, rows, cols), BF),
        "sum_rows",
    )


def sum_cols(*groups):
    zs = lax.axis_size("tensor")
    rows, cols = groups[0][0][0].shape[-2:]
    cols = cols // zs
    return sum_call(
        groups,
        zs,
        (rows, cols),
        lambda i: (0, i),
        pl.BlockSpec((1, 2, rows, cols), lambda i: (i, 0, 0, 0)),
        jax.ShapeDtypeStruct((zs, 2, rows, cols), BF),
        "sum_cols",
    )


def conv7_kernel(rows, cols, back, x_ref, k_ref, out_ref, wide):
    wide[...] = x_ref[0].astype(F32)

    def tap_row(i, sums):
        sums = list(sums)
        taps = k_ref[6 - i if back else i]
        for m in range(cols + 6):
            x = wide[m, pl.ds(i + EDGE - 3, rows), :]
            for j in range(7):
                c = m - j
                if 0 <= c < cols:
                    tap = 6 - j if back else j
                    sums[c] = sums[c] + x * taps[tap : tap + 1]
        return tuple(sums)

    sums = lax.fori_loop(0, 7, tap_row, tuple(jnp.zeros((rows, 128), F32) for _ in range(cols)))
    for c in range(cols):
        out_ref[0, c] = sums[c]


def conv7(padded, taps, rows, cols, back=False):
    items, _, _, channels = padded.shape
    return pl.pallas_call(
        functools.partial(conv7_kernel, rows, cols, back),
        grid=(items, channels // 128),
        in_specs=[
            pl.BlockSpec((1, cols + 6, rows + 2 * EDGE, 128), lambda b, c: (b, 0, 0, c)),
            pl.BlockSpec((7, 8, 128), lambda b, c: (0, 0, c)),
        ],
        out_specs=pl.BlockSpec((1, cols, rows, 128), lambda b, c: (b, 0, 0, c)),
        out_shape=jax.ShapeDtypeStruct((items, cols, rows, channels), F32),
        scratch_shapes=[pltpu.VMEM((cols + 6, rows + 2 * EDGE, 128), F32)],
        compiler_params=params(8 * 2**20),
        cost_estimate=LIGHT,
        name="depthwise",
    )(padded, taps)


def tap_grad_kernel(rows, cols, x_ref, g_ref, out_ref, wide, full):
    wide[...] = x_ref[0].astype(F32)
    full[...] = g_ref[0].astype(F32)

    @pl.when(pl.program_id(1) == 0)
    def _():
        out_ref[...] = jnp.zeros_like(out_ref)

    def tap_row(i, _):
        sums = [jnp.zeros((8, 128), F32) for _ in range(7)]
        grads = [full[c] for c in range(cols)]
        for m in range(cols + 6):
            x = wide[m, pl.ds(i + EDGE - 3, rows), :]
            for j in range(7):
                c = m - j
                if 0 <= c < cols:
                    sums[j] = sums[j] + (x * grads[c]).reshape(rows // 8, 8, 128).sum(axis=0)
        lines = [jnp.sum(s, axis=0, keepdims=True) for s in sums]
        out_ref[i] += jnp.concatenate(lines + [jnp.zeros((1, 128), F32)], axis=0)
        return 0

    lax.fori_loop(0, 7, tap_row, 0)


def tap_grad(padded, grad, rows, cols):
    items, _, _, channels = padded.shape
    return pl.pallas_call(
        functools.partial(tap_grad_kernel, rows, cols),
        grid=(channels // 128, items),
        in_specs=[
            pl.BlockSpec((1, cols + 6, rows + 2 * EDGE, 128), lambda c, b: (b, 0, 0, c)),
            pl.BlockSpec((1, cols, rows, 128), lambda c, b: (b, 0, 0, c)),
        ],
        out_specs=pl.BlockSpec((7, 8, 128), lambda c, b: (0, 0, c)),
        out_shape=jax.ShapeDtypeStruct((7, 8, channels), F32),
        scratch_shapes=[pltpu.VMEM((cols + 6, rows + 2 * EDGE, 128), F32), pltpu.VMEM((cols, rows, 128), F32)],
        compiler_params=params(8 * 2**20),
        cost_estimate=LIGHT,
        name="tap_grad",
    )(padded, grad)


def map_kernel(here_ref, there_ref, masked_ref, mask_ref, scale_ref, branch_ref, value_ref):
    branch = here_ref[...] + there_ref[...].astype(F32)
    branch_ref[...] = branch.astype(BF)
    value_ref[...] = (mask_ref[...] * (masked_ref[...].astype(F32) + scale_ref[...] * branch)).astype(BF)


def map_value_rows(here, there, masked, mask, scale):
    rows, width = here.shape
    block = row_block(rows, 144)
    tile, line = pl.BlockSpec((block, width), lambda i: (i, 0)), pl.BlockSpec((1, width), lambda i: (0, 0))
    return pl.pallas_call(
        map_kernel,
        grid=(rows // block,),
        in_specs=[tile, tile, tile, pl.BlockSpec((block, 1), lambda i: (i, 0)), line],
        out_specs=[tile, tile],
        out_shape=[jax.ShapeDtypeStruct((rows, width), BF)] * 2,
        compiler_params=params(20 * 2**20),
        cost_estimate=LIGHT,
        name="map_value",
    )(here, there, masked, mask, scale.reshape(1, width))


def norm_kernel(v_ref, gain_ref, bias_ref, out_ref):
    unit, _ = normalise(v_ref[...])
    out_ref[...] = (unit * gain_ref[...] + bias_ref[...]).astype(BF)


def norm_rows(v, gain, bias):
    rows, width = v.shape
    block = row_block(rows, 144)
    tile, line = pl.BlockSpec((block, width), lambda i: (i, 0)), pl.BlockSpec((1, width), lambda i: (0, 0))
    return pl.pallas_call(
        norm_kernel,
        grid=(rows // block,),
        in_specs=[tile, line, line],
        out_specs=tile,
        out_shape=jax.ShapeDtypeStruct((rows, width), BF),
        compiler_params=params(16 * 2**20),
        cost_estimate=LIGHT,
        name="norm",
    )(v, gain.reshape(1, width), bias.reshape(1, width))


def norm_back_kernel(here_ref, there_ref, v_ref, gain_ref, out_ref, sums_ref):
    @pl.when(pl.program_id(0) == 0)
    def _():
        sums_ref[...] = jnp.zeros_like(sums_ref)

    grad = here_ref[...] + there_ref[...].astype(F32)
    unit, scale = normalise(v_ref[...])
    sums_ref[...] += lines(jnp.sum(grad * unit, axis=0, keepdims=True), jnp.sum(grad, axis=0, keepdims=True))
    out_ref[...] = normalise_back(grad, unit, scale, gain_ref[...]).astype(BF)


def norm_rows_back(here, there, v, gain):
    rows, width = v.shape
    block = row_block(rows, 144)
    tile, line = pl.BlockSpec((block, width), lambda i: (i, 0)), pl.BlockSpec((1, width), lambda i: (0, 0))
    return pl.pallas_call(
        norm_back_kernel,
        grid=(rows // block,),
        in_specs=[tile, tile, tile, line],
        out_specs=[tile, pl.BlockSpec((8, width), lambda i: (0, 0))],
        out_shape=[jax.ShapeDtypeStruct((rows, width), BF), jax.ShapeDtypeStruct((8, width), F32)],
        compiler_params=params(20 * 2**20),
        cost_estimate=LIGHT,
        name="norm_back",
    )(here, there, v, gain.reshape(1, width))


def gelu_pair(h):
    cdf = 0.5 * (1.0 + lax.erf(h * (0.5**0.5)))
    pdf = jnp.exp(h * h * -0.5) * 0.3989422804014327
    return h * cdf, cdf + h * pdf


def expand_kernel(step, x_ref, w_ref, act_ref, slope_ref):
    x = x_ref[...]
    for at in range(0, w_ref.shape[1], step):
        h = jnp.dot(x, w_ref[:, at : at + step], preferred_element_type=F32)
        act, slope = gelu_pair(h)
        act_ref[:, at : at + step] = act.astype(BF)
        slope_ref[:, at : at + step] = slope.astype(BF)


def row_block(rows, most):
    best = 16
    for block in range(16, most + 1, 16):
        if rows % block == 0:
            best = block
    return best


def expand(x, w):
    m, k = x.shape
    n = w.shape[1]
    bm = row_block(m, 432)
    bn = min(n, 768)
    spec = pl.BlockSpec((bm, bn), lambda j, i: (i, j))
    return pl.pallas_call(
        functools.partial(expand_kernel, 256),
        grid=(n // bn, m // bm),
        in_specs=[pl.BlockSpec((bm, k), lambda j, i: (i, 0)), pl.BlockSpec((k, bn), lambda j, i: (0, j))],
        out_specs=[spec, spec],
        out_shape=[jax.ShapeDtypeStruct((m, n), BF)] * 2,
        compiler_params=params(20 * 2**20),
        cost_estimate=LIGHT,
        name="expand_gelu",
    )(x, w)


def back_sum_kernel(count, *refs):
    out_ref = refs[-1]
    total = None
    for a_ref, w_ref in zip(refs[:count], refs[count : 2 * count]):
        term = lax.dot_general(a_ref[...], w_ref[...], ACROSS, preferred_element_type=F32)
        total = term if total is None else total + term
    out_ref[...] = total.astype(out_ref.dtype)


def back_sum(parts, weights, first, rows, dtype):
    n = weights[0].shape[0]
    ks = [w.shape[1] for w in weights]
    bm = row_block(rows, 432)
    bn = 512
    skip = first // bm
    return pl.pallas_call(
        functools.partial(back_sum_kernel, len(parts)),
        grid=(n // bn, rows // bm),
        in_specs=[pl.BlockSpec((bm, k), lambda j, i: (i + skip, 0)) for k in ks]
        + [pl.BlockSpec((bn, k), lambda j, i: (j, 0)) for k in ks],
        out_specs=pl.BlockSpec((bm, bn), lambda j, i: (i, j)),
        out_shape=jax.ShapeDtypeStruct((rows, n), dtype),
        compiler_params=params(52 * 2**20),
        cost_estimate=LIGHT,
        name="reduce_sum",
    )(*parts, *weights)


def tall(a, rights, uses, name):
    m, n = a.shape
    cols = rights[0].shape[1]
    bm = 256
    steps = n // 2 // bm

    def kernel(a_ref, *refs):
        outs = refs[-2:]
        for half in range(2):

            @pl.when(pl.program_id(0) // steps == half)
            def _():
                left = a_ref[...]
                for i, use in enumerate(uses[half]):
                    outs[half][i] = lax.dot_general(left, refs[use][...], DOWN_ROWS, preferred_element_type=F32).astype(BF)

    def out_spec(half):
        place = lambda i: (0, jnp.clip(i - half * steps, 0, steps - 1), 0)
        return pl.BlockSpec((len(uses[half]), bm, cols), place)

    return pl.pallas_call(
        kernel,
        grid=(2 * steps,),
        in_specs=[pl.BlockSpec((m, bm), lambda i: (0, i))] + [pl.BlockSpec((m, cols), lambda i: (0, 0)) for _ in rights],
        out_specs=[out_spec(0), out_spec(1)],
        out_shape=[jax.ShapeDtypeStruct((len(u), n // 2, cols), BF) for u in uses],
        compiler_params=params(28 * 2**20),
        cost_estimate=LIGHT,
        name=name,
    )(a, *rights)


def back_slope(a, w, slope):
    m, k = a.shape
    n = w.shape[1]
    bm, bn = row_block(m, 432), min(n, 768)

    def kernel(a_ref, w_ref, s_ref, out_ref):
        left = a_ref[...]
        for at in range(0, bn, 256):
            cut = slice(at, at + 256)
            grad = jnp.dot(left, w_ref[:, cut], preferred_element_type=F32)
            out_ref[:, cut] = (grad * s_ref[:, cut].astype(F32)).astype(BF)

    spec = pl.BlockSpec((bm, bn), lambda j, i: (i, j))
    return pl.pallas_call(
        kernel,
        grid=(n // bn, m // bm),
        in_specs=[pl.BlockSpec((bm, k), lambda j, i: (i, 0)), pl.BlockSpec((k, bn), lambda j, i: (0, j)), spec],
        out_specs=spec,
        out_shape=jax.ShapeDtypeStruct((m, n), BF),
        compiler_params=params(20 * 2**20),
        cost_estimate=LIGHT,
        name="back_slope",
    )(a, w, slope)


def whole_call(kernel, outs, args, flops, name):
    vmem = pl.BlockSpec(memory_space=pltpu.VMEM)
    bytes_accessed = sum(a.size * a.dtype.itemsize for a in args) + sum(o.size * o.dtype.itemsize for o in outs)
    return pl.pallas_call(
        kernel,
        in_specs=[vmem] * len(args),
        out_specs=[vmem] * len(outs),
        out_shape=outs,
        compiler_params=params(36 * 2**20),
        cost_estimate=LIGHT,
        name=name,
    )(*args)


def shape(dtype, *dims):
    return jax.ShapeDtypeStruct(dims, dtype)


def shares(w_ref, z, a):
    _, count, _, rows, cols = w_ref.shape
    return w_ref[z, :, a].reshape(count * rows, cols)


def qkv_kernel(zs, group, joined_ref, gain_ref, bias_ref, w_ref, normed_ref, out_ref):
    unit, _ = normalise(joined_ref[...])
    normed = (unit * gain_ref[...] + bias_ref[...]).astype(BF)
    normed_ref[...] = normed
    for z in range(zs):
        for a in range(3):
            part = jnp.dot(normed, shares(w_ref, z, a), preferred_element_type=F32).astype(BF)
            for core in range(2):
                out_ref[core * zs + z, :, a * group : (a + 1) * group] = part[:, core * group : (core + 1) * group]


def tokens_of(ref):
    v = ref[:, 0].astype(F32)
    return v.reshape(v.shape[0] * v.shape[1], v.shape[2]).astype(BF)


def head_lanes(heads, lanes):
    lane = lax.broadcasted_iota(jnp.int32, (1, lanes), 1)
    return [jnp.logical_and(lane >= h * HD, lane < (h + 1) * HD) for h in range(heads)]


def only(lanes, v):
    return jnp.where(lanes, v, jnp.zeros((), v.dtype))


def head_probs(q, k):
    scores = lax.dot_general(q, k, ACROSS, preferred_element_type=F32) * HD**-0.5
    powers = jnp.exp(scores - jnp.max(scores, axis=-1, keepdims=True))
    return powers * (1.0 / jnp.sum(powers, axis=-1, keepdims=True))


def attention_kernel(group, qkv_ref, out_ref):
    qkv = tokens_of(qkv_ref)
    q, k, v = (qkv[:, a * group : (a + 1) * group] for a in range(3))
    mixed = jnp.zeros(v.shape, F32)
    for lanes in head_lanes(group // HD, group):
        probs = head_probs(only(lanes, q), k).astype(BF)
        mixed = jnp.where(lanes, jnp.dot(probs, v, preferred_element_type=F32), mixed)
    out_ref[:, 0] = mixed.reshape(out_ref.shape[0], out_ref.shape[2], group).astype(BF)


def attention_back_kernel(group, qkv_ref, grad_ref, out_ref):
    qkv = tokens_of(qkv_ref)
    grad = tokens_of(grad_ref)
    q, k, v = (qkv[:, a * group : (a + 1) * group] for a in range(3))
    sums = [jnp.zeros(v.shape, F32) for _ in range(3)]
    for lanes in head_lanes(group // HD, group):
        probs = head_probs(only(lanes, q), k)
        grad_h = only(lanes, grad)
        grad_probs = lax.dot_general(grad_h, v, ACROSS, preferred_element_type=F32)
        along = jnp.sum(probs * grad_probs, axis=-1, keepdims=True)
        grad_scores = (probs * (grad_probs - along)).astype(BF)
        terms = (
            jnp.dot(grad_scores, k, preferred_element_type=F32) * HD**-0.5,
            lax.dot_general(grad_scores, q, DOWN_ROWS, preferred_element_type=F32) * HD**-0.5,
            lax.dot_general(probs.astype(BF), grad, DOWN_ROWS, preferred_element_type=F32),
        )
        sums = [jnp.where(lanes, term, total) for term, total in zip(terms, sums)]
    for a, total in enumerate(sums):
        part = total.reshape(out_ref.shape[0], out_ref.shape[2], group).astype(BF)
        out_ref[:, 0, :, a * group : (a + 1) * group] = part


def by_item(kernel, arrays, lanes, flops, name):
    sources, items, tokens, _ = arrays[0].shape
    block = lambda n: pl.BlockSpec((sources, 1, tokens, n), lambda b: (0, b, 0, 0))
    return pl.pallas_call(
        kernel,
        grid=(items,),
        in_specs=[block(v.shape[3]) for v in arrays],
        out_specs=block(lanes),
        out_shape=shape(BF, sources, items, tokens, lanes),
        compiler_params=params(28 * 2**20),
        cost_estimate=LIGHT,
        name=name,
    )(*arrays)


def project_kernel(zs, group, heads_ref, w_ref, joined_ref, gain_ref, bias_ref, mixed_ref, after_ref, normed_ref):
    total = joined_ref[...]
    for z in range(zs):
        mixed = jnp.concatenate([heads_ref[z], heads_ref[zs + z]], axis=1)
        mixed_ref[:, z * 2 * group : (z + 1) * 2 * group] = mixed
        total = total + lax.dot_general(mixed, w_ref[z], ACROSS, preferred_element_type=F32)
    after_ref[...] = total
    unit, _ = normalise(total)
    normed_ref[...] = (unit * gain_ref[...] + bias_ref[...]).astype(BF)


def pair_kernel(after_ref, here_ref, there_ref, grad_ref, out_ref):
    out_ref[0] = (after_ref[...] + here_ref[...] + there_ref[...].astype(F32)).astype(BF)
    out_ref[1] = grad_ref[...].astype(BF)


def mlp_kernel(count, x_ref, g_ref, *refs):
    given = 1 if count == 1 else count + 1
    weights = [(r.at[0], r.at[1]) for r in refs[: count - 1 or 1]]
    if count > 1:
        weights.append((refs[count - 1], refs[count]))
    out_ref, back_ref = refs[given : given + 2]
    acts, grads = refs[given + 2 : given + 2 + count], refs[given + 2 + count :]
    x, g = x_ref[...], g_ref[...]
    for p, (up, down) in enumerate(weights):
        act, slope = gelu_pair(jnp.dot(x, up[...], preferred_element_type=F32))
        act = act.astype(BF)
        acts[p][...] = act
        grad = (jnp.dot(g, down[...], preferred_element_type=F32) * slope).astype(BF)
        grads[p][...] = grad
        out = lax.dot_general(act, down[...], ACROSS, preferred_element_type=F32)
        back = lax.dot_general(grad, up[...], ACROSS, preferred_element_type=F32)
        if p == 0:
            out_ref[...] = out
            back_ref[...] = back
        else:
            out_ref[...] += out
            back_ref[...] += back


def mlp_terms(two, grad_out, actives, grads, dp_at):
    count = len(actives)
    cells, width = two.shape
    cols = actives[0].shape[1]

    def kernel(at_ref, two_ref, out_ref, *refs):
        acts, ups, terms = refs[:count], refs[count : 2 * count], refs[-1]
        for k in range(count):

            @pl.when(pl.program_id(0) == k)
            def _():
                terms[0, 0] = lax.dot_general(two_ref[...], ups[k][...], DOWN_ROWS, preferred_element_type=F32).astype(BF)
                terms[0, 1] = lax.dot_general(out_ref[...], acts[k][...], DOWN_ROWS, preferred_element_type=F32).astype(BF)

    whole = lambda v: pl.BlockSpec(v.shape, lambda k, at: (0, 0))
    arrays = [two, grad_out, *actives, *grads]
    return pl.pallas_call(
        kernel,
        grid_spec=pltpu.PrefetchScalarGridSpec(
            num_scalar_prefetch=1,
            grid=(count,),
            in_specs=[whole(v) for v in arrays],
            out_specs=pl.BlockSpec((1, 2, width, cols), lambda k, at: (k ^ at[0], 0, 0, 0)),
        ),
        out_shape=jax.ShapeDtypeStruct((count, 2, width, cols), BF),
        compiler_params=params(32 * 2**20),
        cost_estimate=LIGHT,
        name="mlp_terms",
    )(dp_at.astype(jnp.int32).reshape(1) if count > 1 else jnp.zeros((1,), jnp.int32), *arrays)


def lines(*rows):
    width = rows[0].shape[1]
    return jnp.concatenate(list(rows) + [jnp.zeros((8 - len(rows), width), F32)], axis=0)


def norm_back_two_kernel(zs, group, here_ref, there_ref, after_ref, d_ref, gain_ref, w_ref, grad_ref, low_ref, sums_ref, out_ref):
    grad_two = here_ref[...] + there_ref[...].astype(F32)
    unit, scale = normalise(after_ref[...])
    sums_ref[...] = lines(jnp.sum(grad_two * unit, axis=0, keepdims=True), jnp.sum(grad_two, axis=0, keepdims=True))
    grad = d_ref[...] + normalise_back(grad_two, unit, scale, gain_ref[...])
    grad_ref[...] = grad
    low = grad.astype(BF)
    low_ref[...] = low
    for z in range(zs):
        part = jnp.dot(low, w_ref[z], preferred_element_type=F32).astype(BF)
        for core in range(2):
            out_ref[core * zs + z] = part[:, core * group : (core + 1) * group]


def norm_back_one_kernel(zs, group, g_ref, w_ref, joined_ref, after_ref, gain_ref, all_ref, grad_ref, sums_ref):
    grad_one = jnp.zeros(joined_ref.shape, F32)
    for z in range(zs):
        for a in range(3):
            part = jnp.concatenate([g_ref[core * zs + z, :, a * group : (a + 1) * group] for core in range(2)], axis=1)
            at = (3 * z + a) * 2 * group
            all_ref[:, at : at + 2 * group] = part
            grad_one = grad_one + lax.dot_general(part, shares(w_ref, z, a), ACROSS, preferred_element_type=F32)
    unit, scale = normalise(joined_ref[...])
    sums_ref[...] = lines(jnp.sum(grad_one * unit, axis=0, keepdims=True), jnp.sum(grad_one, axis=0, keepdims=True))
    grad_ref[...] = after_ref[...] + normalise_back(grad_one, unit, scale, gain_ref[...])


def normalise(v):
    center = jnp.mean(v, axis=-1, keepdims=True)
    shifted = v - center
    scale = lax.rsqrt(jnp.mean(shifted * shifted, axis=-1, keepdims=True) + EPS)
    return shifted * scale, scale


def normalise_back(g, unit, scale, gain):
    gg = g * gain
    along = jnp.mean(gg * unit, axis=-1, keepdims=True)
    return scale * (gg - jnp.mean(gg, axis=-1, keepdims=True) - unit * along)


def pool_matrix(pooled_index, buffer_index, map_side, offset):
    map_place = buffer_index[None, :] - offset
    bin_start = pooled_index[:, None] * map_side // G
    bin_stop = ((pooled_index[:, None] + 1) * map_side + G - 1) // G
    inside = jnp.logical_and(map_place >= bin_start, map_place < bin_stop)
    real = jnp.logical_and(pooled_index >= 0, pooled_index < G)[:, None]
    return jnp.where(jnp.logical_and(inside, real), 1.0, 0.0).astype(F32) / (bin_stop - bin_start).astype(F32)


def depthwise3(padded, kernel, rows, cols):
    total = None
    for i in range(3):
        for j in range(3):
            term = padded[:, i : i + rows, j : j + cols, :] * kernel[:, 3 * i + j]
            total = term if total is None else total + term
    return total


def rim(v):
    v = jnp.concatenate([shift(v[:, -1:], "strip", 1), v, shift(v[:, :1], "strip", -1)], axis=1)
    return jnp.concatenate([shift(v[:, :, -1:], "tensor", 1), v, shift(v[:, :, :1], "tensor", -1)], axis=2)


def rows_rim(v):
    return jnp.concatenate([shift(v[:, :, -EDGE:], "strip", 1), v, shift(v[:, :, :EDGE], "strip", -1)], axis=2)


def shards(
    res_code, vit_in, map_in, dw_kernel, conv_gain, conv_bias, w_expand, w_reduce, layer_scale, adapt_w, mix_kernel,
    gate_logit, gain_one, bias_one, w_qkv, w_proj, gain_two, bias_two, w_up, w_down, d_vit, d_map,
):
    strip_at, tensor_at, dp_at = (lax.axis_index(a) for a in ("strip", "tensor", "dp"))
    dps, zs = lax.axis_size("dp"), lax.axis_size("tensor")
    items, grid_rows, _, width = vit_in.shape
    _, map_rows, map_cols, channels = map_in.shape
    grid_cols = G // zs
    cells = items * map_rows * map_cols
    tokens = items * grid_rows * grid_cols
    head_cols = w_qkv.shape[2]
    score_scale = HD**-0.5

    expand_z, reduce_z = gather_conv_weight(w_expand, 1), gather_conv_weight(w_reduce, 0.5)
    expand_own, reduce_own = expand_z(0), reduce_z(0)
    expand_near = dp_neighbours(expand_own)
    mlp_own, mlp_gathered = gather_mlp_weights(w_up, w_down)
    qkv_whole = gather_rows(jnp.swapaxes(w_qkv, 0, 1), mlp_gathered)
    proj_whole = gather_rows(w_proj[None]).reshape(zs, width, head_cols)
    count = quarters()

    side = res_code // 32
    offset = (MAXS - side) // 2
    row_cells = strip_at * map_rows + jnp.arange(map_rows, dtype=jnp.int32)
    col_cells = tensor_at * map_cols + jnp.arange(map_cols, dtype=jnp.int32)

    def inside(at):
        low, high = offset[:, None], (offset + side)[:, None]
        return jnp.logical_and(at[None] >= low, at[None] < high).astype(F32)

    row_ok, col_ok = inside(row_cells), inside(col_cells)
    cell_mask = col_ok[:, :, None, None] * row_ok[:, None, :, None]
    many_pools = jax.vmap(pool_matrix, in_axes=(None, None, 0, 0))
    pooled_rows = strip_at * grid_rows + jnp.arange(grid_rows, dtype=jnp.int32)
    pooled_cols = (tensor_at - 1) * grid_cols + jnp.arange(3 * grid_cols, dtype=jnp.int32)
    row_pool = many_pools(pooled_rows, row_cells, side, offset)
    col_pool = many_pools(pooled_cols, col_cells, side, offset).reshape(items, 3, grid_cols, map_cols)
    pool = jnp.einsum("bir,bgjc->bgijcr", row_pool, col_pool)
    pool = pool.reshape(items, 3 * grid_rows * grid_cols, map_cols * map_rows).astype(BF)

    masked = jnp.swapaxes(map_in, 1, 2) * cell_mask.astype(BF)
    taps = jnp.pad(dw_kernel.T.reshape(7, 7, channels), ((0, 0), (0, 1), (0, 0)))
    edges = [later(shift(e, "tensor", step), pool, expand_own) for e, step in ((masked[:, -3:], 1), (masked[:, :3], -1))]
    padded = rows_rim(jnp.concatenate([edges[0], masked, edges[1]], axis=1))
    spread = conv7(padded, taps, map_rows, map_cols).reshape(cells, channels)
    reduce_near = dp_neighbours(later(reduce_own, spread))
    normed = norm_rows(spread, conv_gain, conv_bias)
    if expand_near:
        normed = later(normed, *expand_near)
    normed_both = jnp.concatenate([normed, core_swap(normed)], axis=0)
    expand_pieces, reduce_pieces, pairs = [expand_own, *expand_near], [reduce_own, *reduce_near], []
    x = normed_both
    for k in range(count):
        if k == 3:
            expand_pieces.append(expand_z(1, pairs[2][0]))
        pairs.append(expand(x, expand_pieces[k]))
        x = later(normed_both, pairs[k][0])
    acts, slopes = zip(*pairs)
    if count > 1:
        reduce_pieces.append(dp_across(reduce_near, reduce_z(1, acts[2]), acts[2]))
    branch_sent = back_sum(acts, reduce_pieces, cells, cells, BF)
    branch_there = core_swap(branch_sent)
    branch_here = back_sum(acts, reduce_pieces, 0, cells, F32)
    branch, map_low = map_value_rows(
        branch_here, branch_there, masked.reshape(cells, channels), cell_mask.reshape(cells, 1), layer_scale
    )
    branch, map_low = branch.reshape(masked.shape), map_low.reshape(masked.shape)
    map_out = jnp.swapaxes(map_low, 1, 2)

    pooled3 = lax.dot_general(
        pool, map_low.reshape(items, -1, channels), (((2,), (1,)), ((0,), (0,))), preferred_element_type=F32
    ).reshape(items, 3, -1, channels)
    pooled = (
        pooled3[:, 1]
        + shift(pooled3[:, 0].astype(BF), "tensor", -1).astype(F32)
        + shift(pooled3[:, 2].astype(BF), "tensor", 1).astype(F32)
    )
    pooled_low = pooled.astype(BF).reshape(tokens, channels)
    grid_shape = (items, grid_rows, grid_cols, width)
    adapted = jnp.dot(pooled_low, adapt_w, preferred_element_type=F32).reshape(grid_shape)
    adapted_pad = rim(adapted)
    local_mix = depthwise3(adapted_pad, mix_kernel, grid_rows, grid_cols)
    gate = jnp.tanh(gate_logit)
    mine = lambda v: lax.dynamic_slice_in_dim(v, tensor_at * grid_cols, grid_cols, 2)
    grad_out = mine(d_vit).reshape(tokens, width)
    grad_mlp = grad_out.astype(BF)
    grad_mlp_both = jnp.concatenate([grad_mlp, core_swap(grad_mlp)], axis=0)
    joined = (mine(vit_in) + gate * local_mix).reshape(tokens, width)

    group = head_cols // 2
    line = lambda v: v.reshape(1, width)
    dots = lambda m, n, k: 2 * m * n * k
    spread_heads = lambda v: lax.all_to_all(v, ("strip", "tensor"), 0, 0, tiled=True)
    by_source = lambda v: v.reshape(2 * zs, items, -1, v.shape[-1])
    normed_one, qkv = whole_call(
        functools.partial(qkv_kernel, zs, group),
        [shape(BF, tokens, width), shape(BF, 2 * zs, tokens, 3 * group)],
        [joined, line(gain_one), line(bias_one), qkv_whole],
        dots(tokens, width, 3 * zs * head_cols),
        "qkv",
    )
    mlp_near = dp_neighbours(mlp_own)
    qkv = later(by_source(spread_heads(qkv)), mlp_own, *mlp_near)
    mlp_weights = [mlp_own, *mlp_near, *mlp_far(mlp_near)]
    attention_flops = items * 2 * dots(24 * 24, 24 * 24, group)
    heads = by_item(functools.partial(attention_kernel, group), [qkv], group, 2 * attention_flops, "attention")
    heads = later(spread_heads(heads).reshape(2 * zs, tokens, group), *mlp_weights)
    mixed, after_attn, normed_two = whole_call(
        functools.partial(project_kernel, zs, group),
        [shape(BF, tokens, width), shape(F32, tokens, width), shape(BF, tokens, width)],
        [heads, proj_whole, joined, line(gain_two), line(bias_two)],
        dots(tokens, width, width),
        "project",
    )

    two_both = jnp.concatenate([normed_two, core_swap(normed_two)], axis=0)
    some = mlp_own.shape[2]
    mlp, back, *halves = whole_call(
        functools.partial(mlp_kernel, count),
        [shape(F32, 2 * tokens, width)] * 2 + [shape(BF, 2 * tokens, some)] * (2 * count),
        [two_both, grad_mlp_both, *mlp_weights],
        4 * count * dots(2 * tokens, width, some),
        "mlp",
    )
    actives, grad_ups = halves[:count], halves[count:]
    back_there = core_swap(back[tokens:].astype(BF))
    grad_after, grad_att, sums_two, grad_heads = whole_call(
        functools.partial(norm_back_two_kernel, zs, group),
        [shape(F32, tokens, width), shape(BF, tokens, width), shape(F32, 8, width), shape(BF, 2 * zs, tokens, group)],
        [back[:tokens], back_there, after_attn, grad_out, line(gain_two), proj_whole],
        dots(tokens, width, width),
        "norm_back_two",
    )
    down_terms = lambda left, rights: [
        lax.dot_general(left, r, DOWN_ROWS, preferred_element_type=F32).astype(BF) for r in rights
    ]
    four = count > 1
    mlp_grads = mlp_terms(later(two_both, grad_heads), grad_mlp_both, actives, grad_ups, dp_at)
    grad_heads = later(by_source(spread_heads(grad_heads)), mlp_grads)
    mlp_view, mlp_over_z = mlp_scatter(mlp_grads, dps)
    mlp_there = core_swap(mlp[tokens:].astype(BF))
    to_grid = lambda v: jnp.concatenate(list(v), axis=2).astype(F32)

    grad_qkv = by_item(
        functools.partial(attention_back_kernel, group), [qkv, grad_heads], 3 * group, 5 * attention_flops, "attention_back"
    )
    grad_qkv = later(spread_heads(grad_qkv).reshape(2 * zs, tokens, 3 * group), mlp_grads)
    grad_qkv, grad_joined, sums_one = whole_call(
        functools.partial(norm_back_one_kernel, zs, group),
        [shape(BF, tokens, 3 * width), shape(F32, tokens, width), shape(F32, 8, width)],
        [grad_qkv, qkv_whole, joined, grad_after, line(gain_one)],
        dots(tokens, width, 3 * width),
        "norm_back_one",
    )

    grad_grid = grad_joined.reshape(grid_shape)
    over = (0, 1, 2)
    grad_mix = grad_grid * gate
    grad_adapted = depthwise3(rim(grad_mix), mix_kernel[:, ::-1], grid_rows, grid_cols)
    grad_adapted = grad_adapted.astype(BF).reshape(tokens, width)
    grad_adapted = later(grad_adapted, mlp_view)
    grad_pooled = lax.dot_general(grad_adapted, adapt_w, ACROSS, preferred_element_type=F32).astype(BF)
    grad_late = later(grad_grid, grad_pooled)
    grad_gate = jnp.sum(grad_late * local_mix, axis=over) * (1.0 - gate * gate)
    grad_taps = [
        jnp.sum(adapted_pad[:, i : i + grid_rows, j : j + grid_cols] * (grad_late * gate), axis=over)
        for i in range(3)
        for j in range(3)
    ]
    small_vit = jnp.stack(
        grad_taps
        + [
            grad_gate,
            sums_one[0],
            sums_one[1],
            sums_two[0],
            sums_two[1],
        ],
        axis=0,
    )
    small_vit = scatter_steps(scatter_steps(later(small_vit, grad_pooled), "dp"), "strip")
    row_terms = (
        down_terms(later(normed_one, grad_pooled), [grad_qkv])
        + down_terms(later(grad_att, grad_pooled), [mixed])
        + down_terms(later(pooled_low, grad_pooled), [grad_adapted])
    )
    grad_pooled = grad_pooled.reshape(items, -1, channels)
    rows_sums, rows_over_z = rows_scatter(row_terms)
    grad_pooled = jnp.concatenate(
        [later(shift(grad_pooled, "tensor", 1), *row_terms, small_vit), grad_pooled, shift(grad_pooled, "tensor", -1)], axis=1
    )
    grad_map = lax.dot_general(pool, grad_pooled, (((1,), (1,)), ((0,), (0,))), preferred_element_type=F32)
    grad_map = jnp.swapaxes(d_map, 1, 2).astype(F32) + grad_map.reshape(masked.shape)

    kept = cell_mask * grad_map
    grad_scale = jnp.sum(kept * branch.astype(F32), axis=over)
    grad_branch = (kept * layer_scale).astype(BF).reshape(cells, channels)
    grad_branch_both = jnp.concatenate([grad_branch, core_swap(grad_branch)], axis=0)
    rows_part = rows_over_z(grad_map)
    reduce_terms = conv_terms(grad_branch_both, acts, lambda v: later(v, rows_sums))
    grad_hidden, last = [], [reduce_terms[-1]]
    if four:
        reduce_first = conv_dp(reduce_terms)
    for k in range(count):
        last = [back_slope(later(grad_branch_both, *last), reduce_pieces[k], slopes[k])]
        grad_hidden += last
    (both_low,) = whole_call(
        pair_kernel,
        [shape(BF, 2, tokens, width)],
        [after_attn, mlp[:tokens], later(mlp_there, rows_sums), grad_joined],
        tokens * width,
        "vit_pair",
    )
    both_every = lax.all_gather(both_low.reshape(2, *grid_shape), "tensor", axis=0)
    if four:
        near = tall(later(normed_both, last[0]), grad_hidden[1:], [(0, 2), (1, 2)], "tall_near")
        keep = tall(later(normed_both, near[0]), grad_hidden[:3], [(0, 2), (0, 1)], "tall_keep")
        expand_first = conv_dp([*near, *keep])
        done = keep[0]
    else:
        expand_terms = conv_terms(normed_both, grad_hidden, lambda v: later(v, *last))
        done = expand_terms[0]
    last = [done]
    if four:
        reduce_sent, reduce_second = reduce_first(done)
        last += [*reduce_sent]
    sent = later(grad_hidden[0], *last)
    normed_sent = back_sum([sent] + grad_hidden[1:], expand_pieces, cells, cells, BF)
    normed_there = core_swap(normed_sent)
    kept_here = later(grad_hidden[0], normed_sent)
    normed_here = back_sum([kept_here] + grad_hidden[1:], expand_pieces, 0, cells, F32)
    last = [normed_here, rows_part]
    if four:
        reduce_view = reduce_second(normed_here)
        last += [reduce_view]
    else:
        reduce_view, expand_view = (
            jnp.swapaxes(t[0].reshape(2, zs, -1, t[0].shape[1]), 0, 1) for t in (reduce_terms, expand_terms)
        )
    reduce_part = conv_scatter(reduce_view)
    grad_spread, sums_conv = norm_rows_back(later(normed_here, *last), normed_there, spread, conv_gain)
    grad_spread = grad_spread.reshape(masked.shape)
    beside = shift(grad_spread[:, -3:], "tensor", 1), shift(grad_spread[:, :3], "tensor", -1)
    last = [both_every]
    if four:
        expand_sent, expand_second = expand_first(grad_spread)
        last += [*expand_sent]
    grad_taps = tap_grad(padded, later(grad_spread, *last), map_rows, map_cols)
    last = [grad_taps]
    if four:
        expand_view = expand_second(grad_taps)
        last += [expand_view]
    small_conv = jnp.concatenate([grad_taps.reshape(56, channels), sums_conv[:2], grad_scale[None]], axis=0)
    rim_spread = jnp.concatenate([later(beside[0], *last), grad_spread, later(beside[1], *last)], axis=1)
    expand_part = conv_scatter(expand_view)
    reduce_both = conv_cores(later(reduce_part, rim_spread))
    small_conv = scatter_steps(later(small_conv, rim_spread), "strip")
    wide_spread = rows_rim(rim_spread)
    mlp_part = mlp_over_z(wide_spread)
    grad_map_in = conv7(
        later(wide_spread, reduce_both, small_conv),
        taps,
        map_rows,
        map_cols,
        True,
    )
    out_reduce = conv_rows(reduce_both, grad_map_in)
    small_conv = sum_dp(small_conv, reduce_both, grad_map_in)
    out_qkv, out_proj, out_adapt = rows_sum(row_terms, rows_part, grad_map_in)
    grad_map_in = jnp.swapaxes(cell_mask * (kept + grad_map_in), 1, 2)
    expand_both = conv_cores(later(expand_part, grad_map_in))
    out_expand = conv_rows(expand_both)
    out_up, out_down = mlp_rows(jnp.swapaxes(later(mlp_part, expand_both), 0, 1), dps)
    both_every = later(both_every, expand_both)
    vit_out, grad_vit = to_grid(both_every[:, 0]), to_grid(both_every[:, 1])
    out_adapt = gather_bits(later(out_adapt.astype(BF), expand_both)).astype(F32)
    small_conv = scatter_steps(later(small_conv, expand_both), "tensor")
    small_vit = all_sum(later(small_vit, expand_both), ("tensor",))
    conv_share = channels // (2 * zs)
    out_taps = small_conv[:56].reshape(7, 8, conv_share)[:, :7].reshape(49, conv_share).T
    return (
        vit_out,
        map_out,
        grad_vit,
        grad_map_in,
        out_taps,
        small_conv[56],
        small_conv[57],
        out_expand,
        out_reduce,
        small_conv[58],
        out_adapt,
        small_vit[:9].T,
        small_vit[9],
        small_vit[10],
        small_vit[11],
        out_qkv.reshape(-1, 3, head_cols),
        out_proj,
        small_vit[12],
        small_vit[13],
        out_up,
        out_down,
    )


def solution(mesh):
    rows = P("dp", "strip", None, None)
    maps = P("dp", "strip", "tensor", None)
    conv = ("strip", "tensor")
    vit = ("dp", "strip")
    in_specs = (
        P("dp"), rows, maps, P(), P(), P(), P(conv, None), P(conv, None), P(), P(), P(), P(), P(), P(),
        P(None, None, "tensor"), P(None, "tensor"), P(), P(), P(None, "tensor"), P(None, "tensor"), rows, maps,
    )
    out_specs = (
        rows, maps, rows, maps, P(conv, None), P(conv), P(conv), P(conv, None), P(conv, None), P(conv),
        P(vit, None), P(vit, None), P(vit), P(vit), P(vit), P(vit, None, "tensor"), P(vit, "tensor"), P(vit), P(vit),
        P(vit, "tensor"), P(vit, "tensor"),
    )
    return jax.shard_map(shards, mesh=mesh, in_specs=in_specs, out_specs=out_specs, check_vma=False)
```

```python
import functools

import jax
import jax.numpy as jnp
from jax import lax
from jax.experimental import pallas as pl
from jax.experimental.pallas import tpu as pltpu
from jax.sharding import PartitionSpec as P

HD = 64
G = 24
MAXS = 48
EPS = 1e-06
BF = jnp.bfloat16
F32 = jnp.float32
DOWN_ROWS = (((0,), (0,)), ((), ()))
ACROSS = (((1,), (1,)), ((), ()))
VMEM = 48 * 2**20
EDGE = 8
LIGHT = pl.CostEstimate(flops=1, bytes_accessed=1, transcendentals=0)


def core_swap(v):
    return lax.ppermute(v, "strip", [(0, 1), (1, 0)])


def dp_swap(v, bit):
    return lax.ppermute(v, "dp", [(i, i ^ bit) for i in range(lax.axis_size("dp"))])


def shift(v, axis, step):
    count = lax.axis_size(axis)
    pairs = [(i, i + step) for i in range(count) if 0 <= i + step < count]
    return lax.ppermute(v, axis, pairs)


def all_sum(v, axes):
    for axis in axes:
        count, bit = lax.axis_size(axis), 1
        while bit < count:
            v = v + lax.ppermute(v, axis, [(i, i ^ bit) for i in range(count)])
            bit *= 2
    return v


def gather_bits(v, axis="tensor"):
    count, at, bit = lax.axis_size(axis), lax.axis_index(axis), 1
    while bit < count:
        other = lax.ppermute(v, axis, [(i, i ^ bit) for i in range(count)])
        upper = (at // bit) % 2 == 1
        v = jnp.concatenate([jnp.where(upper, other, v), jnp.where(upper, v, other)], axis=1)
        bit *= 2
    return v


def quarters():
    return 4 if lax.axis_size("dp") == 4 else 1


def reduce_dp(near_a, near_b, keep_a, keep_b, arrange):
    near_a, near_b = dp_swap(near_a, 1), dp_swap(near_b, 2)

    def first(*waits):
        a, b = later(near_a, *waits), later(near_b, *waits)
        sent = sum_pairs([keep_a[1], (a, 1)], [keep_b[1], (b, 1)])
        last_a, last_b = dp_swap(sent[0], 2), dp_swap(sent[1], 1)

        def second(*waits):
            got_a, got_b = later(last_a, *waits), later(last_b, *waits)
            return arrange([keep_a[0], (a, 0), (got_a, None)], [keep_b[0], (b, 0), (got_b, None)])

        return sent, second

    return first


def in_order(mine, other, at):
    first = at == 0
    return jnp.stack([jnp.where(first, mine, other), jnp.where(first, other, mine)], axis=0)


def dp_order(pieces):
    at = lax.axis_index("dp")
    bit_x, bit_y = at % 2 == 1, at // 2 == 1
    row_own = [jnp.where(bit_x, pieces[1], pieces[0]), jnp.where(bit_x, pieces[0], pieces[1])]
    row_far = [jnp.where(bit_x, pieces[3], pieces[2]), jnp.where(bit_x, pieces[2], pieces[3])]
    return jnp.stack(
        [jnp.where(bit_y, f, o) for o, f in zip(row_own, row_far)]
        + [jnp.where(bit_y, o, f) for o, f in zip(row_own, row_far)],
        axis=0,
    )


def later(v, *others):
    return lax.optimization_barrier((v, *others))[0]


def add(*terms):
    return functools.reduce(lambda a, b: a + b, [t.astype(F32) for t in terms])


def sum_dp(v, before, after):
    count = lax.axis_size("dp")
    v = later(v, before)
    return functools.reduce(lambda a, b: a + b, [v] + [later(dp_swap(v, k), after) for k in range(1, count)])


def at_index(v, i, axis=0):
    return lax.dynamic_index_in_dim(v, i, axis, keepdims=False)


def hidden_share(block, strip_at, part, q):
    width = block.shape[1] // (2 * q)
    return lax.dynamic_slice_in_dim(block, (strip_at * q + part) * width, width, 1)


def gather_conv_weight(block, across):
    q = quarters()
    strip_at = lax.axis_index("strip")
    width = block.shape[1] // (2 * q)
    parts = [(0, width)] if q == 1 else [(lax.axis_index("dp"), width), (lax.axis_index("dp") ^ 3, int(width * across))]
    cut = lambda core: [hidden_share(block, core, part, q)[:, :cols] for part, cols in parts]
    mine = cut(strip_at)
    others = core_swap(jnp.concatenate(cut(1 - strip_at), axis=1))
    ends = [0, width, others.shape[1]]
    both = [in_order(own, others[:, ends[i] : ends[i + 1]], strip_at) for i, own in enumerate(mine)]

    def along_z(i, *waits):
        whole = lax.all_gather(both[i], "tensor", axis=0)
        whole = later(whole, *waits) if waits else whole
        return jnp.swapaxes(whole, 0, 1).reshape(-1, both[i].shape[2])

    return along_z


def dp_across(near, first, *waits):
    half, skip = near[0].shape[0] // 2, first.shape[1]
    near = [later(n, *waits)[:, skip:] for n in near]
    rest = jnp.concatenate([dp_swap(near[0][:half], 2), dp_swap(near[1][half:], 1)], axis=0)
    return jnp.concatenate([first, rest], axis=1)


def dp_neighbours(own):
    return [] if quarters() == 1 else [dp_swap(own, 1), dp_swap(own, 2)]


def conv_terms(left, rights, in_turn):
    if len(rights) == 1:
        return [lax.dot_general(left, rights[0], DOWN_ROWS, preferred_element_type=F32).astype(BF)]
    own, beside_x, beside_y, far = rights
    near = tall(in_turn(left), [beside_x, beside_y, far], [(0, 2), (1, 2)], "tall_near")
    keep = tall(later(left, near[0]), [own, beside_x, beside_y], [(0, 2), (0, 1)], "tall_keep")
    return [*near, *keep]


def conv_dp(terms):
    near_a, near_b, keep_a, keep_b = terms
    return reduce_dp(near_a, near_b, [(keep_a, 0), (keep_a, 1)], [(keep_b, 0), (keep_b, 1)], sum_rows)


def conv_scatter(view):
    _, _, rows, width = view.shape
    return lax.psum_scatter(view.reshape(-1, width), "tensor", scatter_dimension=0, tiled=True).reshape(2, rows, width)


def conv_cores(part):
    strip_at = lax.axis_index("strip")
    mine = at_index(part, strip_at)
    other = core_swap(at_index(part, 1 - strip_at))
    return in_order(mine, other, strip_at)


def conv_rows(both, *waits):
    if quarters() == 1:
        return jnp.concatenate(list(lax.psum(both, "dp")), axis=1).astype(F32)
    near = [dp_swap(both, k) for k in (1, 2, 3)]
    every = dp_order([both] + [later(n, *waits) for n in near])
    return jnp.concatenate([every[d, c] for c in range(2) for d in range(4)], axis=1).astype(F32)


def gather_mlp_weights(up, down):
    q = quarters()
    strip_at, dp_at = lax.axis_index("strip"), lax.axis_index("dp") if q > 1 else 0
    mine = jnp.concatenate([hidden_share(w, strip_at, dp_at, q) for w in (up, down)], axis=0)
    whole = lax.all_gather(mine, "tensor", axis=0)
    return jnp.concatenate(list(whole), axis=1).reshape(2, up.shape[0], -1), whole


def mlp_far(near):
    return [dp_swap(near[0][0], 2), dp_swap(near[1][1], 1)] if near else []


def mlp_scatter(terms, dps):
    _, _, width, cols = terms.shape
    if quarters() > 1:
        terms = lax.psum_scatter(terms.reshape(-1, cols), "dp", scatter_dimension=0, tiled=True)
    terms = terms.reshape(2, width, cols)
    view = sum_cols([(terms, 0)], [(terms, 1)])
    cols = view.shape[3]

    def over_z(*waits):
        part = lax.psum_scatter(later(view, *waits).reshape(-1, cols), "tensor", scatter_dimension=0, tiled=True)
        return part.reshape(2, dps * 2, -1, cols)

    return view, over_z


def mlp_rows(part, dps):
    rows, cols = part.shape[2:]
    if quarters() > 1:
        parts = lax.all_to_all(part, ("dp", "strip"), 0, 0).reshape(dps, 2, 2, rows, cols)
        return [
            jnp.concatenate([parts[d, c, i] for c in range(2) for d in range(dps)], axis=1).astype(F32) for i in range(2)
        ]
    strip_at = lax.axis_index("strip")
    part = lax.psum_scatter(part.reshape(dps, 2, 2, rows, cols), "dp", scatter_dimension=0)
    mine = at_index(part, strip_at)
    other = core_swap(at_index(part, 1 - strip_at))
    both = in_order(mine, other, strip_at)
    return [jnp.concatenate([both[0, i], both[1, i]], axis=1).astype(F32) for i in range(2)]


def rows_layout(whole):
    zs, dps = lax.axis_size("tensor"), lax.axis_size("dp")
    cut = min(w.shape[1] for w in whole) // zs
    return [w.reshape(dps, 2, -1, w.shape[1]) for w in whole], cut


def rows_scatter(whole):
    zs, dps, strip_at = lax.axis_size("tensor"), lax.axis_size("dp"), lax.axis_index("strip")
    view, cut = rows_layout(whole)

    def of_core(core):
        parts = [at_index(v, core, 1) for v in view]
        groups = []
        for z in range(zs):
            group = []
            for v in parts:
                share = v.shape[2] // zs
                group += [v[:, :, z * share + c : z * share + c + cut] for c in range(0, share, cut)]
            groups.append(jnp.concatenate(group, axis=1))
        return jnp.concatenate(groups, axis=0)

    sums = add(of_core(strip_at), core_swap(of_core(1 - strip_at))).astype(BF)

    def over_z(*waits):
        part = lax.psum_scatter(later(sums, *waits).reshape(-1, cut), "tensor", scatter_dimension=0, tiled=True)
        return part.reshape(dps, -1, cut)

    return sums, over_z


def rows_sum(whole, part, *waits):
    zs, dp_at = lax.axis_size("tensor"), lax.axis_index("dp")
    view, cut = rows_layout(whole)
    if quarters() == 1:
        total = lax.psum_scatter(part, "dp", scatter_dimension=0).astype(F32)
    else:
        near = [dp_swap(at_index(part, dp_at ^ k), k) for k in (1, 2, 3)]
        total = add(at_index(part, dp_at), *[later(n, *waits) for n in near])
    outs, at = [], 0
    for v in view:
        rows = v.shape[2]
        count = v.shape[3] // zs // cut
        outs.append(jnp.concatenate([total[at + i * rows : at + (i + 1) * rows] for i in range(count)], axis=1))
        at += count * rows
    return outs


def scatter_steps(v, axis):
    count, bit, at = lax.axis_size(axis), lax.axis_size(axis) // 2, lax.axis_index(axis)
    while bit >= 1:
        half = v.shape[1] // 2
        upper = (at // bit) % 2
        mine = lax.dynamic_slice_in_dim(v, upper * half, half, 1)
        other = lax.dynamic_slice_in_dim(v, (1 - upper) * half, half, 1)
        v = mine + lax.ppermute(other, axis, [(i, i ^ bit) for i in range(count)])
        bit //= 2
    return v


def gather_rows(block, *waits):
    _, width, cols = block.shape
    dps, zs = lax.axis_size("dp"), lax.axis_size("tensor")
    rows = width // (2 * dps)
    at = lax.axis_index("dp") * 2 + lax.axis_index("strip")
    mine = lax.dynamic_slice_in_dim(block, at * rows, rows, 1)
    if waits:
        mine = later(mine, *waits)
    whole = lax.all_gather(mine, ("tensor", "dp", "strip"), axis=0)
    return whole.reshape(zs, 2 * dps, -1, rows, cols)


def params(limit=VMEM):
    return pltpu.CompilerParams(vmem_limit_bytes=limit)


def add_kernel(counts, *refs):
    outs = refs[sum(counts) :]
    at = 0
    for i, count in enumerate(counts):
        total = add(*[r[0] if len(r.shape) == 3 else r[...] for r in refs[at : at + count]]).astype(BF)
        if len(outs) == 1:
            outs[0][0, i] = total
        else:
            outs[i][...] = total
        at += count


def sum_call(groups, grid, block, place, out_specs, out_shape, name):
    specs = []
    for array, lead in [term for group in groups for term in group]:
        if lead is None:
            specs.append(pl.BlockSpec(block, place))
        else:
            specs.append(pl.BlockSpec((1, *block), lambda i, lead=lead: (lead, *place(i))))
    return pl.pallas_call(
        functools.partial(add_kernel, [len(g) for g in groups]),
        grid=(grid,),
        in_specs=specs,
        out_specs=out_specs,
        out_shape=out_shape,
        compiler_params=params(20 * 2**20),
        cost_estimate=LIGHT,
        name=name,
    )(*[array for group in groups for array, _ in group])


def sum_pairs(*groups):
    rows, cols = groups[0][0][0].shape[-2:]
    block, place = (256, cols), lambda i: (i, 0)
    return sum_call(
        groups,
        rows // 256,
        block,
        place,
        [pl.BlockSpec(block, place)] * len(groups),
        [jax.ShapeDtypeStruct((rows, cols), BF)] * len(groups),
        "sum_pairs",
    )


def sum_rows(*groups):
    zs = lax.axis_size("tensor")
    rows, cols = groups[0][0][0].shape[-2:]
    rows = rows // zs
    return sum_call(
        groups,
        zs,
        (rows, cols),
        lambda i: (i, 0),
        pl.BlockSpec((1, 2, rows, cols), lambda i: (i, 0, 0, 0)),
        jax.ShapeDtypeStruct((zs, 2, rows, cols), BF),
        "sum_rows",
    )


def sum_cols(*groups):
    zs = lax.axis_size("tensor")
    rows, cols = groups[0][0][0].shape[-2:]
    cols = cols // zs
    return sum_call(
        groups,
        zs,
        (rows, cols),
        lambda i: (0, i),
        pl.BlockSpec((1, 2, rows, cols), lambda i: (i, 0, 0, 0)),
        jax.ShapeDtypeStruct((zs, 2, rows, cols), BF),
        "sum_cols",
    )


def conv7_kernel(rows, cols, back, x_ref, k_ref, out_ref, wide):
    wide[...] = x_ref[0].astype(F32)

    def tap_row(i, sums):
        sums = list(sums)
        taps = k_ref[6 - i if back else i]
        for m in range(cols + 6):
            x = wide[m, pl.ds(i + EDGE - 3, rows), :]
            for j in range(7):
                c = m - j
                if 0 <= c < cols:
                    tap = 6 - j if back else j
                    sums[c] = sums[c] + x * taps[tap : tap + 1]
        return tuple(sums)

    sums = lax.fori_loop(0, 7, tap_row, tuple(jnp.zeros((rows, 128), F32) for _ in range(cols)))
    for c in range(cols):
        out_ref[0, c] = sums[c]


def conv7(padded, taps, rows, cols, back=False):
    items, _, _, channels = padded.shape
    return pl.pallas_call(
        functools.partial(conv7_kernel, rows, cols, back),
        grid=(items, channels // 128),
        in_specs=[
            pl.BlockSpec((1, cols + 6, rows + 2 * EDGE, 128), lambda b, c: (b, 0, 0, c)),
            pl.BlockSpec((7, 8, 128), lambda b, c: (0, 0, c)),
        ],
        out_specs=pl.BlockSpec((1, cols, rows, 128), lambda b, c: (b, 0, 0, c)),
        out_shape=jax.ShapeDtypeStruct((items, cols, rows, channels), F32),
        scratch_shapes=[pltpu.VMEM((cols + 6, rows + 2 * EDGE, 128), F32)],
        compiler_params=params(8 * 2**20),
        cost_estimate=LIGHT,
        name="depthwise",
    )(padded, taps)


def tap_grad_kernel(rows, cols, x_ref, g_ref, out_ref, wide, full):
    wide[...] = x_ref[0].astype(F32)
    full[...] = g_ref[0].astype(F32)

    @pl.when(pl.program_id(1) == 0)
    def _():
        out_ref[...] = jnp.zeros_like(out_ref)

    def tap_row(i, _):
        sums = [jnp.zeros((8, 128), F32) for _ in range(7)]
        grads = [full[c] for c in range(cols)]
        for m in range(cols + 6):
            x = wide[m, pl.ds(i + EDGE - 3, rows), :]
            for j in range(7):
                c = m - j
                if 0 <= c < cols:
                    sums[j] = sums[j] + (x * grads[c]).reshape(rows // 8, 8, 128).sum(axis=0)
        lines = [jnp.sum(s, axis=0, keepdims=True) for s in sums]
        out_ref[i] += jnp.concatenate(lines + [jnp.zeros((1, 128), F32)], axis=0)
        return 0

    lax.fori_loop(0, 7, tap_row, 0)


def tap_grad(padded, grad, rows, cols):
    items, _, _, channels = padded.shape
    return pl.pallas_call(
        functools.partial(tap_grad_kernel, rows, cols),
        grid=(channels // 128, items),
        in_specs=[
            pl.BlockSpec((1, cols + 6, rows + 2 * EDGE, 128), lambda c, b: (b, 0, 0, c)),
            pl.BlockSpec((1, cols, rows, 128), lambda c, b: (b, 0, 0, c)),
        ],
        out_specs=pl.BlockSpec((7, 8, 128), lambda c, b: (0, 0, c)),
        out_shape=jax.ShapeDtypeStruct((7, 8, channels), F32),
        scratch_shapes=[pltpu.VMEM((cols + 6, rows + 2 * EDGE, 128), F32), pltpu.VMEM((cols, rows, 128), F32)],
        compiler_params=params(8 * 2**20),
        cost_estimate=LIGHT,
        name="tap_grad",
    )(padded, grad)


def map_kernel(here_ref, there_ref, masked_ref, mask_ref, scale_ref, branch_ref, value_ref):
    branch = here_ref[...] + there_ref[...].astype(F32)
    branch_ref[...] = branch.astype(BF)
    value_ref[...] = (mask_ref[...] * (masked_ref[...].astype(F32) + scale_ref[...] * branch)).astype(BF)


def map_value_rows(here, there, masked, mask, scale):
    rows, width = here.shape
    block = row_block(rows, 144)
    tile, line = pl.BlockSpec((block, width), lambda i: (i, 0)), pl.BlockSpec((1, width), lambda i: (0, 0))
    return pl.pallas_call(
        map_kernel,
        grid=(rows // block,),
        in_specs=[tile, tile, tile, pl.BlockSpec((block, 1), lambda i: (i, 0)), line],
        out_specs=[tile, tile],
        out_shape=[jax.ShapeDtypeStruct((rows, width), BF)] * 2,
        compiler_params=params(20 * 2**20),
        cost_estimate=LIGHT,
        name="map_value",
    )(here, there, masked, mask, scale.reshape(1, width))


def norm_kernel(v_ref, gain_ref, bias_ref, out_ref):
    unit, _ = normalise(v_ref[...])
    out_ref[...] = (unit * gain_ref[...] + bias_ref[...]).astype(BF)


def norm_rows(v, gain, bias):
    rows, width = v.shape
    block = row_block(rows, 144)
    tile, line = pl.BlockSpec((block, width), lambda i: (i, 0)), pl.BlockSpec((1, width), lambda i: (0, 0))
    return pl.pallas_call(
        norm_kernel,
        grid=(rows // block,),
        in_specs=[tile, line, line],
        out_specs=tile,
        out_shape=jax.ShapeDtypeStruct((rows, width), BF),
        compiler_params=params(16 * 2**20),
        cost_estimate=LIGHT,
        name="norm",
    )(v, gain.reshape(1, width), bias.reshape(1, width))


def norm_back_kernel(here_ref, there_ref, v_ref, gain_ref, out_ref, sums_ref):
    @pl.when(pl.program_id(0) == 0)
    def _():
        sums_ref[...] = jnp.zeros_like(sums_ref)

    grad = here_ref[...] + there_ref[...].astype(F32)
    unit, scale = normalise(v_ref[...])
    sums_ref[...] += lines(jnp.sum(grad * unit, axis=0, keepdims=True), jnp.sum(grad, axis=0, keepdims=True))
    out_ref[...] = normalise_back(grad, unit, scale, gain_ref[...]).astype(BF)


def norm_rows_back(here, there, v, gain):
    rows, width = v.shape
    block = row_block(rows, 144)
    tile, line = pl.BlockSpec((block, width), lambda i: (i, 0)), pl.BlockSpec((1, width), lambda i: (0, 0))
    return pl.pallas_call(
        norm_back_kernel,
        grid=(rows // block,),
        in_specs=[tile, tile, tile, line],
        out_specs=[tile, pl.BlockSpec((8, width), lambda i: (0, 0))],
        out_shape=[jax.ShapeDtypeStruct((rows, width), BF), jax.ShapeDtypeStruct((8, width), F32)],
        compiler_params=params(20 * 2**20),
        cost_estimate=LIGHT,
        name="norm_back",
    )(here, there, v, gain.reshape(1, width))


def gelu_pair(h):
    cdf = 0.5 * (1.0 + lax.erf(h * (0.5**0.5)))
    pdf = jnp.exp(h * h * -0.5) * 0.3989422804014327
    return h * cdf, cdf + h * pdf


def expand_kernel(step, x_ref, w_ref, act_ref, slope_ref):
    x = x_ref[...]
    for at in range(0, w_ref.shape[1], step):
        h = jnp.dot(x, w_ref[:, at : at + step], preferred_element_type=F32)
        act, slope = gelu_pair(h)
        act_ref[:, at : at + step] = act.astype(BF)
        slope_ref[:, at : at + step] = slope.astype(BF)


def row_block(rows, most):
    best = 16
    for block in range(16, most + 1, 16):
        if rows % block == 0:
            best = block
    return best


def expand(x, w):
    m, k = x.shape
    n = w.shape[1]
    bm = row_block(m, 432)
    bn = min(n, 768)
    spec = pl.BlockSpec((bm, bn), lambda j, i: (i, j))
    return pl.pallas_call(
        functools.partial(expand_kernel, 256),
        grid=(n // bn, m // bm),
        in_specs=[pl.BlockSpec((bm, k), lambda j, i: (i, 0)), pl.BlockSpec((k, bn), lambda j, i: (0, j))],
        out_specs=[spec, spec],
        out_shape=[jax.ShapeDtypeStruct((m, n), BF)] * 2,
        compiler_params=params(20 * 2**20),
        cost_estimate=LIGHT,
        name="expand_gelu",
    )(x, w)


def back_sum_kernel(count, *refs):
    out_ref = refs[-1]
    total = None
    for a_ref, w_ref in zip(refs[:count], refs[count : 2 * count]):
        term = lax.dot_general(a_ref[...], w_ref[...], ACROSS, preferred_element_type=F32)
        total = term if total is None else total + term
    out_ref[...] = total.astype(out_ref.dtype)


def back_sum(parts, weights, first, rows, dtype, bn=512, most=432):
    n = weights[0].shape[0]
    ks = [w.shape[1] for w in weights]
    bm = row_block(rows, most)
    skip = first // bm
    return pl.pallas_call(
        functools.partial(back_sum_kernel, len(parts)),
        grid=(n // bn, rows // bm),
        in_specs=[pl.BlockSpec((bm, k), lambda j, i: (i + skip, 0)) for k in ks]
        + [pl.BlockSpec((bn, k), lambda j, i: (j, 0)) for k in ks],
        out_specs=pl.BlockSpec((bm, bn), lambda j, i: (i, j)),
        out_shape=jax.ShapeDtypeStruct((rows, n), dtype),
        compiler_params=params(52 * 2**20),
        cost_estimate=LIGHT,
        name="reduce_sum",
    )(*parts, *weights)


def tall(a, rights, uses, name):
    m, n = a.shape
    cols = rights[0].shape[1]
    bm = 256
    steps = n // 2 // bm

    def kernel(a_ref, *refs):
        outs = refs[-2:]
        for half in range(2):

            @pl.when(pl.program_id(0) // steps == half)
            def _():
                left = a_ref[...]
                for i, use in enumerate(uses[half]):
                    outs[half][i] = lax.dot_general(left, refs[use][...], DOWN_ROWS, preferred_element_type=F32).astype(BF)

    def out_spec(half):
        place = lambda i: (0, jnp.clip(i - half * steps, 0, steps - 1), 0)
        return pl.BlockSpec((len(uses[half]), bm, cols), place)

    return pl.pallas_call(
        kernel,
        grid=(2 * steps,),
        in_specs=[pl.BlockSpec((m, bm), lambda i: (0, i))] + [pl.BlockSpec((m, cols), lambda i: (0, 0)) for _ in rights],
        out_specs=[out_spec(0), out_spec(1)],
        out_shape=[jax.ShapeDtypeStruct((len(u), n // 2, cols), BF) for u in uses],
        compiler_params=params(28 * 2**20),
        cost_estimate=LIGHT,
        name=name,
    )(a, *rights)


def back_slope(a, w, slope):
    m, k = a.shape
    n = w.shape[1]
    bm, bn = row_block(m, 432), min(n, 768)

    def kernel(a_ref, w_ref, s_ref, out_ref):
        left = a_ref[...]
        for at in range(0, bn, 256):
            cut = slice(at, at + 256)
            grad = jnp.dot(left, w_ref[:, cut], preferred_element_type=F32)
            out_ref[:, cut] = (grad * s_ref[:, cut].astype(F32)).astype(BF)

    spec = pl.BlockSpec((bm, bn), lambda j, i: (i, j))
    return pl.pallas_call(
        kernel,
        grid=(n // bn, m // bm),
        in_specs=[pl.BlockSpec((bm, k), lambda j, i: (i, 0)), pl.BlockSpec((k, bn), lambda j, i: (0, j)), spec],
        out_specs=spec,
        out_shape=jax.ShapeDtypeStruct((m, n), BF),
        compiler_params=params(20 * 2**20),
        cost_estimate=LIGHT,
        name="back_slope",
    )(a, w, slope)


def whole_call(kernel, outs, args, flops, name):
    vmem = pl.BlockSpec(memory_space=pltpu.VMEM)
    bytes_accessed = sum(a.size * a.dtype.itemsize for a in args) + sum(o.size * o.dtype.itemsize for o in outs)
    return pl.pallas_call(
        kernel,
        in_specs=[vmem] * len(args),
        out_specs=[vmem] * len(outs),
        out_shape=outs,
        compiler_params=params(36 * 2**20),
        cost_estimate=LIGHT,
        name=name,
    )(*args)


def shape(dtype, *dims):
    return jax.ShapeDtypeStruct(dims, dtype)


def shares(w_ref, z, a):
    _, count, _, rows, cols = w_ref.shape
    return w_ref[z, :, a].reshape(count * rows, cols)


def qkv_kernel(zs, group, joined_ref, gain_ref, bias_ref, w_ref, normed_ref, out_ref):
    unit, _ = normalise(joined_ref[...])
    normed = (unit * gain_ref[...] + bias_ref[...]).astype(BF)
    normed_ref[...] = normed
    for z in range(zs):
        for a in range(3):
            part = jnp.dot(normed, shares(w_ref, z, a), preferred_element_type=F32).astype(BF)
            for core in range(2):
                out_ref[core * zs + z, :, a * group : (a + 1) * group] = part[:, core * group : (core + 1) * group]


def tokens_of(ref):
    v = ref[:, 0].astype(F32)
    return v.reshape(v.shape[0] * v.shape[1], v.shape[2]).astype(BF)


def head_lanes(heads, lanes):
    lane = lax.broadcasted_iota(jnp.int32, (1, lanes), 1)
    return [jnp.logical_and(lane >= h * HD, lane < (h + 1) * HD) for h in range(heads)]


def only(lanes, v):
    return jnp.where(lanes, v, jnp.zeros((), v.dtype))


def head_probs(q, k):
    scores = lax.dot_general(q, k, ACROSS, preferred_element_type=F32) * HD**-0.5
    powers = jnp.exp(scores - jnp.max(scores, axis=-1, keepdims=True))
    return powers * (1.0 / jnp.sum(powers, axis=-1, keepdims=True))


def attention_kernel(group, qkv_ref, out_ref):
    qkv = tokens_of(qkv_ref)
    q, k, v = (qkv[:, a * group : (a + 1) * group] for a in range(3))
    mixed = jnp.zeros(v.shape, F32)
    for lanes in head_lanes(group // HD, group):
        probs = head_probs(only(lanes, q), k).astype(BF)
        mixed = jnp.where(lanes, jnp.dot(probs, v, preferred_element_type=F32), mixed)
    out_ref[:, 0] = mixed.reshape(out_ref.shape[0], out_ref.shape[2], group).astype(BF)


def attention_back_kernel(group, qkv_ref, grad_ref, out_ref):
    qkv = tokens_of(qkv_ref)
    grad = tokens_of(grad_ref)
    q, k, v = (qkv[:, a * group : (a + 1) * group] for a in range(3))
    sums = [jnp.zeros(v.shape, F32) for _ in range(3)]
    for lanes in head_lanes(group // HD, group):
        probs = head_probs(only(lanes, q), k)
        grad_h = only(lanes, grad)
        grad_probs = lax.dot_general(grad_h, v, ACROSS, preferred_element_type=F32)
        along = jnp.sum(probs * grad_probs, axis=-1, keepdims=True)
        grad_scores = (probs * (grad_probs - along)).astype(BF)
        terms = (
            jnp.dot(grad_scores, k, preferred_element_type=F32) * HD**-0.5,
            lax.dot_general(grad_scores, q, DOWN_ROWS, preferred_element_type=F32) * HD**-0.5,
            lax.dot_general(probs.astype(BF), grad, DOWN_ROWS, preferred_element_type=F32),
        )
        sums = [jnp.where(lanes, term, total) for term, total in zip(terms, sums)]
    for a, total in enumerate(sums):
        part = total.reshape(out_ref.shape[0], out_ref.shape[2], group).astype(BF)
        out_ref[:, 0, :, a * group : (a + 1) * group] = part


def by_item(kernel, arrays, lanes, flops, name):
    sources, items, tokens, _ = arrays[0].shape
    block = lambda n: pl.BlockSpec((sources, 1, tokens, n), lambda b: (0, b, 0, 0))
    return pl.pallas_call(
        kernel,
        grid=(items,),
        in_specs=[block(v.shape[3]) for v in arrays],
        out_specs=block(lanes),
        out_shape=shape(BF, sources, items, tokens, lanes),
        compiler_params=params(28 * 2**20),
        cost_estimate=LIGHT,
        name=name,
    )(*arrays)


def project_kernel(zs, group, heads_ref, w_ref, joined_ref, gain_ref, bias_ref, mixed_ref, after_ref, normed_ref):
    total = joined_ref[...]
    for z in range(zs):
        mixed = jnp.concatenate([heads_ref[z], heads_ref[zs + z]], axis=1)
        mixed_ref[:, z * 2 * group : (z + 1) * 2 * group] = mixed
        total = total + lax.dot_general(mixed, w_ref[z], ACROSS, preferred_element_type=F32)
    after_ref[...] = total
    unit, _ = normalise(total)
    normed_ref[...] = (unit * gain_ref[...] + bias_ref[...]).astype(BF)


def pair_kernel(after_ref, here_ref, there_ref, grad_ref, out_ref):
    out_ref[0] = (after_ref[...] + here_ref[...] + there_ref[...].astype(F32)).astype(BF)
    out_ref[1] = grad_ref[...].astype(BF)


def mlp_kernel(count, x_ref, g_ref, *refs):
    given = 1 if count == 1 else count + 1
    weights = [(r.at[0], r.at[1]) for r in refs[: count - 1 or 1]]
    if count > 1:
        weights.append((refs[count - 1], refs[count]))
    out_ref, back_ref = refs[given : given + 2]
    acts, grads = refs[given + 2 : given + 2 + count], refs[given + 2 + count :]
    x, g = x_ref[...], g_ref[...]
    for p, (up, down) in enumerate(weights):
        act, slope = gelu_pair(jnp.dot(x, up[...], preferred_element_type=F32))
        act = act.astype(BF)
        acts[p][...] = act
        grad = (jnp.dot(g, down[...], preferred_element_type=F32) * slope).astype(BF)
        grads[p][...] = grad
        out = lax.dot_general(act, down[...], ACROSS, preferred_element_type=F32)
        back = lax.dot_general(grad, up[...], ACROSS, preferred_element_type=F32)
        if p == 0:
            out_ref[...] = out
            back_ref[...] = back
        else:
            out_ref[...] += out
            back_ref[...] += back


def mlp_terms(two, grad_out, actives, grads, dp_at):
    count = len(actives)
    cells, width = two.shape
    cols = actives[0].shape[1]

    def kernel(at_ref, two_ref, out_ref, *refs):
        acts, ups, terms = refs[:count], refs[count : 2 * count], refs[-1]
        for k in range(count):

            @pl.when(pl.program_id(0) == k)
            def _():
                terms[0, 0] = lax.dot_general(two_ref[...], ups[k][...], DOWN_ROWS, preferred_element_type=F32).astype(BF)
                terms[0, 1] = lax.dot_general(out_ref[...], acts[k][...], DOWN_ROWS, preferred_element_type=F32).astype(BF)

    whole = lambda v: pl.BlockSpec(v.shape, lambda k, at: (0, 0))
    arrays = [two, grad_out, *actives, *grads]
    return pl.pallas_call(
        kernel,
        grid_spec=pltpu.PrefetchScalarGridSpec(
            num_scalar_prefetch=1,
            grid=(count,),
            in_specs=[whole(v) for v in arrays],
            out_specs=pl.BlockSpec((1, 2, width, cols), lambda k, at: (k ^ at[0], 0, 0, 0)),
        ),
        out_shape=jax.ShapeDtypeStruct((count, 2, width, cols), BF),
        compiler_params=params(32 * 2**20),
        cost_estimate=LIGHT,
        name="mlp_terms",
    )(dp_at.astype(jnp.int32).reshape(1) if count > 1 else jnp.zeros((1,), jnp.int32), *arrays)


def lines(*rows):
    width = rows[0].shape[1]
    return jnp.concatenate(list(rows) + [jnp.zeros((8 - len(rows), width), F32)], axis=0)


def norm_back_two_kernel(zs, group, here_ref, there_ref, after_ref, d_ref, gain_ref, w_ref, grad_ref, low_ref, sums_ref, out_ref):
    grad_two = here_ref[...] + there_ref[...].astype(F32)
    unit, scale = normalise(after_ref[...])
    sums_ref[...] = lines(jnp.sum(grad_two * unit, axis=0, keepdims=True), jnp.sum(grad_two, axis=0, keepdims=True))
    grad = d_ref[...] + normalise_back(grad_two, unit, scale, gain_ref[...])
    grad_ref[...] = grad
    low = grad.astype(BF)
    low_ref[...] = low
    for z in range(zs):
        part = jnp.dot(low, w_ref[z], preferred_element_type=F32).astype(BF)
        for core in range(2):
            out_ref[core * zs + z] = part[:, core * group : (core + 1) * group]


def norm_back_one_kernel(zs, group, g_ref, w_ref, joined_ref, after_ref, gain_ref, all_ref, grad_ref, sums_ref):
    grad_one = jnp.zeros(joined_ref.shape, F32)
    for z in range(zs):
        for a in range(3):
            part = jnp.concatenate([g_ref[core * zs + z, :, a * group : (a + 1) * group] for core in range(2)], axis=1)
            at = (3 * z + a) * 2 * group
            all_ref[:, at : at + 2 * group] = part
            grad_one = grad_one + lax.dot_general(part, shares(w_ref, z, a), ACROSS, preferred_element_type=F32)
    unit, scale = normalise(joined_ref[...])
    sums_ref[...] = lines(jnp.sum(grad_one * unit, axis=0, keepdims=True), jnp.sum(grad_one, axis=0, keepdims=True))
    grad_ref[...] = after_ref[...] + normalise_back(grad_one, unit, scale, gain_ref[...])


def normalise(v):
    center = jnp.mean(v, axis=-1, keepdims=True)
    shifted = v - center
    scale = lax.rsqrt(jnp.mean(shifted * shifted, axis=-1, keepdims=True) + EPS)
    return shifted * scale, scale


def normalise_back(g, unit, scale, gain):
    gg = g * gain
    along = jnp.mean(gg * unit, axis=-1, keepdims=True)
    return scale * (gg - jnp.mean(gg, axis=-1, keepdims=True) - unit * along)


def pool_matrix(pooled_index, buffer_index, map_side, offset):
    map_place = buffer_index[None, :] - offset
    bin_start = pooled_index[:, None] * map_side // G
    bin_stop = ((pooled_index[:, None] + 1) * map_side + G - 1) // G
    inside = jnp.logical_and(map_place >= bin_start, map_place < bin_stop)
    real = jnp.logical_and(pooled_index >= 0, pooled_index < G)[:, None]
    return jnp.where(jnp.logical_and(inside, real), 1.0, 0.0).astype(F32) / (bin_stop - bin_start).astype(F32)


def depthwise3(padded, kernel, rows, cols):
    total = None
    for i in range(3):
        for j in range(3):
            term = padded[:, i : i + rows, j : j + cols, :] * kernel[:, 3 * i + j]
            total = term if total is None else total + term
    return total


def rim(v):
    v = jnp.concatenate([shift(v[:, -1:], "strip", 1), v, shift(v[:, :1], "strip", -1)], axis=1)
    return jnp.concatenate([shift(v[:, :, -1:], "tensor", 1), v, shift(v[:, :, :1], "tensor", -1)], axis=2)


def rows_rim(v):
    return jnp.concatenate([shift(v[:, :, -EDGE:], "strip", 1), v, shift(v[:, :, :EDGE], "strip", -1)], axis=2)


def shards(
    res_code, vit_in, map_in, dw_kernel, conv_gain, conv_bias, w_expand, w_reduce, layer_scale, adapt_w, mix_kernel,
    gate_logit, gain_one, bias_one, w_qkv, w_proj, gain_two, bias_two, w_up, w_down, d_vit, d_map,
):
    strip_at, tensor_at, dp_at = (lax.axis_index(a) for a in ("strip", "tensor", "dp"))
    dps, zs = lax.axis_size("dp"), lax.axis_size("tensor")
    items, grid_rows, _, width = vit_in.shape
    _, map_rows, map_cols, channels = map_in.shape
    grid_cols = G // zs
    cells = items * map_rows * map_cols
    tokens = items * grid_rows * grid_cols
    head_cols = w_qkv.shape[2]
    score_scale = HD**-0.5

    expand_z, reduce_z = gather_conv_weight(w_expand, 1), gather_conv_weight(w_reduce, 0.5)
    expand_own, reduce_own = expand_z(0), reduce_z(0)
    expand_near = dp_neighbours(expand_own)
    mlp_own, mlp_gathered = gather_mlp_weights(w_up, w_down)
    qkv_whole = gather_rows(jnp.swapaxes(w_qkv, 0, 1), mlp_gathered)
    proj_whole = gather_rows(w_proj[None]).reshape(zs, width, head_cols)
    count = quarters()

    side = res_code // 32
    offset = (MAXS - side) // 2
    row_cells = strip_at * map_rows + jnp.arange(map_rows, dtype=jnp.int32)
    col_cells = tensor_at * map_cols + jnp.arange(map_cols, dtype=jnp.int32)

    def inside(at):
        low, high = offset[:, None], (offset + side)[:, None]
        return jnp.logical_and(at[None] >= low, at[None] < high).astype(F32)

    row_ok, col_ok = inside(row_cells), inside(col_cells)
    cell_mask = col_ok[:, :, None, None] * row_ok[:, None, :, None]
    many_pools = jax.vmap(pool_matrix, in_axes=(None, None, 0, 0))
    pooled_rows = strip_at * grid_rows + jnp.arange(grid_rows, dtype=jnp.int32)
    pooled_cols = (tensor_at - 1) * grid_cols + jnp.arange(3 * grid_cols, dtype=jnp.int32)
    row_pool = many_pools(pooled_rows, row_cells, side, offset)
    col_pool = many_pools(pooled_cols, col_cells, side, offset).reshape(items, 3, grid_cols, map_cols)
    pool = jnp.einsum("bir,bgjc->bgijcr", row_pool, col_pool)
    pool = pool.reshape(items, 3 * grid_rows * grid_cols, map_cols * map_rows).astype(BF)

    masked = jnp.swapaxes(map_in, 1, 2) * cell_mask.astype(BF)
    taps = jnp.pad(dw_kernel.T.reshape(7, 7, channels), ((0, 0), (0, 1), (0, 0)))
    edges = [later(shift(e, "tensor", step), pool, expand_own) for e, step in ((masked[:, -3:], 1), (masked[:, :3], -1))]
    padded = rows_rim(jnp.concatenate([edges[0], masked, edges[1]], axis=1))
    spread = conv7(padded, taps, map_rows, map_cols).reshape(cells, channels)
    reduce_near = dp_neighbours(later(reduce_own, spread))
    normed = norm_rows(spread, conv_gain, conv_bias)
    if expand_near:
        normed = later(normed, *expand_near)
    normed_both = jnp.concatenate([normed, core_swap(normed)], axis=0)
    expand_pieces, reduce_pieces, pairs = [expand_own, *expand_near], [reduce_own, *reduce_near], []
    x = normed_both
    for k in range(count):
        if k == 3:
            expand_pieces.append(expand_z(1, pairs[2][0]))
        pairs.append(expand(x, expand_pieces[k]))
        x = later(normed_both, pairs[k][0])
    acts, slopes = zip(*pairs)
    if count > 1:
        reduce_pieces.append(dp_across(reduce_near, reduce_z(1, acts[2]), acts[2]))
    branch_sent = back_sum(acts, reduce_pieces, cells, cells, BF, 256, cells)
    branch_there = core_swap(branch_sent)
    branch_here = back_sum(acts, reduce_pieces, 0, cells, F32, 256, cells)
    branch, map_low = map_value_rows(
        branch_here, branch_there, masked.reshape(cells, channels), cell_mask.reshape(cells, 1), layer_scale
    )
    branch, map_low = branch.reshape(masked.shape), map_low.reshape(masked.shape)
    map_out = jnp.swapaxes(map_low, 1, 2)

    pooled3 = lax.dot_general(
        pool, map_low.reshape(items, -1, channels), (((2,), (1,)), ((0,), (0,))), preferred_element_type=F32
    ).reshape(items, 3, -1, channels)
    pooled = (
        pooled3[:, 1]
        + shift(pooled3[:, 0].astype(BF), "tensor", -1).astype(F32)
        + shift(pooled3[:, 2].astype(BF), "tensor", 1).astype(F32)
    )
    pooled_low = pooled.astype(BF).reshape(tokens, channels)
    grid_shape = (items, grid_rows, grid_cols, width)
    adapted = jnp.dot(pooled_low, adapt_w, preferred_element_type=F32).reshape(grid_shape)
    adapted_pad = rim(adapted)
    local_mix = depthwise3(adapted_pad, mix_kernel, grid_rows, grid_cols)
    gate = jnp.tanh(gate_logit)
    mine = lambda v: lax.dynamic_slice_in_dim(v, tensor_at * grid_cols, grid_cols, 2)
    grad_out = mine(d_vit).reshape(tokens, width)
    grad_mlp = grad_out.astype(BF)
    grad_mlp_both = jnp.concatenate([grad_mlp, core_swap(grad_mlp)], axis=0)
    joined = (mine(vit_in) + gate * local_mix).reshape(tokens, width)

    group = head_cols // 2
    line = lambda v: v.reshape(1, width)
    dots = lambda m, n, k: 2 * m * n * k
    spread_heads = lambda v: lax.all_to_all(v, ("strip", "tensor"), 0, 0, tiled=True)
    by_source = lambda v: v.reshape(2 * zs, items, -1, v.shape[-1])
    normed_one, qkv = whole_call(
        functools.partial(qkv_kernel, zs, group),
        [shape(BF, tokens, width), shape(BF, 2 * zs, tokens, 3 * group)],
        [joined, line(gain_one), line(bias_one), qkv_whole],
        dots(tokens, width, 3 * zs * head_cols),
        "qkv",
    )
    mlp_near = dp_neighbours(mlp_own)
    qkv = later(by_source(spread_heads(qkv)), mlp_own, *mlp_near)
    mlp_weights = [mlp_own, *mlp_near, *mlp_far(mlp_near)]
    attention_flops = items * 2 * dots(24 * 24, 24 * 24, group)
    heads = by_item(functools.partial(attention_kernel, group), [qkv], group, 2 * attention_flops, "attention")
    heads = later(spread_heads(heads).reshape(2 * zs, tokens, group), *mlp_weights)
    mixed, after_attn, normed_two = whole_call(
        functools.partial(project_kernel, zs, group),
        [shape(BF, tokens, width), shape(F32, tokens, width), shape(BF, tokens, width)],
        [heads, proj_whole, joined, line(gain_two), line(bias_two)],
        dots(tokens, width, width),
        "project",
    )

    two_both = jnp.concatenate([normed_two, core_swap(normed_two)], axis=0)
    some = mlp_own.shape[2]
    mlp, back, *halves = whole_call(
        functools.partial(mlp_kernel, count),
        [shape(F32, 2 * tokens, width)] * 2 + [shape(BF, 2 * tokens, some)] * (2 * count),
        [two_both, grad_mlp_both, *mlp_weights],
        4 * count * dots(2 * tokens, width, some),
        "mlp",
    )
    actives, grad_ups = halves[:count], halves[count:]
    back_there = core_swap(back[tokens:].astype(BF))
    grad_after, grad_att, sums_two, grad_heads = whole_call(
        functools.partial(norm_back_two_kernel, zs, group),
        [shape(F32, tokens, width), shape(BF, tokens, width), shape(F32, 8, width), shape(BF, 2 * zs, tokens, group)],
        [back[:tokens], back_there, after_attn, grad_out, line(gain_two), proj_whole],
        dots(tokens, width, width),
        "norm_back_two",
    )
    down_terms = lambda left, rights: [
        lax.dot_general(left, r, DOWN_ROWS, preferred_element_type=F32).astype(BF) for r in rights
    ]
    four = count > 1
    mlp_grads = mlp_terms(later(two_both, grad_heads), grad_mlp_both, actives, grad_ups, dp_at)
    grad_heads = later(by_source(spread_heads(grad_heads)), mlp_grads)
    mlp_view, mlp_over_z = mlp_scatter(mlp_grads, dps)
    mlp_there = core_swap(mlp[tokens:].astype(BF))
    to_grid = lambda v: jnp.concatenate(list(v), axis=2).astype(F32)

    grad_qkv = by_item(
        functools.partial(attention_back_kernel, group), [qkv, grad_heads], 3 * group, 5 * attention_flops, "attention_back"
    )
    grad_qkv = later(spread_heads(grad_qkv).reshape(2 * zs, tokens, 3 * group), mlp_grads)
    grad_qkv, grad_joined, sums_one = whole_call(
        functools.partial(norm_back_one_kernel, zs, group),
        [shape(BF, tokens, 3 * width), shape(F32, tokens, width), shape(F32, 8, width)],
        [grad_qkv, qkv_whole, joined, grad_after, line(gain_one)],
        dots(tokens, width, 3 * width),
        "norm_back_one",
    )

    grad_grid = grad_joined.reshape(grid_shape)
    over = (0, 1, 2)
    grad_mix = grad_grid * gate
    grad_adapted = depthwise3(rim(grad_mix), mix_kernel[:, ::-1], grid_rows, grid_cols)
    grad_adapted = grad_adapted.astype(BF).reshape(tokens, width)
    grad_adapted = later(grad_adapted, mlp_view)
    grad_pooled = lax.dot_general(grad_adapted, adapt_w, ACROSS, preferred_element_type=F32).astype(BF)
    grad_late = later(grad_grid, grad_pooled)
    grad_gate = jnp.sum(grad_late * local_mix, axis=over) * (1.0 - gate * gate)
    grad_taps = [
        jnp.sum(adapted_pad[:, i : i + grid_rows, j : j + grid_cols] * (grad_late * gate), axis=over)
        for i in range(3)
        for j in range(3)
    ]
    small_vit = jnp.stack(
        grad_taps
        + [
            grad_gate,
            sums_one[0],
            sums_one[1],
            sums_two[0],
            sums_two[1],
        ],
        axis=0,
    )
    small_vit = scatter_steps(scatter_steps(later(small_vit, grad_pooled), "dp"), "strip")
    row_terms = (
        down_terms(later(normed_one, grad_pooled), [grad_qkv])
        + down_terms(later(grad_att, grad_pooled), [mixed])
        + down_terms(later(pooled_low, grad_pooled), [grad_adapted])
    )
    grad_pooled = grad_pooled.reshape(items, -1, channels)
    rows_sums, rows_over_z = rows_scatter(row_terms)
    grad_pooled = jnp.concatenate(
        [later(shift(grad_pooled, "tensor", 1), *row_terms, small_vit), grad_pooled, shift(grad_pooled, "tensor", -1)], axis=1
    )
    grad_map = lax.dot_general(pool, grad_pooled, (((1,), (1,)), ((0,), (0,))), preferred_element_type=F32)
    grad_map = jnp.swapaxes(d_map, 1, 2).astype(F32) + grad_map.reshape(masked.shape)

    kept = cell_mask * grad_map
    grad_scale = jnp.sum(kept * branch.astype(F32), axis=over)
    grad_branch = (kept * layer_scale).astype(BF).reshape(cells, channels)
    grad_branch_both = jnp.concatenate([grad_branch, core_swap(grad_branch)], axis=0)
    rows_part = rows_over_z(grad_map)
    reduce_terms = conv_terms(grad_branch_both, acts, lambda v: later(v, rows_sums))
    grad_hidden, last = [], [reduce_terms[-1]]
    if four:
        reduce_first = conv_dp(reduce_terms)
    for k in range(count):
        last = [back_slope(later(grad_branch_both, *last), reduce_pieces[k], slopes[k])]
        grad_hidden += last
    (both_low,) = whole_call(
        pair_kernel,
        [shape(BF, 2, tokens, width)],
        [after_attn, mlp[:tokens], later(mlp_there, rows_sums), grad_joined],
        tokens * width,
        "vit_pair",
    )
    both_every = lax.all_gather(both_low.reshape(2, *grid_shape), "tensor", axis=0)
    if four:
        near = tall(later(normed_both, last[0]), grad_hidden[1:], [(0, 2), (1, 2)], "tall_near")
        keep = tall(later(normed_both, near[0]), grad_hidden[:3], [(0, 2), (0, 1)], "tall_keep")
        expand_first = conv_dp([*near, *keep])
        done = keep[0]
    else:
        expand_terms = conv_terms(normed_both, grad_hidden, lambda v: later(v, *last))
        done = expand_terms[0]
    last = [done]
    if four:
        reduce_sent, reduce_second = reduce_first(done)
        last += [*reduce_sent]
    sent = later(grad_hidden[0], *last)
    normed_sent = back_sum([sent] + grad_hidden[1:], expand_pieces, cells, cells, BF)
    normed_there = core_swap(normed_sent)
    kept_here = later(grad_hidden[0], normed_sent)
    normed_here = back_sum([kept_here] + grad_hidden[1:], expand_pieces, 0, cells, F32)
    last = [normed_here, rows_part]
    if four:
        reduce_view = reduce_second(normed_here)
        last += [reduce_view]
    else:
        reduce_view, expand_view = (
            jnp.swapaxes(t[0].reshape(2, zs, -1, t[0].shape[1]), 0, 1) for t in (reduce_terms, expand_terms)
        )
    reduce_part = conv_scatter(reduce_view)
    grad_spread, sums_conv = norm_rows_back(later(normed_here, *last), normed_there, spread, conv_gain)
    grad_spread = grad_spread.reshape(masked.shape)
    beside = shift(grad_spread[:, -3:], "tensor", 1), shift(grad_spread[:, :3], "tensor", -1)
    last = [both_every]
    if four:
        expand_sent, expand_second = expand_first(grad_spread)
        last += [*expand_sent]
    grad_taps = tap_grad(padded, later(grad_spread, *last), map_rows, map_cols)
    last = [grad_taps]
    if four:
        expand_view = expand_second(grad_taps)
        last += [expand_view]
    small_conv = jnp.concatenate([grad_taps.reshape(56, channels), sums_conv[:2], grad_scale[None]], axis=0)
    rim_spread = jnp.concatenate([later(beside[0], *last), grad_spread, later(beside[1], *last)], axis=1)
    expand_part = conv_scatter(expand_view)
    reduce_both = conv_cores(later(reduce_part, rim_spread))
    small_conv = scatter_steps(later(small_conv, rim_spread), "strip")
    wide_spread = rows_rim(rim_spread)
    mlp_part = mlp_over_z(wide_spread)
    grad_map_in = conv7(
        later(wide_spread, reduce_both, small_conv),
        taps,
        map_rows,
        map_cols,
        True,
    )
    out_reduce = conv_rows(reduce_both, grad_map_in)
    small_conv = sum_dp(small_conv, reduce_both, grad_map_in)
    out_qkv, out_proj, out_adapt = rows_sum(row_terms, rows_part, grad_map_in)
    grad_map_in = jnp.swapaxes(cell_mask * (kept + grad_map_in), 1, 2)
    expand_both = conv_cores(later(expand_part, grad_map_in))
    out_expand = conv_rows(expand_both)
    out_up, out_down = mlp_rows(jnp.swapaxes(later(mlp_part, expand_both), 0, 1), dps)
    both_every = later(both_every, expand_both)
    vit_out, grad_vit = to_grid(both_every[:, 0]), to_grid(both_every[:, 1])
    out_adapt = gather_bits(later(out_adapt.astype(BF), expand_both)).astype(F32)
    small_conv = scatter_steps(later(small_conv, expand_both), "tensor")
    small_vit = all_sum(later(small_vit, expand_both), ("tensor",))
    conv_share = channels // (2 * zs)
    out_taps = small_conv[:56].reshape(7, 8, conv_share)[:, :7].reshape(49, conv_share).T
    return (
        vit_out,
        map_out,
        grad_vit,
        grad_map_in,
        out_taps,
        small_conv[56],
        small_conv[57],
        out_expand,
        out_reduce,
        small_conv[58],
        out_adapt,
        small_vit[:9].T,
        small_vit[9],
        small_vit[10],
        small_vit[11],
        out_qkv.reshape(-1, 3, head_cols),
        out_proj,
        small_vit[12],
        small_vit[13],
        out_up,
        out_down,
    )


def solution(mesh):
    rows = P("dp", "strip", None, None)
    maps = P("dp", "strip", "tensor", None)
    conv = ("strip", "tensor")
    vit = ("dp", "strip")
    in_specs = (
        P("dp"), rows, maps, P(), P(), P(), P(conv, None), P(conv, None), P(), P(), P(), P(), P(), P(),
        P(None, None, "tensor"), P(None, "tensor"), P(), P(), P(None, "tensor"), P(None, "tensor"), rows, maps,
    )
    out_specs = (
        rows, maps, rows, maps, P(conv, None), P(conv), P(conv), P(conv, None), P(conv, None), P(conv),
        P(vit, None), P(vit, None), P(vit), P(vit), P(vit), P(vit, None, "tensor"), P(vit, "tensor"), P(vit), P(vit),
        P(vit, "tensor"), P(vit, "tensor"),
    )
    return jax.shard_map(shards, mesh=mesh, in_specs=in_specs, out_specs=out_specs, check_vma=False)
```
